128 devices in a mesh: frame: 8 (over y_hi, x), head: 16 (over y_lo, z, core).
Axes of the slice: x: 4, y: 4 (y_hi: 2, y_lo: 2; y = y_hi * 2 + y_lo), z: 4, core: 2. Of those that a mesh axis runs over, the one named last changes fastest.
Arguments:
- tokens: bfloat16 [8192, 5120], P('frame', 'head'), may hold values from -16 to 16
- qkv_weight: bfloat16 [3, 5120, 4096], P(None, None, 'head'), may hold values from -0.1118034 to 0.1118034
- out_weight: bfloat16 [4096, 5120], P('head'), may hold values from -0.125 to 0.125
- modulation: float32 [3, 5120], replicated, may hold values from -3 to 3
- block_mask: int32 [32, 64, 64], P('head', 'frame'), may hold values from 0 to 1, as said below
Outputs:
- mixed: bfloat16 [8192, 5120], P('frame', 'head')
The draws below stay inside these ranges and needn't reach their ends.
Inputs may be any that keep to these rules, and one draw needn't show every extreme that they name: `block_mask`: 1 keeps a pair of 128-token blocks; every query block keeps its own block.
All inputs are finite; a program needn't handle non-finite values.
Results may differ from the reference program's by a relative error of at most 0.0085.
Values may be sent and summed in bfloat16 or wider, within the bound.
No kernel may reach another device: no remote copies, remote signals or barrier semaphores. Data moves between devices by JAX's collectives and lax.ppermute only.
A program may use at most 256 MiB of HBM per device.

```python
import math
import jax
import jax.numpy as jnp
from jax import lax

D = 5120
HD = 128
BLK = 128
TPF = 1024
HEADS = 32
N_FRAME = 8


def draw_tokens(key, part):
    first, second = jax.random.split(key, 2)
    seq_len = TPF * N_FRAME
    place = jnp.arange(D, dtype=jnp.float32) / (D - 1)
    rough = jax.random.uniform(second, (D,), jnp.float32, 0.5, 1.5)
    column = 1.0 + 2.0 * place
    values = jax.random.normal(first, (seq_len, D), jnp.float32) * column * rough
    return jnp.clip(values, -16.0, 16.0).astype(jnp.bfloat16)


def draw_qkv_weight(key, part):
    first = jax.random.fold_in(key, 0)
    width = HEADS * HD
    limit = 8.0 / math.sqrt(D)
    values = jax.random.normal(first, (3, D, width), jnp.float32) / math.sqrt(D)
    return jnp.clip(values, -limit, limit).astype(jnp.bfloat16)


def draw_modulation(key, part):
    first, second, third, fourth = jax.random.split(key, 4)
    rough = jax.random.uniform(fourth, (D,), jnp.float32, 0.5, 1.5)
    shift = jnp.clip(0.5 * jax.random.normal(first, (D,), jnp.float32) * rough, -2.5, 2.5)
    scale = jax.random.uniform(second, (D,), jnp.float32, -0.2, 1.0)
    gate = jax.random.uniform(third, (D,), jnp.float32, 0.5, 1.5)
    return jnp.stack([shift, scale, gate])


def draw_block_mask(key, part):
    first, second, third = jax.random.split(key, 3)
    per_frame = TPF // BLK
    frame_count = N_FRAME
    blocks = TPF * N_FRAME // BLK
    spatial = jax.random.randint(first, (HEADS, 1, 1), 0, 2)
    chosen = jax.random.randint(second, (HEADS, frame_count, frame_count), 0, 4) == 0
    extra = jax.random.randint(third, (HEADS, blocks, blocks), 0, 2) == 1
    query_block = jnp.arange(blocks, dtype=jnp.int32)[:, None]
    key_block = jnp.arange(blocks, dtype=jnp.int32)[None, :]
    query_frame = query_block // per_frame
    key_frame = key_block // per_frame
    same = query_frame == key_frame
    pair_chosen = jnp.take_along_axis(chosen.reshape(HEADS, frame_count * frame_count), (query_frame * frame_count + key_frame).reshape(1, -1) * jnp.ones((HEADS, 1), jnp.int32), axis=1).reshape(HEADS, blocks, blocks)
    spatial_keep = same[None] | pair_chosen & extra
    temporal_keep = (key_block % per_frame == query_block % per_frame)[None] | (same & (jnp.abs(query_block - key_block) <= 1))[None]
    keep = jnp.where(spatial == 1, spatial_keep, temporal_keep)
    return keep.astype(jnp.int32)


def spiked(drawn, own_key, source, target, parts, factor):
    owner, partner = [(jnp.arange(drawn.shape[dim]) // (drawn.shape[dim] // parts)).reshape([-1 if axis == dim else 1 for axis in range(drawn.ndim)]) for dim in (source, target)]
    chosen = jax.random.permutation(own_key, parts)[partner]
    strong = (owner == chosen) | (owner == (partner + parts // 2) % parts)
    return jnp.where(strong, factor * drawn, drawn)


def level_of(rng, shape, shards, low, high):
    level, own = 1.0, jax.random.fold_in(rng, 6)
    for dim, shards_of in shards:
        steps = jnp.exp(jax.random.uniform(jax.random.fold_in(own, dim), (shards_of,), jnp.float32, low / len(shards), high / len(shards)))
        level = level * jnp.repeat(steps, shape[dim] // shards_of).reshape([-1 if axis == dim else 1 for axis in range(len(shape))])
    return level


def bell_draw_with(key, extent, scale, reach, pieces, heavy, held_as=jnp.bfloat16):
    values = scale * jax.random.normal(key, extent, jnp.float32)
    if pieces:
        values = values * level_of(key, extent, pieces, -0.22, 0.18)
    return jnp.clip(spiked(values, jax.random.fold_in(key, 3), *heavy), -reach, reach).astype(held_as)


def setup_inputs(seed: int = 0) -> dict:
    splits = jax.random.split(jax.random.key(seed), 6)
    return {
        "tokens": draw_tokens(jax.random.fold_in(splits[5], 71), 0),
        "qkv_weight": draw_qkv_weight(jax.random.fold_in(splits[5], 71), 0),
        "out_weight": bell_draw_with(splits[2], (HEADS * HD, D), (HEADS * HD) ** -0.5, 0.125, ((0, 16),), (0, 1, 16, 2.0)),
        "modulation": draw_modulation(jax.random.fold_in(splits[5], 71), 0),
        "block_mask": draw_block_mask(jax.random.fold_in(splits[5], 71), 0),
    }


def reference(tokens, qkv_weight, out_weight, modulation, block_mask):
    wide = tokens.astype(jnp.float32)
    center = lax.optimization_barrier(jnp.mean(wide, axis=1, keepdims=True))
    spread = lax.optimization_barrier(jnp.mean(jnp.square(wide - center), axis=1, keepdims=True))
    normed = ((wide - center) * lax.rsqrt(spread + 1e-06) * (1.0 + modulation[1]) + modulation[0]).astype(jnp.bfloat16)
    query = jnp.dot(normed, qkv_weight[0], preferred_element_type=jnp.float32).astype(jnp.bfloat16)
    keyed = jnp.dot(normed, qkv_weight[1], preferred_element_type=jnp.float32).astype(jnp.bfloat16)
    valued = jnp.dot(normed, qkv_weight[2], preferred_element_type=jnp.float32).astype(jnp.bfloat16)
    seq_len = tokens.shape[0]
    heads_count = block_mask.shape[0]
    head_size = qkv_weight.shape[2] // heads_count
    scale = 1.0 / math.sqrt(head_size)

    def split_heads(values):
        return values.reshape(seq_len, heads_count, head_size).transpose(1, 0, 2)

    def one_head(items):
        head_query, head_key, head_value, head_mask = items
        keep = jnp.repeat(jnp.repeat(head_mask > 0, BLK, axis=0), BLK, axis=1)
        scores = jnp.dot(head_query, head_key.T, preferred_element_type=jnp.float32) * scale
        masked = jnp.where(keep, scores, -jnp.inf)
        top = lax.optimization_barrier(jnp.max(masked, axis=1, keepdims=True))
        weights = jnp.where(keep, jnp.exp(scores - top), 0.0)
        total = lax.optimization_barrier(jnp.sum(weights, axis=1, keepdims=True))
        summed = jnp.dot(weights.astype(jnp.bfloat16), head_value, preferred_element_type=jnp.float32)
        return (summed / total).astype(jnp.bfloat16)
    heads_done = lax.map(one_head, (split_heads(query), split_heads(keyed), split_heads(valued), block_mask))
    heads_out = heads_done.transpose(1, 0, 2).reshape(seq_len, heads_count * head_size)
    projected = jnp.dot(heads_out, out_weight, preferred_element_type=jnp.float32)
    return (wide + modulation[2] * projected).astype(jnp.bfloat16)
```

```python
import math

import jax
import jax.numpy as jnp
from jax import lax
from jax.experimental import pallas as pl
from jax.experimental.pallas import tpu as pltpu
from jax.sharding import Mesh
from jax.sharding import PartitionSpec as P

BLK = 128
EPSILON = 1e-06
NEGATIVE = -1e30
FRAME = ("yh", "x")
CHIP = ("yl", "z")
HEAD = ("yl", "z", "core")
SWAP = [(0, 1), (1, 0)]
MIB = 1 << 20


def project_kernel(x0, x1, x2, x3, weight, gain, shift, center, rate, q_out, k0, k1, v0, v1, total):
    step = pl.program_id(0)

    @pl.when(step == 0)
    def _():
        total[...] = jnp.zeros_like(total)

    wide_gain = gain[...]
    wide_shift = shift[...]
    for chunk, x in enumerate((x0, x1, x2, x3)):
        width = x.shape[1]
        parts = []
        for part in range(width // BLK):
            columns = slice(chunk * width + part * BLK, chunk * width + (part + 1) * BLK)
            wide = x[:, part * BLK : (part + 1) * BLK].astype(jnp.float32)
            part_normed = (wide - center[:, columns]) * rate[:, columns] * wide_gain + wide_shift
            parts.append(part_normed.astype(jnp.bfloat16))
        normed = jnp.concatenate(parts, axis=1)
        columns = slice(chunk * width, (chunk + 1) * width)
        total[:, columns] += jnp.dot(weight[...], normed, preferred_element_type=jnp.float32)

    @pl.when(step == pl.num_programs(0) - 1)
    def _():
        inner = q_out.shape[0]
        half = inner // 2
        q_out[...] = total[:inner].astype(jnp.bfloat16)
        k0[...] = total[inner : inner + half].T.astype(jnp.bfloat16)
        k1[...] = total[inner + half : 2 * inner].T.astype(jnp.bfloat16)
        v0[...] = total[2 * inner : 2 * inner + half].astype(jnp.bfloat16)
        v1[...] = total[2 * inner + half :].astype(jnp.bfloat16)


def project(xs, weight, gain, shift, center, rate):
    features, width = xs[0].shape
    count = width * len(xs)
    outs = weight.shape[0]
    inner = outs // 3
    half = inner // 2
    deep = 512
    whole = lambda shape: pl.BlockSpec(shape, lambda k: (0, 0))
    return pl.pallas_call(
        project_kernel,
        grid=(features // deep,),
        in_specs=[pl.BlockSpec((deep, width), lambda k: (k, 0))] * len(xs)
        + [
            pl.BlockSpec((outs, deep), lambda k: (0, k)),
            pl.BlockSpec((deep, BLK), lambda k: (k, 0)),
            pl.BlockSpec((deep, BLK), lambda k: (k, 0)),
            whole((1, count)),
            whole((1, count)),
        ],
        out_specs=[
            whole((inner, count)),
            whole((count, half)),
            whole((count, half)),
            whole((half, count)),
            whole((half, count)),
        ],
        out_shape=[
            jax.ShapeDtypeStruct((inner, count), jnp.bfloat16),
            jax.ShapeDtypeStruct((count, half), jnp.bfloat16),
            jax.ShapeDtypeStruct((count, half), jnp.bfloat16),
            jax.ShapeDtypeStruct((half, count), jnp.bfloat16),
            jax.ShapeDtypeStruct((half, count), jnp.bfloat16),
        ],
        scratch_shapes=[pltpu.VMEM((outs, count), jnp.float32)],
        compiler_params=pltpu.CompilerParams(vmem_limit_bytes=40 * MIB),
        cost_estimate=pl.CostEstimate(
            flops=2 * outs * features * count,
            bytes_accessed=2 * features * (count + outs),
            transcendentals=0,
        ),
        name="project",
    )(*xs, weight, gain, shift, center, rate)


GROUP = 4


def attend_kernel(factor, places, counts, q_ref, k0, k1, v0, v1, out, scores):
    head_size = k0.shape[1]
    per_head = q_ref.shape[1] // BLK
    per_frame = v0.shape[1] // BLK

    for head, (keys, values) in enumerate(((k0, v0), (k1, v1))):

        def one(block, _):
            row = head * per_head + block
            column = pl.multiple_of(block * BLK, BLK)
            query = q_ref[head * head_size : (head + 1) * head_size, pl.ds(column, BLK)]
            count = counts[row]
            groups = (count + GROUP - 1) // GROUP

            def rate(group, top):
                for item in range(GROUP):
                    place = group * GROUP + item
                    start = pl.multiple_of(places[row, place] * BLK, BLK)
                    score = jnp.dot(
                        keys[pl.ds(start, BLK), :], query, preferred_element_type=jnp.float32
                    )
                    scores[pl.ds(pl.multiple_of(place * BLK, BLK), BLK), :] = score
                    best = jnp.max(score.reshape(BLK // 8, 8, BLK), axis=0)
                    top = jnp.maximum(top, best + jnp.where(place < count, 0.0, NEGATIVE))
                return top

            top = lax.fori_loop(0, groups, rate, jnp.full((8, BLK), NEGATIVE, jnp.float32))
            top = jnp.max(top, axis=0, keepdims=True) * factor

            def gather(group, state):
                total, summed = state
                weights, held = [], []
                for item in range(GROUP):
                    place = group * GROUP + item
                    score = scores[pl.ds(pl.multiple_of(place * BLK, BLK), BLK), :]
                    offset = top + jnp.where(place < count, 0.0, -NEGATIVE)
                    weight = jnp.exp2(score * factor - offset)
                    total = total + jnp.sum(weight.reshape(BLK // 8, 8, BLK), axis=0)
                    weights.append(weight.astype(jnp.bfloat16))
                    where = places[row, place]
                    first = pl.multiple_of((where // per_frame) * head_size, head_size)
                    start = pl.multiple_of((where % per_frame) * BLK, BLK)
                    held.append(values[pl.ds(first, head_size), pl.ds(start, BLK)])
                summed = summed + jnp.dot(
                    jnp.concatenate(held, axis=1),
                    jnp.concatenate(weights, axis=0),
                    preferred_element_type=jnp.float32,
                )
                return total, summed

            total, summed = lax.fori_loop(
                0,
                groups,
                gather,
                (jnp.zeros((8, BLK), jnp.float32), jnp.zeros((head_size, BLK), jnp.float32)),
            )
            total = jnp.sum(total, axis=0, keepdims=True)
            out[head * head_size : (head + 1) * head_size, pl.ds(column, BLK)] = (
                summed / total
            ).astype(jnp.bfloat16)
            return 0

        lax.fori_loop(0, per_head, one, 0)


def attend(factor, places, counts, query, k0, k1, v0, v1):
    def kernel(*refs):
        attend_kernel(factor, *refs)

    return pl.pallas_call(
        kernel,
        in_specs=[pl.BlockSpec(memory_space=pltpu.SMEM)] * 2
        + [pl.BlockSpec(memory_space=pltpu.VMEM)] * 5,
        out_specs=pl.BlockSpec(memory_space=pltpu.VMEM),
        out_shape=jax.ShapeDtypeStruct(query.shape, jnp.bfloat16),
        scratch_shapes=[pltpu.VMEM((k0.shape[0], BLK), jnp.float32)],
        compiler_params=pltpu.CompilerParams(vmem_limit_bytes=40 * MIB),
        cost_estimate=pl.CostEstimate(
            flops=query.shape[0] * query.shape[1] * k0.shape[0],
            bytes_accessed=4 * 2 * k0.shape[0] * k0.shape[1],
            transcendentals=query.shape[1] * k0.shape[0] // 2,
        ),
        name="attend",
    )(places, counts, query, k0, k1, v0, v1)


def leave_kernel(own_weight, other_weight, own, other, *outs):
    summed = jnp.dot(own_weight[...], own[...], preferred_element_type=jnp.float32)
    summed += jnp.dot(other_weight[...], other[...], preferred_element_type=jnp.float32)
    summed = summed.astype(jnp.bfloat16)
    width = outs[0].shape[1]
    for index, out in enumerate(outs):
        out[...] = summed[:, index * width : (index + 1) * width]


def leave(own_weight, other_weight, own, other, pieces):
    features, inner = own_weight.shape
    count = own.shape[1]
    width = count // pieces
    high = 512
    return pl.pallas_call(
        leave_kernel,
        grid=(features // high,),
        in_specs=[pl.BlockSpec((high, inner), lambda i: (i, 0))] * 2
        + [pl.BlockSpec((inner, count), lambda i: (0, 0))] * 2,
        out_specs=[pl.BlockSpec((high, width), lambda i: (i, 0))] * pieces,
        out_shape=[jax.ShapeDtypeStruct((features, width), jnp.bfloat16)] * pieces,
        compiler_params=pltpu.CompilerParams(vmem_limit_bytes=40 * MIB),
        cost_estimate=pl.CostEstimate(
            flops=4 * features * inner * count,
            bytes_accessed=4 * features * (inner + count),
            transcendentals=0,
        ),
        name="leave",
    )(own_weight, other_weight, own, other)


def shards(tokens, qkv_weight, out_weight, modulation, block_mask):
    rows, local = tokens.shape
    features = modulation.shape[1]
    heads_here = block_mask.shape[0]
    inner = qkv_weight.shape[2]
    head_size = inner // heads_here
    factor = math.log2(math.e) / math.sqrt(head_size)
    core = lax.axis_index("core")
    across = tokens.T

    wide = across.astype(jnp.float32)
    own_center = jnp.mean(wide, axis=0, keepdims=True)
    own_spread = jnp.sum(jnp.square(wide - own_center), axis=0, keepdims=True)
    stats = lax.all_gather(jnp.concatenate([own_center, own_spread], axis=0), HEAD, axis=0)
    center = jnp.mean(stats[:, 0], axis=0, keepdims=True)
    spread = (
        jnp.sum(stats[:, 1], axis=0, keepdims=True)
        + local * jnp.sum(jnp.square(stats[:, 0] - center), axis=0, keepdims=True)
    ) / features
    rate = lax.rsqrt(spread + EPSILON)

    quarter = rows // 4
    xs = [
        lax.all_gather(across[:, i * quarter : (i + 1) * quarter], HEAD, axis=0, tiled=True)
        for i in range(4)
    ]
    weight = jnp.transpose(qkv_weight, (0, 2, 1)).reshape(3 * inner, features)
    gain = jnp.broadcast_to((1.0 + modulation[1])[:, None], (features, BLK))
    shift = jnp.broadcast_to(modulation[0][:, None], (features, BLK))
    own_weight = out_weight.T
    other_weight = lax.ppermute(own_weight, "core", SWAP)

    keep = (block_mask != 0).astype(jnp.int32).reshape(-1, block_mask.shape[2])
    counts = jnp.sum(keep, axis=1)
    blocks = jnp.arange(keep.shape[1], dtype=jnp.int32)
    earlier = blocks[None, :] < blocks[:, None]
    rank = jnp.sum(jnp.where(earlier[None], keep[:, None, :], 0), axis=2)
    chosen = (keep[:, None, :] != 0) & (rank[:, None, :] == blocks[None, :, None])
    places = jnp.sum(jnp.where(chosen, blocks[None, None, :], 0), axis=2)

    query, k0, k1, v0, v1 = project(xs, weight, gain, shift, center, rate)
    k0, k1, v0, v1 = [
        lax.all_gather(part, FRAME, axis=0, tiled=True) for part in (k0, k1, v0, v1)
    ]
    heads = attend(factor, places, counts, query, k0, k1, v0, v1)

    half = rows // 2
    mine = lax.dynamic_slice_in_dim(heads, core * half, half, 1)
    given = lax.dynamic_slice_in_dim(heads, (1 - core) * half, half, 1)
    other = lax.ppermute(given, "core", SWAP)
    shares = leave(own_weight, other_weight, mine, other, 4)
    sums = [lax.psum_scatter(s, CHIP, scatter_dimension=0, tiled=True) for s in shares]
    summed = jnp.concatenate(sums, axis=1)
    kept = lax.dynamic_slice_in_dim(summed, core * local, local, 0)
    given = lax.dynamic_slice_in_dim(summed, (1 - core) * local, local, 0)
    other = lax.ppermute(given, "core", SWAP)
    left = jnp.where(core == 0, kept, other)
    right = jnp.where(core == 0, other, kept)
    projected = jnp.concatenate([left, right], axis=1).astype(jnp.float32)
    first = lax.axis_index(HEAD) * local
    gate = lax.dynamic_slice_in_dim(modulation, first, local, 1)[2][:, None]
    mixed = (wide + gate * projected).astype(jnp.bfloat16)
    return mixed.T


def solution(mesh):
    fine = Mesh(mesh.devices.reshape(2, 4, 2, 4, 2), ("yh", "x", "yl", "z", "core"))
    placed = (
        P(FRAME, HEAD),
        P(None, None, HEAD),
        P(HEAD, None),
        P(),
        P(HEAD, FRAME, None),
    )
    return jax.shard_map(
        shards, mesh=fine, in_specs=placed, out_specs=P(FRAME, HEAD), check_vma=False
    )
```

```python
import math

import jax
import jax.numpy as jnp
from jax import lax
from jax.experimental import pallas as pl
from jax.experimental.pallas import tpu as pltpu
from jax.sharding import Mesh
from jax.sharding import PartitionSpec as P

BLK = 128
EPSILON = 1e-06
NEGATIVE = -1e30
FRAME = ("yh", "x")
HEAD = ("yl", "z", "core")
MIB = 1 << 20
GROUP = 4
CUTS = ((0, 224), (224, 432), (432, 640))


def shift(value, axis, steps):
    count = lax.axis_size(axis)
    return lax.ppermute(value, axis, [(i, (i + steps) % count) for i in range(count)])


def swap(value, axis):
    return shift(value, axis, 1)


def tile_of(rows):
    return {640: 128, 224: 112}.get(rows, rows)


def project_kernel(
    chips, heads, *refs
):
    xs, (own, other, gain, bias), outs, (normed, total) = (
        refs[:10],
        refs[10:14],
        refs[14:22],
        refs[22:],
    )
    step = pl.program_id(0)
    features = normed.shape[0] * normed.shape[1]
    count = normed.shape[2]
    lay = [(piece, 0, x) for piece, x in enumerate(xs[:7])]
    lay += [(7, cut[0], x) for cut, x in zip(CUTS, xs[7:])]

    def fold(values):
        return jnp.sum(values.reshape(values.shape[0] // 8, 8, count), axis=0)

    @pl.when(step == 0)
    def _():
        total[...] = jnp.zeros_like(total)
        summed = jnp.zeros((8, count), jnp.float32)
        for _, _, x in lay:
            tile = tile_of(x.shape[0])

            def add(i, state, x=x, tile=tile):
                wide = x[pl.ds(pl.multiple_of(i * tile, 16), tile), :].astype(jnp.float32)
                return state + fold(wide)

            summed = lax.fori_loop(0, x.shape[0] // tile, add, summed)
        center = jnp.sum(summed, axis=0, keepdims=True) / features
        summed = jnp.zeros((8, count), jnp.float32)
        for _, _, x in lay:
            tile = tile_of(x.shape[0])

            def square(i, state, x=x, tile=tile):
                wide = x[pl.ds(pl.multiple_of(i * tile, 16), tile), :].astype(jnp.float32)
                return state + fold(jnp.square(wide - center))

            summed = lax.fori_loop(0, x.shape[0] // tile, square, summed)
        rate = lax.rsqrt(jnp.sum(summed, axis=0, keepdims=True) / features + EPSILON)
        for piece, first, x in lay:
            tile = tile_of(x.shape[0])

            def norm(i, _, x=x, tile=tile, piece=piece, first=first):
                start = pl.multiple_of(i * tile, 16)
                row = pl.multiple_of(chips[piece] * normed.shape[1] + first + start, 16)
                part_gain = gain[pl.ds(row, tile), :]
                part_bias = bias[pl.ds(row, tile), :]
                for part in range(count // BLK):
                    columns = slice(part * BLK, (part + 1) * BLK)
                    wide = x[pl.ds(start, tile), columns].astype(jnp.float32)
                    value = (wide - center[:, columns]) * rate[:, columns] * part_gain + part_bias
                    normed[
                        piece, pl.ds(pl.multiple_of(first + start, 16), tile), columns
                    ] = value.astype(jnp.bfloat16)
                return 0

            lax.fori_loop(0, x.shape[0] // tile, norm, 0)

    held = normed[step]
    outs_own = own.shape[0]
    total[:outs_own] += jnp.dot(own[...], held, preferred_element_type=jnp.float32)
    total[outs_own:] += jnp.dot(other[...], held, preferred_element_type=jnp.float32)

    @pl.when(step == pl.num_programs(0) - 1)
    def _():
        for index in range(4):
            kv, q = outs[2 * index], outs[2 * index + 1]
            base = pl.multiple_of(heads[index] * BLK, BLK)
            q[...] = total[pl.ds(base, BLK), :].astype(jnp.bfloat16)
            keys = total[pl.ds(base + 2 * BLK, BLK), :]
            for part in range(count // BLK):
                columns = slice(part * BLK, (part + 1) * BLK)
                kv[:BLK, columns] = keys[:, columns].T.astype(jnp.bfloat16)
            kv[BLK:, :] = total[pl.ds(base + 4 * BLK, BLK), :].astype(jnp.bfloat16)


def project(chips, heads, xs, own, other, gain, bias):
    outs, features = own.shape
    deep, count = xs[0].shape
    whole = lambda shape: pl.BlockSpec(shape, lambda k, *_: (0, 0))
    block = pl.BlockSpec((outs, deep), lambda k, chips, heads: (0, chips[k]))
    shapes = [(2 * BLK, count), (BLK, count)] * 4
    return pl.pallas_call(
        project_kernel,
        grid_spec=pltpu.PrefetchScalarGridSpec(
            num_scalar_prefetch=2,
            grid=(features // deep,),
            in_specs=[whole(x.shape) for x in xs]
            + [block, block, whole(gain.shape), whole(bias.shape)],
            out_specs=[whole(s) for s in shapes],
            scratch_shapes=[
                pltpu.VMEM((features // deep, deep, count), jnp.bfloat16),
                pltpu.VMEM((2 * outs, count), jnp.float32),
            ],
        ),
        out_shape=[jax.ShapeDtypeStruct(s, jnp.bfloat16) for s in shapes],
        compiler_params=pltpu.CompilerParams(vmem_limit_bytes=50 * MIB),
        cost_estimate=pl.CostEstimate(
            flops=4 * outs * features * count,
            bytes_accessed=2 * features * (count + 2 * outs),
            transcendentals=0,
        ),
        name="project",
    )(chips, heads, *xs, own, other, gain, bias)


def attend_kernel(factor, places, counts, *refs):
    queries, pieces, outs, (kv, scores, arrived) = refs[:4], refs[4:20], refs[20:24], refs[24:]
    copies = [
        pltpu.make_async_copy(piece, kv.at[index], arrived.at[index])
        for index, piece in enumerate(pieces)
    ]
    for copy in copies:
        copy.start()
    for copy in copies:
        copy.wait()
    per_piece = kv.shape[2] // BLK

    for index, (query_ref, out) in enumerate(zip(queries, outs)):

        def one(block, _):
            row = index * per_piece + block
            column = pl.multiple_of(block * BLK, BLK)
            query = query_ref[:, pl.ds(column, BLK)]
            count = counts[row]
            groups = (count + GROUP - 1) // GROUP

            def rate(group, top):
                for item in range(GROUP):
                    place = group * GROUP + item
                    where = places[row, place]
                    start = pl.multiple_of((where % per_piece) * BLK, BLK)
                    score = jnp.dot(
                        kv[where // per_piece, :BLK, pl.ds(start, BLK)],
                        query,
                        preferred_element_type=jnp.float32,
                    )
                    scores[pl.ds(pl.multiple_of(place * BLK, BLK), BLK), :] = score
                    best = jnp.max(score.reshape(BLK // 8, 8, BLK), axis=0)
                    top = jnp.maximum(top, best + jnp.where(place < count, 0.0, NEGATIVE))
                return top

            top = lax.fori_loop(0, groups, rate, jnp.full((8, BLK), NEGATIVE, jnp.float32))
            top = jnp.max(top, axis=0, keepdims=True) * factor

            def gather(group, state):
                total, summed = state
                weights, held = [], []
                for item in range(GROUP):
                    place = group * GROUP + item
                    score = scores[pl.ds(pl.multiple_of(place * BLK, BLK), BLK), :]
                    offset = top + jnp.where(place < count, 0.0, -NEGATIVE)
                    weight = jnp.exp2(score * factor - offset)
                    total = total + jnp.sum(weight.reshape(BLK // 8, 8, BLK), axis=0)
                    weights.append(weight.astype(jnp.bfloat16))
                    where = places[row, place]
                    start = pl.multiple_of((where % per_piece) * BLK, BLK)
                    held.append(kv[where // per_piece, BLK:, pl.ds(start, BLK)])
                summed = summed + jnp.dot(
                    jnp.concatenate(held, axis=1),
                    jnp.concatenate(weights, axis=0),
                    preferred_element_type=jnp.float32,
                )
                return total, summed

            total, summed = lax.fori_loop(
                0,
                groups,
                gather,
                (jnp.zeros((8, BLK), jnp.float32), jnp.zeros((BLK, BLK), jnp.float32)),
            )
            total = jnp.sum(total, axis=0, keepdims=True)
            out[:, pl.ds(column, BLK)] = (summed / total).astype(jnp.bfloat16)
            return 0

        lax.fori_loop(0, per_piece, one, 0)


def attend(factor, places, counts, queries, pieces):
    def kernel(*refs):
        attend_kernel(factor, *refs)

    shape = queries[0].shape
    tokens = len(pieces) * shape[1]
    return pl.pallas_call(
        kernel,
        in_specs=[pl.BlockSpec(memory_space=pltpu.SMEM)] * 2
        + [pl.BlockSpec(memory_space=pltpu.VMEM)] * len(queries)
        + [pl.BlockSpec(memory_space=pl.ANY)] * len(pieces),
        out_specs=[pl.BlockSpec(memory_space=pltpu.VMEM)] * len(queries),
        out_shape=[jax.ShapeDtypeStruct(shape, jnp.bfloat16)] * len(queries),
        scratch_shapes=[
            pltpu.VMEM((len(pieces), *pieces[0].shape), jnp.bfloat16),
            pltpu.VMEM((tokens, BLK), jnp.float32),
            pltpu.SemaphoreType.DMA((len(pieces),)),
        ],
        compiler_params=pltpu.CompilerParams(vmem_limit_bytes=40 * MIB),
        cost_estimate=pl.CostEstimate(
            flops=tokens * BLK * shape[1] * len(queries),
            bytes_accessed=4 * tokens * BLK,
            transcendentals=tokens * shape[1],
        ),
        name="attend",
    )(places, counts, *queries, *pieces)


def leave_kernel(plan, chips, columns, *refs):
    weights, heads, rest = refs[:4], refs[4:8], refs[8:]
    step = pl.program_id(0)
    summed = jnp.dot(
        jnp.concatenate([weight[...] for weight in weights], axis=1),
        jnp.concatenate([head[...] for head in heads], axis=0),
        preferred_element_type=jnp.float32,
    )
    adds = sum(len(given) for given, _ in plan)
    taken, outs = rest[:adds], list(rest[adds:])
    at = 0
    for index, (given, cuts) in enumerate(plan):
        here = taken[at : at + len(given)]
        at += len(given)
        mine = [outs.pop(0) for _ in cuts]

        @pl.when(step == index)
        def _():
            for cut, out in zip(cuts, mine):
                value = summed[cut[0] : cut[1]]
                parts = []
                for (first, last), ref in zip(given, here):
                    if (first, last) == cut:
                        value = value + ref[...].astype(jnp.float32)
                    else:
                        parts.append((first, last, ref))
                if parts:
                    ((first, last, ref),) = parts
                    middle = value[first:last] + ref[...].astype(jnp.float32)
                    pieces = [value[:first]] if first else []
                    pieces.append(middle)
                    pieces += [value[last:]] if last < cut[1] else []
                    value = jnp.concatenate(pieces, axis=0)
                out[...] = value.astype(out.dtype)


def leave(chips, columns, weight, heads, plan, taken):
    high = CUTS[-1][1]
    count = heads[0].shape[1]
    steps = len(plan)

    def block(index):
        return pl.BlockSpec((high, BLK), lambda i, chips, columns: (chips[i], columns[index]))

    whole = lambda shape: pl.BlockSpec(shape, lambda i, *_: (0, 0))
    shapes = [(cut[1] - cut[0], count) for _, cuts in plan for cut in cuts]

    def kernel(*refs):
        leave_kernel(plan, *refs)

    return pl.pallas_call(
        kernel,
        grid_spec=pltpu.PrefetchScalarGridSpec(
            num_scalar_prefetch=2,
            grid=(steps,),
            in_specs=[block(i) for i in range(4)]
            + [whole(h.shape) for h in heads]
            + [whole(t.shape) for t in taken],
            out_specs=[whole(s) for s in shapes],
        ),
        out_shape=[jax.ShapeDtypeStruct(s, jnp.bfloat16) for s in shapes],
        compiler_params=pltpu.CompilerParams(vmem_limit_bytes=40 * MIB),
        cost_estimate=pl.CostEstimate(
            flops=2 * steps * high * 4 * BLK * count,
            bytes_accessed=2 * steps * high * (4 * BLK + count),
            transcendentals=0,
        ),
        name="leave",
    )(chips, columns, *[weight] * 4, *heads, *taken)


def gather_tokens(own):
    below = shift(own, "z", 1)
    above = shift(own, "z", -1)
    beside = swap(own, "yl")
    far = shift(below, "z", 1)
    beside_below = swap(below, "yl")
    beside_above = shift(beside, "z", -1)
    first, second, third = [slice(*cut) for cut in CUTS]
    parts = [
        swap(far[first], "yl"),
        shift(beside_above[second], "z", -1),
        shift(beside_below[third], "z", 1),
    ]
    places = [(0, 0), (0, -1), (0, 1), (1, 0), (0, 2), (1, -1), (1, 1), (1, 2)]
    return places, [own, below, above, beside, far, beside_below, beside_above, *parts]


def shards(tokens, qkv_weight, out_weight, modulation, block_mask):
    rows, local = tokens.shape
    features = modulation.shape[1]
    heads_here = block_mask.shape[0]
    inner = qkv_weight.shape[2]
    head_size = inner // heads_here
    factor = math.log2(math.e) / math.sqrt(head_size)
    half = rows // 2
    core = lax.axis_index("core")
    frame_x, frame_y = lax.axis_index("x"), lax.axis_index("yh")
    chip_y, chip_z = lax.axis_index("yl"), lax.axis_index("z")
    across = tokens.T

    def chip(dy, dz):
        return ((chip_y + dy) % 2) * 4 + (chip_z + dz) % 4

    def mine_and_given(value, axis):
        size = value.shape[axis] // 2
        mine = lax.dynamic_slice_in_dim(value, core * size, size, axis)
        return mine, lax.dynamic_slice_in_dim(value, (1 - core) * size, size, axis)

    def head_slot(steps):
        head = (frame_x + steps) % 4
        return jnp.where(head // 2 == core, 0, 1), head % 2

    mine, given = mine_and_given(across, 1)
    other = swap(given, "core")
    own = jnp.concatenate(
        [jnp.where(core == 0, mine, other), jnp.where(core == 0, other, mine)], axis=0
    )
    places, xs = gather_tokens(own)

    own_weight = jnp.transpose(qkv_weight, (0, 2, 1)).reshape(3 * inner, features)
    other_weight = swap(own_weight, "core")
    gain = jnp.broadcast_to((1.0 + modulation[1])[:, None], (features, BLK))
    bias = jnp.broadcast_to(modulation[0][:, None], (features, BLK))
    leaving = jnp.concatenate([out_weight, swap(out_weight, "core")], axis=0).T

    mask_mine, mask_given = mine_and_given(block_mask, 1)
    mask_heads = jnp.stack([mask_mine, swap(mask_given, "core")])
    mask_rows = []
    for steps in range(4):
        side, slot = head_slot(steps)
        part = lax.dynamic_slice(
            mask_heads, (side, slot, 0, 0), (1, 1, *mask_heads.shape[2:])
        )[0, 0]
        mask_rows.append(shift(part, "x", steps) if steps else part)
    keep = jnp.concatenate(mask_rows, axis=0) != 0
    blocks = jnp.arange(keep.shape[1], dtype=jnp.int32)
    per_core = half // BLK
    piece, inside = blocks // per_core, blocks % per_core
    from_core, from_y, from_x = core ^ (piece // 8), frame_y ^ (piece // 4 % 2), (frame_x - piece % 4) % 4
    origin = (from_y * 4 + from_x) * (2 * per_core) + from_core * per_core + inside
    same = origin[:, None] == blocks[None, :]
    keep = jnp.sum(jnp.where(same[None] & keep[:, None, :], 1, 0), axis=2)
    counts = jnp.sum(keep, axis=1)
    earlier = blocks[None, :] < blocks[:, None]
    rank = jnp.sum(jnp.where(earlier[None], keep[:, None, :], 0), axis=2)
    chosen = (keep[:, None, :] != 0) & (rank[:, None, :] == blocks[None, :, None])
    listed = jnp.sum(jnp.where(chosen, blocks[None, None, :], 0), axis=2)

    chips = jnp.stack([chip(*place) for place in places]).astype(jnp.int32)
    slots = [head_slot(steps) for steps in range(4)]
    bases = jnp.stack([side * 3 * heads_here + slot for side, slot in slots]).astype(jnp.int32)
    made = project(chips, bases, xs, own_weight, other_weight, gain, bias)
    order = (0, 1, 3, 2)
    kv = {0: made[0]}
    for steps in order[1:]:
        kv[steps] = shift(made[2 * steps], "x", steps)
    queries = [made[1]] + [shift(made[2 * steps + 1], "x", steps) for steps in (1, 2, 3)]
    away = {steps: swap(kv[steps], "yh") for steps in order}
    pieces = [kv[i] for i in range(4)] + [away[i] for i in range(4)]
    pieces += [swap(p, "core") for p in pieces]
    heads = attend(factor, listed, counts, queries, pieces)
    heads = [heads[0]] + [shift(heads[steps], "x", -steps) for steps in (1, 2, 3)]

    columns = jnp.stack([side * heads_here + slot for side, slot in slots]).astype(jnp.int32)
    whole = CUTS[0][0], CUTS[-1][1]

    def shares(targets, plan, *taken):
        chips = jnp.stack([chip(*target) for target in targets]).astype(jnp.int32)
        return leave(chips, columns, leaving, heads, plan, taken)

    parts = shares([(1, 2)], [((), CUTS)])
    first = swap(parts[0], "yl")
    second = shift(parts[1], "z", 1)
    third = shift(parts[2], "z", -1)
    down, up, side = shares(
        [(0, 2), (1, 1), (1, -1)],
        [((CUTS[0],), (whole,)), ((CUTS[1],), (whole,)), ((CUTS[2],), (whole,))],
        first,
        second,
        third,
    )
    down, up, side = shift(down, "z", -1), shift(up, "z", 1), swap(side, "yl")
    down, up, side = shares(
        [(0, -1), (0, 1), (1, 0)],
        [((whole, whole), (whole,)), ((), (whole,)), ((whole,), (whole,))],
        down,
        side,
        up,
    )
    down, up, side = shift(down, "z", -1), shift(up, "z", 1), swap(side, "yl")
    (summed,) = shares([(0, 0)], [((whole, whole, whole), (whole,))], down, up, side)

    kept, given = mine_and_given(summed, 0)
    other = swap(given, "core")
    projected = jnp.concatenate(
        [jnp.where(core == 0, kept, other), jnp.where(core == 0, other, kept)], axis=1
    ).astype(jnp.float32)
    start = lax.axis_index(HEAD) * local
    gate = lax.dynamic_slice_in_dim(modulation, start, local, 1)[2][:, None]
    return (across.astype(jnp.float32) + gate * projected).astype(jnp.bfloat16).T


def solution(mesh):
    fine = Mesh(mesh.devices.reshape(2, 4, 2, 4, 2), ("yh", "x", "yl", "z", "core"))
    placed = (
        P(FRAME, HEAD),
        P(None, None, HEAD),
        P(HEAD, None),
        P(),
        P(HEAD, FRAME, None),
    )
    return jax.shard_map(
        shards, mesh=fine, in_specs=placed, out_specs=P(FRAME, HEAD), check_vma=False
    )
```

```python
import functools
import math

import jax
import jax.numpy as jnp
from jax import lax
from jax.experimental import pallas as pl
from jax.experimental.pallas import tpu as pltpu
from jax.sharding import Mesh
from jax.sharding import PartitionSpec as P

BLK = 128
EPSILON = 1e-06
NEGATIVE = -1e30
FRAME = ("yh", "x")
HEAD = ("yl", "z", "core")
MIB = 1 << 20
PAIRS = 8
CUTS = ((0, 224), (224, 432), (432, 640))


DEEP = CUTS[-1][1]


def shift(value, axis, steps):
    count = lax.axis_size(axis)
    return lax.ppermute(value, axis, [(i, (i + steps) % count) for i in range(count)])


def swap(value, axis):
    return shift(value, axis, 1)


def tile_of(rows):
    return {640: 128, 224: 112}.get(rows, rows)


def prepare_kernel(qkv, leaving, modulation, _, weight, gain, bias, leaving_out):
    inner = qkv.shape[2]
    for part in range(3):
        weight[part * inner : (part + 1) * inner, :] = qkv[part].T
    leaving_out[...] = leaving[...].T
    for row, out, add in ((1, gain, 1.0), (0, bias, 0.0)):
        for part in range(out.shape[0] // BLK):
            rows = slice(part * BLK, (part + 1) * BLK)
            line = modulation[row : row + 1, rows] + add
            out[rows, :] = jnp.broadcast_to(line, (BLK, BLK)).T


def prepare(qkv_weight, out_weight, modulation, after):
    _, features, inner = qkv_weight.shape
    deep = 512
    return pl.pallas_call(
        prepare_kernel,
        grid=(features // deep,),
        in_specs=[
            pl.BlockSpec((3, deep, inner), lambda i: (0, i, 0)),
            pl.BlockSpec((out_weight.shape[0], deep), lambda i: (0, i)),
            pl.BlockSpec((3, deep), lambda i: (0, i)),
            pl.BlockSpec(memory_space=pl.ANY),
        ],
        out_specs=[
            pl.BlockSpec((3 * inner, deep), lambda i: (0, i)),
            pl.BlockSpec((deep, BLK), lambda i: (i, 0)),
            pl.BlockSpec((deep, BLK), lambda i: (i, 0)),
            pl.BlockSpec((deep, out_weight.shape[0]), lambda i: (i, 0)),
        ],
        out_shape=[
            jax.ShapeDtypeStruct((3 * inner, features), jnp.bfloat16),
            jax.ShapeDtypeStruct((features, BLK), jnp.float32),
            jax.ShapeDtypeStruct((features, BLK), jnp.float32),
            jax.ShapeDtypeStruct((features, out_weight.shape[0]), jnp.bfloat16),
        ],
        compiler_params=pltpu.CompilerParams(vmem_limit_bytes=24 * MIB),
        cost_estimate=pl.CostEstimate(
            flops=0, bytes_accessed=16 * features * inner, transcendentals=0
        ),
        name="prepare",
    )(qkv_weight, out_weight, modulation, after)


def together(*arrays):
    return pl.pallas_call(
        lambda *refs: None,
        in_specs=[pl.BlockSpec(memory_space=pl.ANY)] * len(arrays),
        out_specs=[pl.BlockSpec(memory_space=pl.ANY)] * len(arrays),
        out_shape=[jax.ShapeDtypeStruct(a.shape, a.dtype) for a in arrays],
        input_output_aliases={i: i for i in range(len(arrays))},
        name="together",
    )(*arrays)


def project_kernel(
    chips, heads, *refs
):
    xs, weights, (gain, bias), rest = refs[:10], refs[10:14], refs[14:16], refs[16:]
    (kv0, q0, *packed), (normed, total) = rest[-7:-2], rest[-2:]
    step = pl.program_id(0)
    features = 8 * DEEP
    count = normed.shape[2]
    lay = [(piece, 0, x) for piece, x in enumerate(xs[:7])]
    lay += [(7, cut[0], x) for cut, x in zip(CUTS, xs[7:])]

    def fold(values):
        return jnp.sum(values.reshape(values.shape[0] // 8, 8, count), axis=0)

    @pl.when(step == 0)
    def _():
        total[...] = jnp.zeros_like(total)
        summed = jnp.zeros((8, count), jnp.float32)
        for _, _, x in lay:
            tile = tile_of(x.shape[0])

            def add(i, state, x=x, tile=tile):
                wide = x[pl.ds(pl.multiple_of(i * tile, 16), tile), :].astype(jnp.float32)
                return state + fold(wide)

            summed = lax.fori_loop(0, x.shape[0] // tile, add, summed)
        center = jnp.sum(summed, axis=0, keepdims=True) / features
        summed = jnp.zeros((8, count), jnp.float32)
        for _, _, x in lay:
            tile = tile_of(x.shape[0])

            def square(i, state, x=x, tile=tile):
                wide = x[pl.ds(pl.multiple_of(i * tile, 16), tile), :].astype(jnp.float32)
                return state + fold(jnp.square(wide - center))

            summed = lax.fori_loop(0, x.shape[0] // tile, square, summed)
        rate = lax.rsqrt(jnp.sum(summed, axis=0, keepdims=True) / features + EPSILON)
        for piece, first, x in lay:
            tile = tile_of(x.shape[0])

            def norm(i, _, x=x, tile=tile, piece=piece, first=first):
                start = pl.multiple_of(i * tile, 16)
                row = pl.multiple_of(chips[piece] * DEEP + first + start, 16)
                part_gain = gain[pl.ds(row, tile), :]
                part_bias = bias[pl.ds(row, tile), :]
                for part in range(count // BLK):
                    columns = slice(part * BLK, (part + 1) * BLK)
                    wide = x[pl.ds(start, tile), columns].astype(jnp.float32)
                    value = (wide - center[:, columns]) * rate[:, columns] * part_gain + part_bias
                    normed[
                        piece // 2,
                        pl.ds(pl.multiple_of(piece % 2 * DEEP + first + start, 16), tile),
                        columns,
                    ] = value.astype(jnp.bfloat16)
                return 0

            lax.fori_loop(0, x.shape[0] // tile, norm, 0)

    held = normed[step]
    outs = total.shape[0] // 2
    for side in range(2):
        weight = jnp.concatenate([w[...] for w in weights[2 * side : 2 * side + 2]], axis=1)
        total[side * outs : (side + 1) * outs] += jnp.dot(
            weight, held, preferred_element_type=jnp.float32
        )

    @pl.when(step == pl.num_programs(0) - 1)
    def _():
        for index in range(4):
            if index:
                kv, q = packed[index - 1], packed[index - 1].at[2 * BLK :]
            else:
                kv, q = kv0, q0
            base = pl.multiple_of(heads[index] * BLK, BLK)
            q[...] = total[pl.ds(base, BLK), :].astype(jnp.bfloat16)
            keys = total[pl.ds(base + 2 * BLK, BLK), :]
            for part in range(count // BLK):
                columns = slice(part * BLK, (part + 1) * BLK)
                kv[:BLK, columns] = keys[:, columns].T.astype(jnp.bfloat16)
            kv[BLK : 2 * BLK, :] = total[pl.ds(base + 4 * BLK, BLK), :].astype(jnp.bfloat16)


def project(chips, heads, xs, own, other, gain, bias, after):
    outs, features = own.shape
    deep, count = xs[0].shape
    whole = lambda shape: pl.BlockSpec(shape, lambda k, *_: (0, 0))
    blocks = [
        pl.BlockSpec((outs, deep), lambda k, chips, heads, i=i: (0, chips[2 * k + i]))
        for i in range(2)
    ]
    shapes = [(2 * BLK, count), (BLK, count)] + [(3 * BLK, count)] * 3
    return pl.pallas_call(
        project_kernel,
        grid_spec=pltpu.PrefetchScalarGridSpec(
            num_scalar_prefetch=2,
            grid=(features // deep // 2,),
            in_specs=[whole(x.shape) for x in xs]
            + [*blocks, *blocks, whole(gain.shape), whole(bias.shape)]
            + [pl.BlockSpec(memory_space=pl.ANY)] * len(after),
            out_specs=[whole(s) for s in shapes],
            scratch_shapes=[
                pltpu.VMEM((features // deep // 2, 2 * deep, count), jnp.bfloat16),
                pltpu.VMEM((2 * outs, count), jnp.float32),
            ],
        ),
        out_shape=[jax.ShapeDtypeStruct(s, jnp.bfloat16) for s in shapes],
        compiler_params=pltpu.CompilerParams(vmem_limit_bytes=50 * MIB),
        cost_estimate=pl.CostEstimate(
            flops=4 * outs * features * count,
            bytes_accessed=2 * features * (count + 2 * outs),
            transcendentals=0,
        ),
        name="project",
    )(chips, heads, *xs, own, own, other, other, gain, bias, *after)


def attend_kernel(factor, unroll, plan, places, counts, first, owner, *refs):
    arrays, outs, rest = refs[: -4 - 8], refs[-4 - 8 : -8], refs[-8:]
    kv, query, asked, scores, tops, totals, sums, arrived = rest
    copies = []
    for kind, index, array, start in plan:
        to = (kv if kind == "kv" else query).at[index]
        rows = to.shape[0]
        copies.append(
            pltpu.make_async_copy(
                arrays[array].at[start : start + rows], to, arrived.at[len(copies)]
            )
        )
    for copy in copies:
        copy.start()
    per_piece = kv.shape[2] // BLK
    rows = len(outs) * per_piece
    tops[...] = jnp.full_like(tops, NEGATIVE)
    totals[...] = jnp.zeros_like(totals)
    sums[...] = jnp.zeros_like(sums)
    for copy in copies:
        copy.wait()
    for index in range(len(outs)):
        for part in range(per_piece):
            asked[index * per_piece + part] = query[index, :, part * BLK : (part + 1) * BLK]

    def find(pair, low, high):
        live = pair < high
        pair = jnp.where(live, pair, low)
        row = owner[pair]
        place = 2 * (pair - first[row])
        wheres = [places[row, place], places[row, place + 1]]
        offsets = [
            jnp.where(live, 0.0, NEGATIVE),
            jnp.where(live & (place + 1 < counts[row]), 0.0, NEGATIVE),
        ]
        return row, wheres, offsets

    def held(where, part):
        start = pl.multiple_of((where & (per_piece - 1)) * BLK, BLK)
        return kv[where >> 2, part * BLK : (part + 1) * BLK, pl.ds(start, BLK)]

    def fold(op, value):
        return op(value.reshape(BLK // 8, 8, BLK), axis=0)

    def rate(low, high, step, _):
        found = []
        for item in range(unroll):
            pair = step * unroll + item
            row, wheres, offsets = find(low + pair, low, high)
            keys = jnp.concatenate([held(where, 0) for where in wheres], axis=0)
            score = jnp.dot(keys, asked[row], preferred_element_type=jnp.float32)
            scores[pair] = score
            best = jnp.maximum(
                fold(jnp.max, score[:BLK]) + offsets[0], fold(jnp.max, score[BLK:]) + offsets[1]
            )
            found.append((row, best))
        for row, best in found:
            tops[row] = jnp.maximum(tops[row], best)
        return 0

    def gather(low, high, step, _):
        found = []
        for item in range(unroll):
            pair = step * unroll + item
            row, wheres, offsets = find(low + pair, low, high)
            top = tops[row][:1]
            score = scores[pair]
            halves = [
                jnp.exp2(score[part * BLK : (part + 1) * BLK] * factor - (top - offsets[part]))
                for part in range(2)
            ]
            total = fold(jnp.sum, halves[0]) + fold(jnp.sum, halves[1])
            weights = jnp.concatenate([half.astype(jnp.bfloat16) for half in halves], axis=0)
            values = jnp.concatenate([held(where, 1) for where in wheres], axis=1)
            summed = jnp.dot(values, weights, preferred_element_type=jnp.float32)
            found.append((row, total, summed))
        for row, total, summed in found:
            totals[row] += total
            sums[row] += summed
        return 0

    for index in range(len(outs)):
        low, high = first[index * per_piece], first[(index + 1) * per_piece]
        steps = (high - low + unroll - 1) // unroll
        lax.fori_loop(0, steps, functools.partial(rate, low, high), 0)
        for row in range(index * per_piece, (index + 1) * per_piece):
            top = jnp.max(tops[row], axis=0, keepdims=True) * factor
            tops[row] = jnp.broadcast_to(top, tops.shape[1:])
        lax.fori_loop(0, steps, functools.partial(gather, low, high), 0)

    for index, out in enumerate(outs):
        for part in range(per_piece):
            row = index * per_piece + part
            total = jnp.sum(totals[row], axis=0, keepdims=True)
            out[:, part * BLK : (part + 1) * BLK] = (sums[row] / total).astype(jnp.bfloat16)


def pair_lists(counts, most):
    twos = (counts + 1) // 2
    rows = counts.shape[0]
    order = jnp.arange(rows + 1, dtype=jnp.int32)
    first = jnp.sum(jnp.where(order[None, :rows] < order[:, None], twos[None, :], 0), axis=1)
    slots = jnp.arange(rows * most // 2, dtype=jnp.int32)
    return first, jnp.sum(jnp.where(first[None, 1:] <= slots[:, None], 1, 0), axis=1)


def attend(factor, lists, plan, arrays, count):
    rows, most = lists[0].shape
    pieces = most * BLK // count
    asking = rows * BLK // count

    def kernel(*refs):
        attend_kernel(factor, PAIRS, plan, *refs)

    shape = (BLK, count)
    return pl.pallas_call(
        kernel,
        in_specs=[pl.BlockSpec(memory_space=pltpu.SMEM)] * len(lists)
        + [pl.BlockSpec(memory_space=pl.ANY)] * len(arrays),
        out_specs=[pl.BlockSpec(memory_space=pltpu.VMEM)] * asking,
        out_shape=[jax.ShapeDtypeStruct(shape, jnp.bfloat16)] * asking,
        scratch_shapes=[
            pltpu.VMEM((pieces, 2 * BLK, count), jnp.bfloat16),
            pltpu.VMEM((asking, *shape), jnp.bfloat16),
            pltpu.VMEM((rows, BLK, BLK), jnp.bfloat16),
            pltpu.VMEM((rows * most // 2 // asking + PAIRS, 2 * BLK, BLK), jnp.float32),
            pltpu.VMEM((rows, 8, BLK), jnp.float32),
            pltpu.VMEM((rows, 8, BLK), jnp.float32),
            pltpu.VMEM((rows, BLK, BLK), jnp.float32),
            pltpu.SemaphoreType.DMA((len(plan),)),
        ],
        compiler_params=pltpu.CompilerParams(vmem_limit_bytes=32 * MIB),
        cost_estimate=pl.CostEstimate(
            flops=rows * BLK * most * BLK * BLK,
            bytes_accessed=4 * most * BLK * BLK,
            transcendentals=rows * BLK * most * BLK // 4,
        ),
        name="attend",
    )(*lists, *arrays)


def leave_kernel(plan, chips, columns, *refs):
    weights, heads, rest, ordered = refs[:2], refs[2:6], refs[6:-1], refs[-1]
    step = pl.program_id(0)

    @pl.when(step == 0)
    def _():
        for index, head in enumerate(heads):
            ordered[pl.ds(pl.multiple_of(columns[index] * BLK, BLK), BLK), :] = head[...]

    summed = jnp.dot(
        jnp.concatenate([weight[...] for weight in weights], axis=1),
        ordered[...],
        preferred_element_type=jnp.float32,
    )
    adds = sum(len(given) for given, _ in plan)
    taken, outs = rest[:adds], list(rest[adds:])
    at = 0
    for index, (given, cuts) in enumerate(plan):
        here = taken[at : at + len(given)]
        at += len(given)
        mine = [outs.pop(0) for _ in cuts]

        @pl.when(step == index)
        def _():
            for cut, out in zip(cuts, mine):
                value = summed[cut[0] : cut[1]]
                parts = []
                for (first, last), ref in zip(given, here):
                    if (first, last) == cut:
                        value = value + ref[...].astype(jnp.float32)
                    else:
                        parts.append((first, last, ref))
                if parts:
                    ((first, last, ref),) = parts
                    middle = value[first:last] + ref[...].astype(jnp.float32)
                    pieces = [value[:first]] if first else []
                    pieces.append(middle)
                    pieces += [value[last:]] if last < cut[1] else []
                    value = jnp.concatenate(pieces, axis=0)
                out[...] = value.astype(out.dtype)


def leave(chips, columns, weights, heads, plan, taken):
    high = CUTS[-1][1]
    count = heads[0].shape[1]
    steps = len(plan)
    inner = weights[0].shape[1]
    block = pl.BlockSpec((high, inner), lambda i, chips, columns: (chips[i], 0))
    whole = lambda shape: pl.BlockSpec(shape, lambda i, *_: (0, 0))
    shapes = [(cut[1] - cut[0], count) for _, cuts in plan for cut in cuts]

    def kernel(*refs):
        leave_kernel(plan, *refs)

    return pl.pallas_call(
        kernel,
        grid_spec=pltpu.PrefetchScalarGridSpec(
            num_scalar_prefetch=2,
            grid=(steps,),
            in_specs=[block] * 2
            + [whole(h.shape) for h in heads]
            + [whole(t.shape) for t in taken],
            out_specs=[whole(s) for s in shapes],
            scratch_shapes=[pltpu.VMEM((2 * inner, count), jnp.bfloat16)],
        ),
        out_shape=[jax.ShapeDtypeStruct(s, jnp.bfloat16) for s in shapes],
        compiler_params=pltpu.CompilerParams(vmem_limit_bytes=32 * MIB),
        cost_estimate=pl.CostEstimate(
            flops=4 * steps * high * inner * count,
            bytes_accessed=2 * steps * high * (2 * inner + count),
            transcendentals=0,
        ),
        name="leave",
    )(chips, columns, *weights, *heads, *taken)


def gather_tokens(own):
    below = shift(own, "z", 1)
    above = shift(own, "z", -1)
    beside = swap(own, "yl")
    below, above, beside = together(below, above, beside)
    far = shift(below, "z", 1)
    beside_below = swap(below, "yl")
    beside_above = shift(beside, "z", -1)
    first, second, third = [slice(*cut) for cut in CUTS]
    parts = [
        swap(far[first], "yl"),
        shift(beside_above[second], "z", -1),
        shift(beside_below[third], "z", 1),
    ]
    places = [(0, 0), (0, -1), (0, 1), (1, 0), (0, 2), (1, -1), (1, 1), (1, 2)]
    return places, [own, below, above, beside, far, beside_below, beside_above, *parts]


def shards(tokens, qkv_weight, out_weight, modulation, block_mask):
    rows, local = tokens.shape
    features = modulation.shape[1]
    heads_here = block_mask.shape[0]
    inner = qkv_weight.shape[2]
    head_size = inner // heads_here
    factor = math.log2(math.e) / math.sqrt(head_size)
    half = rows // 2
    core = lax.axis_index("core")
    frame_x, frame_y = lax.axis_index("x"), lax.axis_index("yh")
    chip_y, chip_z = lax.axis_index("yl"), lax.axis_index("z")
    across = tokens.T

    def chip(dy, dz):
        return ((chip_y + dy) % 2) * 4 + (chip_z + dz) % 4

    def mine_and_given(value, axis):
        size = value.shape[axis] // 2
        mine = lax.dynamic_slice_in_dim(value, core * size, size, axis)
        return mine, lax.dynamic_slice_in_dim(value, (1 - core) * size, size, axis)

    def head_slot(steps):
        head = (frame_x + steps) % 4
        return jnp.where(head // 2 == core, 0, 1), head % 2

    mine, given = mine_and_given(across, 1)
    other = swap(given, "core")
    own = jnp.concatenate(
        [jnp.where(core == 0, mine, other), jnp.where(core == 0, other, mine)], axis=0
    )
    places, xs = gather_tokens(own)

    own_weight, gain, bias, leaving = prepare(qkv_weight, out_weight, modulation, own)
    other_weight = swap(own_weight, "core")
    leaving = leaving, swap(leaving, "core")

    mask_mine, mask_given = mine_and_given(block_mask, 1)
    mask_heads = jnp.stack([mask_mine, swap(mask_given, "core")])
    mask_rows = []
    for steps in range(4):
        side, slot = head_slot(steps)
        part = lax.dynamic_slice(
            mask_heads, (side, slot, 0, 0), (1, 1, *mask_heads.shape[2:])
        )[0, 0]
        mask_rows.append(shift(part, "x", steps) if steps else part)
    keep = jnp.concatenate(mask_rows, axis=0) != 0
    blocks = jnp.arange(keep.shape[1], dtype=jnp.int32)
    per_core = half // BLK
    piece, inside = blocks // per_core, blocks % per_core
    from_core, from_y, from_x = core ^ (piece // 8), frame_y ^ (piece // 4 % 2), (frame_x - piece % 4) % 4
    origin = (from_y * 4 + from_x) * (2 * per_core) + from_core * per_core + inside
    same = origin[:, None] == blocks[None, :]
    keep = jnp.sum(jnp.where(same[None] & keep[:, None, :], 1, 0), axis=2)
    counts = jnp.sum(keep, axis=1)
    earlier = blocks[None, :] < blocks[:, None]
    rank = jnp.sum(jnp.where(earlier[None], keep[:, None, :], 0), axis=2)
    chosen = (keep[:, None, :] != 0) & (rank[:, None, :] == blocks[None, :, None])
    listed = jnp.sum(jnp.where(chosen, blocks[None, None, :], 0), axis=2)

    chips = jnp.stack([chip(*place) for place in places]).astype(jnp.int32)
    slots = [head_slot(steps) for steps in range(4)]
    bases = jnp.stack([side * 3 * heads_here + slot for side, slot in slots]).astype(jnp.int32)
    lists = (listed, counts, *pair_lists(counts, listed.shape[1]))
    kv, query, *packed = project(
        chips, bases, xs, own_weight, other_weight, gain, bias, (*lists, leaving[1])
    )
    two, one, three = [shift(packed[i - 1], "x", i) for i in (2, 1, 3)]
    both = jnp.concatenate([one[: 2 * BLK], three[: 2 * BLK]], axis=0)
    last = two[: 2 * BLK]
    away = [swap(part, "yh") for part in (kv, both, last)]
    near = jnp.concatenate([kv, both, last], axis=0)
    arrays = [kv, query, one, two, three, *away, swap(near, "core"), *[swap(a, "core") for a in away]]
    step = 2 * BLK
    plan = [("kv", 0, 0, 0), ("q", 0, 1, 0)]
    for steps, array in ((1, 2), (2, 3), (3, 4)):
        plan += [("kv", steps, array, 0), ("q", steps, array, step)]
    for index, array in ((4, 5), (12, 9)):
        plan += [("kv", index, array, 0), ("kv", index + 1, array + 1, 0)]
        plan += [("kv", index + 3, array + 1, step), ("kv", index + 2, array + 2, 0)]
    plan += [("kv", 8 + steps, 8, at * step) for at, steps in enumerate((0, 1, 3, 2))]
    heads = attend(factor, lists, plan, arrays, half)
    heads = [heads[0]] + [shift(heads[steps], "x", -steps) for steps in (1, 2, 3)]

    columns = jnp.stack([side * heads_here + slot for side, slot in slots]).astype(jnp.int32)
    whole = CUTS[0][0], CUTS[-1][1]

    def shares(targets, plan, *taken):
        chips = jnp.stack([chip(*target) for target in targets]).astype(jnp.int32)
        return leave(chips, columns, leaving, heads, plan, taken)

    parts = shares([(1, 2)], [((), CUTS)])
    first = swap(parts[0], "yl")
    second = shift(parts[1], "z", 1)
    third = shift(parts[2], "z", -1)
    down, up, side = shares(
        [(0, 2), (1, 1), (1, -1)],
        [((CUTS[0],), (whole,)), ((CUTS[1],), (whole,)), ((CUTS[2],), (whole,))],
        first,
        second,
        third,
    )
    down, up, side = shift(down, "z", -1), shift(up, "z", 1), swap(side, "yl")
    down, up, side = shares(
        [(0, -1), (0, 1), (1, 0)],
        [((whole, whole), (whole,)), ((), (whole,)), ((whole,), (whole,))],
        down,
        side,
        up,
    )
    down, up, side = shift(down, "z", -1), shift(up, "z", 1), swap(side, "yl")
    (summed,) = shares([(0, 0)], [((whole, whole, whole), (whole,))], down, up, side)

    kept, given = mine_and_given(summed, 0)
    other = swap(given, "core")
    projected = jnp.concatenate(
        [jnp.where(core == 0, kept, other), jnp.where(core == 0, other, kept)], axis=1
    ).astype(jnp.float32)
    start = lax.axis_index(HEAD) * local
    gate = lax.dynamic_slice_in_dim(modulation, start, local, 1)[2][:, None]
    return (across.astype(jnp.float32) + gate * projected).astype(jnp.bfloat16).T


def solution(mesh):
    fine = Mesh(mesh.devices.reshape(2, 4, 2, 4, 2), ("yh", "x", "yl", "z", "core"))
    placed = (
        P(FRAME, HEAD),
        P(None, None, HEAD),
        P(HEAD, None),
        P(),
        P(HEAD, FRAME, None),
    )
    return jax.shard_map(
        shards, mesh=fine, in_specs=placed, out_specs=P(FRAME, HEAD), check_vma=False
    )
```

```python
import functools
import math

import jax
import jax.numpy as jnp
from jax import lax
from jax.experimental import pallas as pl
from jax.experimental.pallas import tpu as pltpu
from jax.sharding import Mesh
from jax.sharding import PartitionSpec as P

BLK = 128
EPSILON = 1e-06
NEGATIVE = -1e30
FRAME = ("yh", "x")
HEAD = ("yl", "z", "core")
MIB = 1 << 20
PAIRS = 8
CUTS = ((0, 224), (224, 432), (432, 640))


DEEP = CUTS[-1][1]


def shift(value, axis, steps):
    count = lax.axis_size(axis)
    return lax.ppermute(value, axis, [(i, (i + steps) % count) for i in range(count)])


def swap(value, axis):
    return shift(value, axis, 1)


def tile_of(rows):
    return {640: 128, 224: 112}.get(rows, rows)


def turn_kernel(weight, out):
    inner = weight.shape[2]
    for part in range(weight.shape[0]):
        out[part * inner : (part + 1) * inner, :] = weight[part].T


def turn(weight):
    parts, features, inner = weight.shape
    deep = 512
    return pl.pallas_call(
        turn_kernel,
        grid=(features // deep,),
        in_specs=[pl.BlockSpec((parts, deep, inner), lambda i: (0, i, 0))],
        out_specs=pl.BlockSpec((parts * inner, deep), lambda i: (0, i)),
        out_shape=jax.ShapeDtypeStruct((parts * inner, features), weight.dtype),
        compiler_params=pltpu.CompilerParams(vmem_limit_bytes=16 * MIB),
        cost_estimate=pl.CostEstimate(
            flops=0, bytes_accessed=4 * weight.size, transcendentals=0
        ),
        name="turn",
    )(weight)


def prepare_kernel(own, other, modulation, gain, bias, own_out, other_out):
    own_out[...] = own[...].T
    other_out[...] = other[...].T
    for row, out, add in ((1, gain, 1.0), (0, bias, 0.0)):
        for part in range(out.shape[0] // BLK):
            rows = slice(part * BLK, (part + 1) * BLK)
            line = modulation[row : row + 1, rows] + add
            out[rows, :] = jnp.broadcast_to(line, (BLK, BLK)).T


def prepare(own, other, modulation):
    inner, features = own.shape
    deep = 512
    return pl.pallas_call(
        prepare_kernel,
        grid=(features // deep,),
        in_specs=[
            pl.BlockSpec((inner, deep), lambda i: (0, i)),
            pl.BlockSpec((inner, deep), lambda i: (0, i)),
            pl.BlockSpec((3, deep), lambda i: (0, i)),
        ],
        out_specs=[
            pl.BlockSpec((deep, BLK), lambda i: (i, 0)),
            pl.BlockSpec((deep, BLK), lambda i: (i, 0)),
            pl.BlockSpec((deep, inner), lambda i: (i, 0)),
            pl.BlockSpec((deep, inner), lambda i: (i, 0)),
        ],
        out_shape=[
            jax.ShapeDtypeStruct((features, BLK), jnp.float32),
            jax.ShapeDtypeStruct((features, BLK), jnp.float32),
            jax.ShapeDtypeStruct((features, inner), jnp.bfloat16),
            jax.ShapeDtypeStruct((features, inner), jnp.bfloat16),
        ],
        compiler_params=pltpu.CompilerParams(vmem_limit_bytes=16 * MIB),
        cost_estimate=pl.CostEstimate(
            flops=0, bytes_accessed=12 * features * inner, transcendentals=0
        ),
        name="prepare",
    )(own, other, modulation)


def together(arrays, others=()):
    return lax.optimization_barrier((*arrays, *others))[: len(arrays)]


def project_kernel(
    chips, heads, *refs
):
    xs, weights, (gain, bias), rest = refs[:10], refs[10:14], refs[14:16], refs[16:]
    (kv0, q0, *packed), (normed, total) = rest[-7:-2], rest[-2:]
    step = pl.program_id(0)
    features = 8 * DEEP
    count = normed.shape[2]
    lay = [(piece, 0, x) for piece, x in enumerate(xs[:7])]
    lay += [(7, cut[0], x) for cut, x in zip(CUTS, xs[7:])]

    def fold(values):
        return jnp.sum(values.reshape(values.shape[0] // 8, 8, count), axis=0)

    @pl.when(step == 0)
    def _():
        total[...] = jnp.zeros_like(total)
        summed = jnp.zeros((8, count), jnp.float32)
        for _, _, x in lay:
            tile = tile_of(x.shape[0])

            def add(i, state, x=x, tile=tile):
                wide = x[pl.ds(pl.multiple_of(i * tile, 16), tile), :].astype(jnp.float32)
                return state + fold(wide)

            summed = lax.fori_loop(0, x.shape[0] // tile, add, summed)
        center = jnp.sum(summed, axis=0, keepdims=True) / features
        summed = jnp.zeros((8, count), jnp.float32)
        for _, _, x in lay:
            tile = tile_of(x.shape[0])

            def square(i, state, x=x, tile=tile):
                wide = x[pl.ds(pl.multiple_of(i * tile, 16), tile), :].astype(jnp.float32)
                return state + fold(jnp.square(wide - center))

            summed = lax.fori_loop(0, x.shape[0] // tile, square, summed)
        rate = lax.rsqrt(jnp.sum(summed, axis=0, keepdims=True) / features + EPSILON)
        for piece, first, x in lay:
            tile = tile_of(x.shape[0])

            def norm(i, _, x=x, tile=tile, piece=piece, first=first):
                start = pl.multiple_of(i * tile, 16)
                row = pl.multiple_of(chips[piece] * DEEP + first + start, 16)
                part_gain = gain[pl.ds(row, tile), :]
                part_bias = bias[pl.ds(row, tile), :]
                for part in range(count // BLK):
                    columns = slice(part * BLK, (part + 1) * BLK)
                    wide = x[pl.ds(start, tile), columns].astype(jnp.float32)
                    value = (wide - center[:, columns]) * rate[:, columns] * part_gain + part_bias
                    normed[
                        piece // 2,
                        pl.ds(pl.multiple_of(piece % 2 * DEEP + first + start, 16), tile),
                        columns,
                    ] = value.astype(jnp.bfloat16)
                return 0

            lax.fori_loop(0, x.shape[0] // tile, norm, 0)

    held = normed[step]
    outs = total.shape[0] // 2
    for side in range(2):
        weight = jnp.concatenate([w[...] for w in weights[2 * side : 2 * side + 2]], axis=1)
        total[side * outs : (side + 1) * outs] += jnp.dot(
            weight, held, preferred_element_type=jnp.float32
        )

    @pl.when(step == pl.num_programs(0) - 1)
    def _():
        for index in range(4):
            if index:
                kv, q = packed[index - 1], packed[index - 1].at[2 * BLK :]
            else:
                kv, q = kv0, q0
            base = pl.multiple_of(heads[index] * BLK, BLK)
            q[...] = total[pl.ds(base, BLK), :].astype(jnp.bfloat16)
            keys = total[pl.ds(base + 2 * BLK, BLK), :]
            for part in range(count // BLK):
                columns = slice(part * BLK, (part + 1) * BLK)
                kv[:BLK, columns] = keys[:, columns].T.astype(jnp.bfloat16)
            kv[BLK : 2 * BLK, :] = total[pl.ds(base + 4 * BLK, BLK), :].astype(jnp.bfloat16)


def project(chips, heads, xs, own, other, gain, bias, after):
    outs, features = own.shape
    deep, count = xs[0].shape
    whole = lambda shape: pl.BlockSpec(shape, lambda k, *_: (0, 0))
    blocks = [
        pl.BlockSpec((outs, deep), lambda k, chips, heads, i=i: (0, chips[2 * k + i]))
        for i in range(2)
    ]
    shapes = [(2 * BLK, count), (BLK, count)] + [(3 * BLK, count)] * 3
    return pl.pallas_call(
        project_kernel,
        grid_spec=pltpu.PrefetchScalarGridSpec(
            num_scalar_prefetch=2,
            grid=(features // deep // 2,),
            in_specs=[whole(x.shape) for x in xs]
            + [*blocks, *blocks, whole(gain.shape), whole(bias.shape)]
            + [pl.BlockSpec(memory_space=pl.ANY)] * len(after),
            out_specs=[whole(s) for s in shapes],
            scratch_shapes=[
                pltpu.VMEM((features // deep // 2, 2 * deep, count), jnp.bfloat16),
                pltpu.VMEM((2 * outs, count), jnp.float32),
            ],
        ),
        out_shape=[jax.ShapeDtypeStruct(s, jnp.bfloat16) for s in shapes],
        compiler_params=pltpu.CompilerParams(vmem_limit_bytes=50 * MIB),
        cost_estimate=pl.CostEstimate(
            flops=4 * outs * features * count,
            bytes_accessed=2 * features * (count + 2 * outs),
            transcendentals=0,
        ),
        name="project",
    )(chips, heads, *xs, own, own, other, other, gain, bias, *after)


def attend_kernel(factor, unroll, plan, places, counts, first, owner, *refs):
    arrays, outs, rest = refs[: -4 - 8], refs[-4 - 8 : -8], refs[-8:]
    kv, query, asked, scores, tops, totals, sums, arrived = rest
    copies = []
    for kind, index, array, start in plan:
        to = (kv if kind == "kv" else query).at[index]
        rows = to.shape[0]
        copies.append(
            pltpu.make_async_copy(
                arrays[array].at[start : start + rows], to, arrived.at[len(copies)]
            )
        )
    for copy in copies:
        copy.start()
    per_piece = kv.shape[2] // BLK
    rows = len(outs) * per_piece
    tops[...] = jnp.full_like(tops, NEGATIVE)
    totals[...] = jnp.zeros_like(totals)
    sums[...] = jnp.zeros_like(sums)
    for copy in copies:
        copy.wait()
    for index in range(len(outs)):
        for part in range(per_piece):
            asked[index * per_piece + part] = query[index, :, part * BLK : (part + 1) * BLK]

    def find(pair, low, high):
        live = pair < high
        pair = jnp.where(live, pair, low)
        row = owner[pair]
        place = 2 * (pair - first[row])
        wheres = [places[row, place], places[row, place + 1]]
        offsets = [
            jnp.where(live, 0.0, NEGATIVE),
            jnp.where(live & (place + 1 < counts[row]), 0.0, NEGATIVE),
        ]
        return row, wheres, offsets

    def held(where, part):
        start = pl.multiple_of((where & (per_piece - 1)) * BLK, BLK)
        return kv[where >> 2, part * BLK : (part + 1) * BLK, pl.ds(start, BLK)]

    def fold(op, value):
        return op(value.reshape(BLK // 8, 8, BLK), axis=0)

    def rate(low, high, step, _):
        found = []
        for item in range(unroll):
            pair = step * unroll + item
            row, wheres, offsets = find(low + pair, low, high)
            keys = jnp.concatenate([held(where, 0) for where in wheres], axis=0)
            score = jnp.dot(keys, asked[row], preferred_element_type=jnp.float32)
            scores[pair] = score
            best = jnp.maximum(
                fold(jnp.max, score[:BLK]) + offsets[0], fold(jnp.max, score[BLK:]) + offsets[1]
            )
            found.append((row, best))
        for row, best in found:
            tops[row] = jnp.maximum(tops[row], best)
        return 0

    def gather(low, high, step, _):
        found = []
        for item in range(unroll):
            pair = step * unroll + item
            row, wheres, offsets = find(low + pair, low, high)
            top = tops[row][:1]
            score = scores[pair]
            halves = [
                jnp.exp2(score[part * BLK : (part + 1) * BLK] * factor - (top - offsets[part]))
                for part in range(2)
            ]
            total = fold(jnp.sum, halves[0]) + fold(jnp.sum, halves[1])
            weights = jnp.concatenate([half.astype(jnp.bfloat16) for half in halves], axis=0)
            values = jnp.concatenate([held(where, 1) for where in wheres], axis=1)
            summed = jnp.dot(values, weights, preferred_element_type=jnp.float32)
            found.append((row, total, summed))
        for row, total, summed in found:
            totals[row] += total
            sums[row] += summed
        return 0

    for index in range(len(outs)):
        low, high = first[index * per_piece], first[(index + 1) * per_piece]
        steps = (high - low + unroll - 1) // unroll
        lax.fori_loop(0, steps, functools.partial(rate, low, high), 0)
        for row in range(index * per_piece, (index + 1) * per_piece):
            top = jnp.max(tops[row], axis=0, keepdims=True) * factor
            tops[row] = jnp.broadcast_to(top, tops.shape[1:])
        lax.fori_loop(0, steps, functools.partial(gather, low, high), 0)

    for index, out in enumerate(outs):
        for part in range(per_piece):
            row = index * per_piece + part
            total = jnp.sum(totals[row], axis=0, keepdims=True)
            out[:, part * BLK : (part + 1) * BLK] = (sums[row] / total).astype(jnp.bfloat16)


def pair_lists(counts, most):
    twos = (counts + 1) // 2
    rows = counts.shape[0]
    order = jnp.arange(rows + 1, dtype=jnp.int32)
    first = jnp.sum(jnp.where(order[None, :rows] < order[:, None], twos[None, :], 0), axis=1)
    slots = jnp.arange(rows * most // 2, dtype=jnp.int32)
    return first, jnp.sum(jnp.where(first[None, 1:] <= slots[:, None], 1, 0), axis=1)


def attend(factor, lists, plan, arrays, count):
    rows, most = lists[0].shape
    pieces = most * BLK // count
    asking = rows * BLK // count

    def kernel(*refs):
        attend_kernel(factor, PAIRS, plan, *refs)

    shape = (BLK, count)
    return pl.pallas_call(
        kernel,
        in_specs=[pl.BlockSpec(memory_space=pltpu.SMEM)] * len(lists)
        + [pl.BlockSpec(memory_space=pl.ANY)] * len(arrays),
        out_specs=[pl.BlockSpec(memory_space=pltpu.VMEM)] * asking,
        out_shape=[jax.ShapeDtypeStruct(shape, jnp.bfloat16)] * asking,
        scratch_shapes=[
            pltpu.VMEM((pieces, 2 * BLK, count), jnp.bfloat16),
            pltpu.VMEM((asking, *shape), jnp.bfloat16),
            pltpu.VMEM((rows, BLK, BLK), jnp.bfloat16),
            pltpu.VMEM((rows * most // 2 // asking + PAIRS, 2 * BLK, BLK), jnp.float32),
            pltpu.VMEM((rows, 8, BLK), jnp.float32),
            pltpu.VMEM((rows, 8, BLK), jnp.float32),
            pltpu.VMEM((rows, BLK, BLK), jnp.float32),
            pltpu.SemaphoreType.DMA((len(plan),)),
        ],
        compiler_params=pltpu.CompilerParams(vmem_limit_bytes=32 * MIB),
        cost_estimate=pl.CostEstimate(
            flops=rows * BLK * most * BLK * BLK,
            bytes_accessed=4 * most * BLK * BLK,
            transcendentals=rows * BLK * most * BLK // 4,
        ),
        name="attend",
    )(*lists, *arrays)


def leave_kernel(plan, chips, columns, *refs):
    weights, heads, rest, ordered = refs[:2], refs[2:6], refs[6:-1], refs[-1]
    step = pl.program_id(0)

    @pl.when(step == 0)
    def _():
        for index, head in enumerate(heads):
            ordered[pl.ds(pl.multiple_of(columns[index] * BLK, BLK), BLK), :] = head[...]

    summed = jnp.dot(
        jnp.concatenate([weight[...] for weight in weights], axis=1),
        ordered[...],
        preferred_element_type=jnp.float32,
    )
    outs = list(rest)
    for index, cuts in enumerate(plan):
        mine = [outs.pop(0) for _ in cuts]

        @pl.when(step == index)
        def _():
            for cut, out in zip(cuts, mine):
                out[...] = summed[cut[0] : cut[1]].astype(out.dtype)


def leave(chips, columns, weights, heads, plan):
    high = CUTS[-1][1]
    count = heads[0].shape[1]
    steps = len(plan)
    inner = weights[0].shape[1]
    block = pl.BlockSpec((high, inner), lambda i, chips, columns: (chips[i], 0))
    whole = lambda shape: pl.BlockSpec(shape, lambda i, *_: (0, 0))
    shapes = [(cut[1] - cut[0], count) for cuts in plan for cut in cuts]

    def kernel(*refs):
        leave_kernel(plan, *refs)

    return pl.pallas_call(
        kernel,
        grid_spec=pltpu.PrefetchScalarGridSpec(
            num_scalar_prefetch=2,
            grid=(steps,),
            in_specs=[block] * 2
            + [whole(h.shape) for h in heads],
            out_specs=[whole(s) for s in shapes],
            scratch_shapes=[pltpu.VMEM((2 * inner, count), jnp.bfloat16)],
        ),
        out_shape=[jax.ShapeDtypeStruct(s, jnp.bfloat16) for s in shapes],
        compiler_params=pltpu.CompilerParams(vmem_limit_bytes=32 * MIB),
        cost_estimate=pl.CostEstimate(
            flops=4 * steps * high * inner * count,
            bytes_accessed=2 * steps * high * (2 * inner + count),
            transcendentals=0,
        ),
        name="leave",
    )(chips, columns, *weights, *heads)


def arrive_kernel(plan, *refs):
    outs = refs[-len(plan) :]
    at = 0
    for cuts, out in zip(plan, outs):
        share, arrived = refs[at], refs[at + 1 : at + 1 + len(cuts)]
        at += 1 + len(cuts)
        rows = sorted({0, out.shape[0], *[edge for cut in cuts for edge in cut]})
        for low, high in zip(rows, rows[1:]):
            value = share[low:high].astype(jnp.float32)
            for (first, last), ref in zip(cuts, arrived):
                if first <= low and high <= last:
                    value += ref[low - first : high - first].astype(jnp.float32)
            out[low:high] = value.astype(out.dtype)


def arrive(plan, *arrays):
    shares, at = [], 0
    for cuts in plan:
        shares.append(arrays[at])
        at += 1 + len(cuts)

    def kernel(*refs):
        arrive_kernel(plan, *refs)

    return pl.pallas_call(
        kernel,
        in_specs=[pl.BlockSpec(memory_space=pltpu.VMEM)] * len(arrays),
        out_specs=[pl.BlockSpec(memory_space=pltpu.VMEM)] * len(plan),
        out_shape=[jax.ShapeDtypeStruct(share.shape, share.dtype) for share in shares],
        compiler_params=pltpu.CompilerParams(vmem_limit_bytes=24 * MIB),
        cost_estimate=pl.CostEstimate(
            flops=0, bytes_accessed=8 * shares[0].size, transcendentals=0
        ),
        name="arrive",
    )(*arrays)


def gather_tokens(own, first_others, second_others):
    below = shift(own, "z", 1)
    above = shift(own, "z", -1)
    beside = swap(own, "yl")
    below, above, beside = together((below, above, beside), first_others)
    far = shift(below, "z", 1)
    beside_below = swap(below, "yl")
    beside_above = shift(beside, "z", -1)
    far, beside_below, beside_above = together((far, beside_below, beside_above), second_others)
    first, second, third = [slice(*cut) for cut in CUTS]
    parts = [
        swap(far[first], "yl"),
        shift(beside_above[second], "z", -1),
        shift(beside_below[third], "z", 1),
    ]
    places = [(0, 0), (0, -1), (0, 1), (1, 0), (0, 2), (1, -1), (1, 1), (1, 2)]
    return places, [own, below, above, beside, far, beside_below, beside_above, *parts]


def shards(tokens, qkv_weight, out_weight, modulation, block_mask):
    rows, local = tokens.shape
    features = modulation.shape[1]
    heads_here = block_mask.shape[0]
    inner = qkv_weight.shape[2]
    head_size = inner // heads_here
    factor = math.log2(math.e) / math.sqrt(head_size)
    half = rows // 2
    core = lax.axis_index("core")
    frame_x, frame_y = lax.axis_index("x"), lax.axis_index("yh")
    chip_y, chip_z = lax.axis_index("yl"), lax.axis_index("z")
    across = tokens.T

    def chip(dy, dz):
        return ((chip_y + dy) % 2) * 4 + (chip_z + dz) % 4

    def mine_and_given(value, axis):
        size = value.shape[axis] // 2
        mine = lax.dynamic_slice_in_dim(value, core * size, size, axis)
        return mine, lax.dynamic_slice_in_dim(value, (1 - core) * size, size, axis)

    def head_slot(steps):
        head = (frame_x + steps) % 4
        return jnp.where(head // 2 == core, 0, 1), head % 2

    mine, given = mine_and_given(across, 1)
    other = swap(given, "core")
    own = jnp.concatenate(
        [jnp.where(core == 0, mine, other), jnp.where(core == 0, other, mine)], axis=0
    )
    mask_mine, mask_given = mine_and_given(block_mask, 1)
    mask_other = swap(mask_given, "core")
    mask_heads = jnp.stack([mask_mine, mask_other])
    mask_rows = []
    for steps in range(4):
        side, slot = head_slot(steps)
        part = lax.dynamic_slice(
            mask_heads, (side, slot, 0, 0), (1, 1, *mask_heads.shape[2:])
        )[0, 0]
        mask_rows.append(shift(part, "x", steps) if steps else part)
    raw, _ = lax.optimization_barrier((qkv_weight, own))
    other_raw = swap(raw, "core")
    own_weight, other_weight = turn(raw), turn(other_raw)
    places, xs = gather_tokens(own, (own_weight, *mask_rows[1:]), (other_weight,))
    out_raw, _ = lax.optimization_barrier((out_weight, xs[1]))
    gain, bias, *leaving = prepare(out_weight, swap(out_raw, "core"), modulation)

    keep = jnp.concatenate(mask_rows, axis=0) != 0
    blocks = jnp.arange(keep.shape[1], dtype=jnp.int32)
    per_core = half // BLK
    piece, inside = blocks // per_core, blocks % per_core
    from_core, from_y, from_x = core ^ (piece // 8), frame_y ^ (piece // 4 % 2), (frame_x - piece % 4) % 4
    origin = (from_y * 4 + from_x) * (2 * per_core) + from_core * per_core + inside
    same = origin[:, None] == blocks[None, :]
    keep = jnp.sum(jnp.where(same[None] & keep[:, None, :], 1, 0), axis=2)
    counts = jnp.sum(keep, axis=1)
    earlier = blocks[None, :] < blocks[:, None]
    rank = jnp.sum(jnp.where(earlier[None], keep[:, None, :], 0), axis=2)
    chosen = (keep[:, None, :] != 0) & (rank[:, None, :] == blocks[None, :, None])
    listed = jnp.sum(jnp.where(chosen, blocks[None, None, :], 0), axis=2)

    chips = jnp.stack([chip(*place) for place in places]).astype(jnp.int32)
    slots = [head_slot(steps) for steps in range(4)]
    bases = jnp.stack([side * 3 * heads_here + slot for side, slot in slots]).astype(jnp.int32)
    lists = (listed, counts, *pair_lists(counts, listed.shape[1]))
    kv, query, *packed = project(
        chips, bases, xs, own_weight, other_weight, gain, bias, (*lists, *leaving)
    )
    two, one, three = [shift(packed[i - 1], "x", i) for i in (2, 1, 3)]
    both = jnp.concatenate([one[: 2 * BLK], three[: 2 * BLK]], axis=0)
    last = two[: 2 * BLK]
    away = [swap(part, "yh") for part in (kv, both, last)]
    near = jnp.concatenate([kv, both, last], axis=0)
    arrays = [kv, query, one, two, three, *away, swap(near, "core"), *[swap(a, "core") for a in away]]
    step = 2 * BLK
    plan = [("kv", 0, 0, 0), ("q", 0, 1, 0)]
    for steps, array in ((1, 2), (2, 3), (3, 4)):
        plan += [("kv", steps, array, 0), ("q", steps, array, step)]
    for index, array in ((4, 5), (12, 9)):
        plan += [("kv", index, array, 0), ("kv", index + 1, array + 1, 0)]
        plan += [("kv", index + 3, array + 1, step), ("kv", index + 2, array + 2, 0)]
    plan += [("kv", 8 + steps, 8, at * step) for at, steps in enumerate((0, 1, 3, 2))]
    heads = attend(factor, lists, plan, arrays, half)
    heads = [heads[0]] + [shift(heads[steps], "x", -steps) for steps in (1, 2, 3)]

    columns = jnp.stack([side * heads_here + slot for side, slot in slots]).astype(jnp.int32)
    whole = CUTS[0][0], CUTS[-1][1]

    def shares(targets, cuts):
        chips = jnp.stack([chip(*target) for target in targets]).astype(jnp.int32)
        return leave(chips, columns, leaving, heads, [cuts] * len(targets))

    parts = shares([(1, 2)], CUTS)
    near = [(0, 2), (1, 1), (1, -1), (0, -1), (0, 1), (1, 0), (0, 0)]
    share = dict(zip(near, shares(near, (whole,))))
    first = swap(parts[0], "yl")
    second = shift(parts[1], "z", 1)
    third = shift(parts[2], "z", -1)
    down, up, side = arrive(
        [(CUTS[0],), (CUTS[1],), (CUTS[2],)],
        *[share[0, 2], first, share[1, 1], second, share[1, -1], third],
    )
    down, up, side = shift(down, "z", -1), shift(up, "z", 1), swap(side, "yl")
    down, side = arrive(
        [(whole, whole), (whole,)], share[0, -1], down, side, share[1, 0], up
    )
    down, up, side = shift(down, "z", -1), shift(share[0, 1], "z", 1), swap(side, "yl")
    (summed,) = arrive([(whole, whole, whole)], share[0, 0], down, up, side)

    kept, given = mine_and_given(summed, 0)
    other = swap(given, "core")
    projected = jnp.concatenate(
        [jnp.where(core == 0, kept, other), jnp.where(core == 0, other, kept)], axis=1
    ).astype(jnp.float32)
    start = lax.axis_index(HEAD) * local
    gate = lax.dynamic_slice_in_dim(modulation, start, local, 1)[2][:, None]
    return (across.astype(jnp.float32) + gate * projected).astype(jnp.bfloat16).T


def solution(mesh):
    fine = Mesh(mesh.devices.reshape(2, 4, 2, 4, 2), ("yh", "x", "yl", "z", "core"))
    placed = (
        P(FRAME, HEAD),
        P(None, None, HEAD),
        P(HEAD, None),
        P(),
        P(HEAD, FRAME, None),
    )
    return jax.shard_map(
        shards, mesh=fine, in_specs=placed, out_specs=P(FRAME, HEAD), check_vma=False
    )
```

```python
import functools
import math

import jax
import jax.numpy as jnp
from jax import lax
from jax.experimental import pallas as pl
from jax.experimental.pallas import tpu as pltpu
from jax.sharding import Mesh
from jax.sharding import PartitionSpec as P

BLK = 128
EPSILON = 1e-06
NEGATIVE = -1e30
FRAME = ("yh", "x")
HEAD = ("yl", "z", "core")
MIB = 1 << 20
PAIRS = 8
CUTS = ((0, 224), (224, 432), (432, 640))


DEEP = CUTS[-1][1]


def shift(value, axis, steps):
    count = lax.axis_size(axis)
    return lax.ppermute(value, axis, [(i, (i + steps) % count) for i in range(count)])


def swap(value, axis):
    return shift(value, axis, 1)


def tile_of(rows):
    return {640: 128, 224: 112}.get(rows, rows)


def turn_kernel(weight, out):
    inner = weight.shape[2]
    for part in range(weight.shape[0]):
        out[part * inner : (part + 1) * inner, :] = weight[part].T


def turn(weight):
    parts, features, inner = weight.shape
    deep = 512
    return pl.pallas_call(
        turn_kernel,
        grid=(features // deep,),
        in_specs=[pl.BlockSpec((parts, deep, inner), lambda i: (0, i, 0))],
        out_specs=pl.BlockSpec((parts * inner, deep), lambda i: (0, i)),
        out_shape=jax.ShapeDtypeStruct((parts * inner, features), weight.dtype),
        compiler_params=pltpu.CompilerParams(vmem_limit_bytes=56 * MIB),
        cost_estimate=pl.CostEstimate(
            flops=0, bytes_accessed=4 * weight.size, transcendentals=0
        ),
        name="turn",
    )(weight)


def stand_kernel(*refs):
    half = len(refs) // 2
    for weight, out in zip(refs[:half], refs[half:]):
        out[...] = weight[...].T


def stand(*weights):
    inner, features = weights[0].shape
    deep = 1024
    return pl.pallas_call(
        stand_kernel,
        grid=(features // deep,),
        in_specs=[pl.BlockSpec((inner, deep), lambda i: (0, i))] * len(weights),
        out_specs=[pl.BlockSpec((deep, inner), lambda i: (i, 0))] * len(weights),
        out_shape=[jax.ShapeDtypeStruct((features, inner), w.dtype) for w in weights],
        compiler_params=pltpu.CompilerParams(vmem_limit_bytes=56 * MIB),
        cost_estimate=pl.CostEstimate(
            flops=0, bytes_accessed=4 * features * inner * len(weights), transcendentals=0
        ),
        name="stand",
    )(*weights)


def spread_kernel(modulation, gain, bias):
    for row, out, add in ((1, gain, 1.0), (0, bias, 0.0)):
        for part in range(out.shape[0] // BLK):
            rows = slice(part * BLK, (part + 1) * BLK)
            line = modulation[row : row + 1, rows] + add
            out[rows, :] = jnp.broadcast_to(line, (BLK, BLK)).T


def spread(modulation):
    features = modulation.shape[1]
    deep = 1024
    return pl.pallas_call(
        spread_kernel,
        grid=(features // deep,),
        in_specs=[pl.BlockSpec((3, deep), lambda i: (0, i))],
        out_specs=[pl.BlockSpec((deep, BLK), lambda i: (i, 0))] * 2,
        out_shape=[jax.ShapeDtypeStruct((features, BLK), jnp.float32)] * 2,
        compiler_params=pltpu.CompilerParams(vmem_limit_bytes=56 * MIB),
        cost_estimate=pl.CostEstimate(
            flops=0, bytes_accessed=8 * features * BLK, transcendentals=0
        ),
        name="spread",
    )(modulation)


def together(arrays, others=()):
    return lax.optimization_barrier((*arrays, *others))[: len(arrays)]


def project_kernel(
    chips, heads, *refs
):
    xs, weights, (gain, bias), rest = refs[:10], refs[10:14], refs[14:16], refs[16:]
    (kv0, q0, *packed), (normed, total) = rest[-7:-2], rest[-2:]
    step = pl.program_id(0)
    features = 8 * DEEP
    count = normed.shape[2]
    lay = [(piece, 0, x) for piece, x in enumerate(xs[:7])]
    lay += [(7, cut[0], x) for cut, x in zip(CUTS, xs[7:])]

    def fold(values):
        return jnp.sum(values.reshape(values.shape[0] // 8, 8, count), axis=0)

    @pl.when(step == 0)
    def _():
        total[...] = jnp.zeros_like(total)
        summed = jnp.zeros((8, count), jnp.float32)
        for _, _, x in lay:
            tile = tile_of(x.shape[0])

            def add(i, state, x=x, tile=tile):
                wide = x[pl.ds(pl.multiple_of(i * tile, 16), tile), :].astype(jnp.float32)
                return state + fold(wide)

            summed = lax.fori_loop(0, x.shape[0] // tile, add, summed)
        center = jnp.sum(summed, axis=0, keepdims=True) / features
        summed = jnp.zeros((8, count), jnp.float32)
        for _, _, x in lay:
            tile = tile_of(x.shape[0])

            def square(i, state, x=x, tile=tile):
                wide = x[pl.ds(pl.multiple_of(i * tile, 16), tile), :].astype(jnp.float32)
                return state + fold(jnp.square(wide - center))

            summed = lax.fori_loop(0, x.shape[0] // tile, square, summed)
        rate = lax.rsqrt(jnp.sum(summed, axis=0, keepdims=True) / features + EPSILON)
        for piece, first, x in lay:
            tile = tile_of(x.shape[0])

            def norm(i, _, x=x, tile=tile, piece=piece, first=first):
                start = pl.multiple_of(i * tile, 16)
                row = pl.multiple_of(chips[piece] * DEEP + first + start, 16)
                part_gain = gain[pl.ds(row, tile), :]
                part_bias = bias[pl.ds(row, tile), :]
                for part in range(count // BLK):
                    columns = slice(part * BLK, (part + 1) * BLK)
                    wide = x[pl.ds(start, tile), columns].astype(jnp.float32)
                    value = (wide - center[:, columns]) * rate[:, columns] * part_gain + part_bias
                    normed[
                        piece // 2,
                        pl.ds(pl.multiple_of(piece % 2 * DEEP + first + start, 16), tile),
                        columns,
                    ] = value.astype(jnp.bfloat16)
                return 0

            lax.fori_loop(0, x.shape[0] // tile, norm, 0)

    held = normed[step]
    outs = total.shape[0] // 2
    for side in range(2):
        weight = jnp.concatenate([w[...] for w in weights[2 * side : 2 * side + 2]], axis=1)
        total[side * outs : (side + 1) * outs] += jnp.dot(
            weight, held, preferred_element_type=jnp.float32
        )

    @pl.when(step == pl.num_programs(0) - 1)
    def _():
        for index in range(4):
            if index:
                kv, q = packed[index - 1], packed[index - 1].at[2 * BLK :]
            else:
                kv, q = kv0, q0
            base = pl.multiple_of(heads[index] * BLK, BLK)
            q[...] = total[pl.ds(base, BLK), :].astype(jnp.bfloat16)
            keys = total[pl.ds(base + 2 * BLK, BLK), :]
            for part in range(count // BLK):
                columns = slice(part * BLK, (part + 1) * BLK)
                kv[:BLK, columns] = keys[:, columns].T.astype(jnp.bfloat16)
            kv[BLK : 2 * BLK, :] = total[pl.ds(base + 4 * BLK, BLK), :].astype(jnp.bfloat16)


def project(chips, heads, xs, own, other, gain, bias):
    outs, features = own.shape
    deep, count = xs[0].shape
    whole = lambda shape: pl.BlockSpec(shape, lambda k, *_: (0, 0))
    blocks = [
        pl.BlockSpec((outs, deep), lambda k, chips, heads, i=i: (0, chips[2 * k + i]))
        for i in range(2)
    ]
    shapes = [(2 * BLK, count), (BLK, count)] + [(3 * BLK, count)] * 3
    return pl.pallas_call(
        project_kernel,
        grid_spec=pltpu.PrefetchScalarGridSpec(
            num_scalar_prefetch=2,
            grid=(features // deep // 2,),
            in_specs=[whole(x.shape) for x in xs]
            + [*blocks, *blocks, whole(gain.shape), whole(bias.shape)],
            out_specs=[whole(s) for s in shapes],
            scratch_shapes=[
                pltpu.VMEM((features // deep // 2, 2 * deep, count), jnp.bfloat16),
                pltpu.VMEM((2 * outs, count), jnp.float32),
            ],
        ),
        out_shape=[jax.ShapeDtypeStruct(s, jnp.bfloat16) for s in shapes],
        compiler_params=pltpu.CompilerParams(vmem_limit_bytes=56 * MIB),
        cost_estimate=pl.CostEstimate(
            flops=4 * outs * features * count,
            bytes_accessed=2 * features * (count + 2 * outs),
            transcendentals=0,
        ),
        name="project",
    )(chips, heads, *xs, own, own, other, other, gain, bias)


def attend_kernel(factor, unroll, plan, places, counts, first, owner, *refs):
    arrays, outs, rest = refs[: -4 - 8], refs[-4 - 8 : -8], refs[-8:]
    kv, query, asked, scores, tops, totals, sums, arrived = rest
    copies = []
    for kind, index, array, start in plan:
        to = (kv if kind == "kv" else query).at[index]
        rows = to.shape[0]
        copies.append(
            pltpu.make_async_copy(
                arrays[array].at[start : start + rows], to, arrived.at[len(copies)]
            )
        )
    for copy in copies:
        copy.start()
    per_piece = kv.shape[2] // BLK
    rows = len(outs) * per_piece
    tops[...] = jnp.full_like(tops, NEGATIVE)
    totals[...] = jnp.zeros_like(totals)
    sums[...] = jnp.zeros_like(sums)
    for copy in copies:
        copy.wait()
    for index in range(len(outs)):
        for part in range(per_piece):
            asked[index * per_piece + part] = query[index, :, part * BLK : (part + 1) * BLK]

    def find(pair, low, high):
        live = pair < high
        pair = jnp.where(live, pair, low)
        row = owner[pair]
        place = 2 * (pair - first[row])
        wheres = [places[row, place], places[row, place + 1]]
        offsets = [
            jnp.where(live, 0.0, NEGATIVE),
            jnp.where(live & (place + 1 < counts[row]), 0.0, NEGATIVE),
        ]
        return row, wheres, offsets

    def held(where, part):
        start = pl.multiple_of((where & (per_piece - 1)) * BLK, BLK)
        return kv[where >> 2, part * BLK : (part + 1) * BLK, pl.ds(start, BLK)]

    def fold(op, value):
        return op(value.reshape(BLK // 8, 8, BLK), axis=0)

    def rate(low, high, step, _):
        found = []
        for item in range(unroll):
            pair = step * unroll + item
            row, wheres, offsets = find(low + pair, low, high)
            keys = jnp.concatenate([held(where, 0) for where in wheres], axis=0)
            score = jnp.dot(keys, asked[row], preferred_element_type=jnp.float32)
            scores[pair] = score
            best = jnp.maximum(
                fold(jnp.max, score[:BLK]) + offsets[0], fold(jnp.max, score[BLK:]) + offsets[1]
            )
            found.append((row, best))
        for row, best in found:
            tops[row] = jnp.maximum(tops[row], best)
        return 0

    def gather(low, high, step, _):
        found = []
        for item in range(unroll):
            pair = step * unroll + item
            row, wheres, offsets = find(low + pair, low, high)
            top = tops[row][:1]
            score = scores[pair]
            halves = [
                jnp.exp2(score[part * BLK : (part + 1) * BLK] * factor - (top - offsets[part]))
                for part in range(2)
            ]
            total = fold(jnp.sum, halves[0]) + fold(jnp.sum, halves[1])
            weights = jnp.concatenate([half.astype(jnp.bfloat16) for half in halves], axis=0)
            values = jnp.concatenate([held(where, 1) for where in wheres], axis=1)
            summed = jnp.dot(values, weights, preferred_element_type=jnp.float32)
            found.append((row, total, summed))
        for row, total, summed in found:
            totals[row] += total
            sums[row] += summed
        return 0

    for index in range(len(outs)):
        low, high = first[index * per_piece], first[(index + 1) * per_piece]
        steps = (high - low + unroll - 1) // unroll
        lax.fori_loop(0, steps, functools.partial(rate, low, high), 0)
        for row in range(index * per_piece, (index + 1) * per_piece):
            top = jnp.max(tops[row], axis=0, keepdims=True) * factor
            tops[row] = jnp.broadcast_to(top, tops.shape[1:])
        lax.fori_loop(0, steps, functools.partial(gather, low, high), 0)

    for index, out in enumerate(outs):
        for part in range(per_piece):
            row = index * per_piece + part
            total = jnp.sum(totals[row], axis=0, keepdims=True)
            out[:, part * BLK : (part + 1) * BLK] = (sums[row] / total).astype(jnp.bfloat16)


def pair_lists(counts, most):
    twos = (counts + 1) // 2
    rows = counts.shape[0]
    order = jnp.arange(rows + 1, dtype=jnp.int32)
    first = jnp.sum(jnp.where(order[None, :rows] < order[:, None], twos[None, :], 0), axis=1)
    slots = jnp.arange(rows * most // 2, dtype=jnp.int32)
    return first, jnp.sum(jnp.where(first[None, 1:] <= slots[:, None], 1, 0), axis=1)


def attend(factor, lists, plan, arrays, count):
    rows, most = lists[0].shape
    pieces = most * BLK // count
    asking = rows * BLK // count

    def kernel(*refs):
        attend_kernel(factor, PAIRS, plan, *refs)

    shape = (BLK, count)
    return pl.pallas_call(
        kernel,
        in_specs=[pl.BlockSpec(memory_space=pltpu.SMEM)] * len(lists)
        + [pl.BlockSpec(memory_space=pl.ANY)] * len(arrays),
        out_specs=[pl.BlockSpec(memory_space=pltpu.VMEM)] * asking,
        out_shape=[jax.ShapeDtypeStruct(shape, jnp.bfloat16)] * asking,
        scratch_shapes=[
            pltpu.VMEM((pieces, 2 * BLK, count), jnp.bfloat16),
            pltpu.VMEM((asking, *shape), jnp.bfloat16),
            pltpu.VMEM((rows, BLK, BLK), jnp.bfloat16),
            pltpu.VMEM((rows * most // 2 // asking + PAIRS, 2 * BLK, BLK), jnp.float32),
            pltpu.VMEM((rows, 8, BLK), jnp.float32),
            pltpu.VMEM((rows, 8, BLK), jnp.float32),
            pltpu.VMEM((rows, BLK, BLK), jnp.float32),
            pltpu.SemaphoreType.DMA((len(plan),)),
        ],
        compiler_params=pltpu.CompilerParams(vmem_limit_bytes=56 * MIB),
        cost_estimate=pl.CostEstimate(
            flops=rows * BLK * most * BLK * BLK,
            bytes_accessed=4 * most * BLK * BLK,
            transcendentals=rows * BLK * most * BLK // 4,
        ),
        name="attend",
    )(*lists, *arrays)


def leave_kernel(plan, chips, columns, *refs):
    weights, heads, rest, ordered = refs[:2], refs[2:6], refs[6:-1], refs[-1]
    step = pl.program_id(0)

    @pl.when(step == 0)
    def _():
        for index, head in enumerate(heads):
            ordered[pl.ds(pl.multiple_of(columns[index] * BLK, BLK), BLK), :] = head[...]

    summed = jnp.dot(
        jnp.concatenate([weight[...] for weight in weights], axis=1),
        ordered[...],
        preferred_element_type=jnp.float32,
    )
    outs = list(rest)
    for index, cuts in enumerate(plan):
        mine = [outs.pop(0) for _ in cuts]

        @pl.when(step == index)
        def _():
            for cut, out in zip(cuts, mine):
                out[...] = summed[cut[0] : cut[1]].astype(out.dtype)


def leave(chips, columns, weights, heads, plan):
    high = CUTS[-1][1]
    count = heads[0].shape[1]
    steps = len(plan)
    inner = weights[0].shape[1]
    block = pl.BlockSpec((high, inner), lambda i, chips, columns: (chips[i], 0))
    whole = lambda shape: pl.BlockSpec(shape, lambda i, *_: (0, 0))
    shapes = [(cut[1] - cut[0], count) for cuts in plan for cut in cuts]

    def kernel(*refs):
        leave_kernel(plan, *refs)

    return pl.pallas_call(
        kernel,
        grid_spec=pltpu.PrefetchScalarGridSpec(
            num_scalar_prefetch=2,
            grid=(steps,),
            in_specs=[block] * 2
            + [whole(h.shape) for h in heads],
            out_specs=[whole(s) for s in shapes],
            scratch_shapes=[pltpu.VMEM((2 * inner, count), jnp.bfloat16)],
        ),
        out_shape=[jax.ShapeDtypeStruct(s, jnp.bfloat16) for s in shapes],
        compiler_params=pltpu.CompilerParams(vmem_limit_bytes=56 * MIB),
        cost_estimate=pl.CostEstimate(
            flops=4 * steps * high * inner * count,
            bytes_accessed=2 * steps * high * (2 * inner + count),
            transcendentals=0,
        ),
        name="leave",
    )(chips, columns, *weights, *heads)


def arrive_kernel(plan, *refs):
    outs = refs[-len(plan) :]
    at = 0
    for cuts, out in zip(plan, outs):
        share, arrived = refs[at], refs[at + 1 : at + 1 + len(cuts)]
        at += 1 + len(cuts)
        rows = sorted({0, out.shape[0], *[edge for cut in cuts for edge in cut]})
        for low, high in zip(rows, rows[1:]):
            value = share[low:high].astype(jnp.float32)
            for (first, last), ref in zip(cuts, arrived):
                if first <= low and high <= last:
                    value += ref[low - first : high - first].astype(jnp.float32)
            out[low:high] = value.astype(out.dtype)


def arrive(plan, *arrays):
    shares, at = [], 0
    for cuts in plan:
        shares.append(arrays[at])
        at += 1 + len(cuts)

    def kernel(*refs):
        arrive_kernel(plan, *refs)

    return pl.pallas_call(
        kernel,
        in_specs=[pl.BlockSpec(memory_space=pltpu.VMEM)] * len(arrays),
        out_specs=[pl.BlockSpec(memory_space=pltpu.VMEM)] * len(plan),
        out_shape=[jax.ShapeDtypeStruct(share.shape, share.dtype) for share in shares],
        compiler_params=pltpu.CompilerParams(vmem_limit_bytes=56 * MIB),
        cost_estimate=pl.CostEstimate(
            flops=0, bytes_accessed=8 * shares[0].size, transcendentals=0
        ),
        name="arrive",
    )(*arrays)


def gather_tokens(own, first_others, second_others):
    below = shift(own, "z", 1)
    above = shift(own, "z", -1)
    beside = swap(own, "yl")
    below, above, beside = together((below, above, beside), first_others)
    far = shift(below, "z", 1)
    beside_below = swap(below, "yl")
    beside_above = shift(beside, "z", -1)
    far, beside_below, beside_above = together((far, beside_below, beside_above), second_others)
    first, second, third = [slice(*cut) for cut in CUTS]
    parts = [
        swap(far[first], "yl"),
        shift(beside_above[second], "z", -1),
        shift(beside_below[third], "z", 1),
    ]
    places = [(0, 0), (0, -1), (0, 1), (1, 0), (0, 2), (1, -1), (1, 1), (1, 2)]
    return places, [own, below, above, beside, far, beside_below, beside_above, *parts]


def shards(tokens, qkv_weight, out_weight, modulation, block_mask):
    rows, local = tokens.shape
    features = modulation.shape[1]
    heads_here = block_mask.shape[0]
    inner = qkv_weight.shape[2]
    head_size = inner // heads_here
    factor = math.log2(math.e) / math.sqrt(head_size)
    half = rows // 2
    core = lax.axis_index("core")
    frame_x, frame_y = lax.axis_index("x"), lax.axis_index("yh")
    chip_y, chip_z = lax.axis_index("yl"), lax.axis_index("z")
    across = tokens.T

    def chip(dy, dz):
        return ((chip_y + dy) % 2) * 4 + (chip_z + dz) % 4

    def mine_and_given(value, axis):
        size = value.shape[axis] // 2
        mine = lax.dynamic_slice_in_dim(value, core * size, size, axis)
        return mine, lax.dynamic_slice_in_dim(value, (1 - core) * size, size, axis)

    def head_slot(steps):
        head = (frame_x + steps) % 4
        return jnp.where(head // 2 == core, 0, 1), head % 2

    mine, given = mine_and_given(across, 1)
    other = swap(given, "core")
    own = jnp.concatenate(
        [jnp.where(core == 0, mine, other), jnp.where(core == 0, other, mine)], axis=0
    )
    mask_mine, mask_given = mine_and_given(block_mask, 1)
    mask_other = swap(mask_given, "core")

    raw, *_ = lax.optimization_barrier((qkv_weight, own, mask_other))
    own_weight, other_weight = turn(raw), turn(swap(raw, "core"))
    gain, bias = spread(modulation)
    places, xs = gather_tokens(own, (own_weight, gain, bias), (other_weight,))

    chips = jnp.stack([chip(*place) for place in places]).astype(jnp.int32)
    slots = [head_slot(steps) for steps in range(4)]
    bases = jnp.stack([side * 3 * heads_here + slot for side, slot in slots]).astype(jnp.int32)
    kv, query, *packed = project(chips, bases, xs, own_weight, other_weight, gain, bias)
    two, one, three = [shift(packed[i - 1], "x", i) for i in (2, 1, 3)]
    away_kv = swap(kv, "yh")
    out_own, _ = lax.optimization_barrier((out_weight, kv))
    leaving = stand(out_weight, swap(out_own, "core"))
    one, three = together((one, three), (away_kv, *leaving))
    both = jnp.concatenate([one[: 2 * BLK], three[: 2 * BLK]], axis=0)
    away_both = swap(both, "yh")
    (two,) = together((two,), (away_both,))
    last = two[: 2 * BLK]
    away = [away_kv, away_both, swap(last, "yh")]
    near = jnp.concatenate([kv, both, last], axis=0)
    arrays = [kv, query, one, two, three, *away, swap(near, "core"), *[swap(a, "core") for a in away]]

    mask_mine, mask_other, _ = lax.optimization_barrier((mask_mine, mask_other, one))
    mask_heads = jnp.stack([mask_mine, mask_other])
    mask_rows = []
    for steps in range(4):
        side, slot = head_slot(steps)
        part = lax.dynamic_slice(
            mask_heads, (side, slot, 0, 0), (1, 1, *mask_heads.shape[2:])
        )[0, 0]
        mask_rows.append(shift(part, "x", steps) if steps else part)
    keep = jnp.concatenate(mask_rows, axis=0) != 0
    blocks = jnp.arange(keep.shape[1], dtype=jnp.int32)
    per_core = half // BLK
    piece, inside = blocks // per_core, blocks % per_core
    from_core, from_y = core ^ (piece // 8), frame_y ^ (piece // 4 % 2)
    from_x = (frame_x - piece % 4) % 4
    origin = (from_y * 4 + from_x) * (2 * per_core) + from_core * per_core + inside
    same = origin[:, None] == blocks[None, :]
    keep = jnp.sum(jnp.where(same[None] & keep[:, None, :], 1, 0), axis=2)
    counts = jnp.sum(keep, axis=1)
    earlier = blocks[None, :] < blocks[:, None]
    rank = jnp.sum(jnp.where(earlier[None], keep[:, None, :], 0), axis=2)
    chosen = (keep[:, None, :] != 0) & (rank[:, None, :] == blocks[None, :, None])
    listed = jnp.sum(jnp.where(chosen, blocks[None, None, :], 0), axis=2)
    lists = (listed, counts, *pair_lists(counts, listed.shape[1]))

    step = 2 * BLK
    plan = [("kv", 0, 0, 0), ("q", 0, 1, 0)]
    for steps, array in ((1, 2), (2, 3), (3, 4)):
        plan += [("kv", steps, array, 0), ("q", steps, array, step)]
    for index, array in ((4, 5), (12, 9)):
        plan += [("kv", index, array, 0), ("kv", index + 1, array + 1, 0)]
        plan += [("kv", index + 3, array + 1, step), ("kv", index + 2, array + 2, 0)]
    plan += [("kv", 8 + steps, 8, at * step) for at, steps in enumerate((0, 1, 3, 2))]
    heads = attend(factor, lists, plan, arrays, half)
    heads = [heads[0]] + [shift(heads[steps], "x", -steps) for steps in (1, 2, 3)]

    columns = jnp.stack([side * heads_here + slot for side, slot in slots]).astype(jnp.int32)
    whole = CUTS[0][0], CUTS[-1][1]

    def shares(targets, cuts):
        chips = jnp.stack([chip(*target) for target in targets]).astype(jnp.int32)
        return leave(chips, columns, leaving, heads, [cuts] * len(targets))

    parts = shares([(1, 2)], CUTS)
    near = [(0, 2), (1, 1), (1, -1), (0, -1), (0, 1), (1, 0), (0, 0)]
    share = dict(zip(near, shares(near, (whole,))))
    first = swap(parts[0], "yl")
    second = shift(parts[1], "z", 1)
    third = shift(parts[2], "z", -1)
    down, up, side = arrive(
        [(CUTS[0],), (CUTS[1],), (CUTS[2],)],
        *[share[0, 2], first, share[1, 1], second, share[1, -1], third],
    )
    down, up, side = shift(down, "z", -1), shift(up, "z", 1), swap(side, "yl")
    down, side = arrive(
        [(whole, whole), (whole,)], share[0, -1], down, side, share[1, 0], up
    )
    down, up, side = shift(down, "z", -1), shift(share[0, 1], "z", 1), swap(side, "yl")
    (summed,) = arrive([(whole, whole, whole)], share[0, 0], down, up, side)

    kept, given = mine_and_given(summed, 0)
    other = swap(given, "core")
    projected = jnp.concatenate(
        [jnp.where(core == 0, kept, other), jnp.where(core == 0, other, kept)], axis=1
    ).astype(jnp.float32)
    start = lax.axis_index(HEAD) * local
    gate = lax.dynamic_slice_in_dim(modulation, start, local, 1)[2][:, None]
    return (across.astype(jnp.float32) + gate * projected).astype(jnp.bfloat16).T


def solution(mesh):
    fine = Mesh(mesh.devices.reshape(2, 4, 2, 4, 2), ("yh", "x", "yl", "z", "core"))
    placed = (
        P(FRAME, HEAD),
        P(None, None, HEAD),
        P(HEAD, None),
        P(),
        P(HEAD, FRAME, None),
    )
    return jax.shard_map(
        shards, mesh=fine, in_specs=placed, out_specs=P(FRAME, HEAD), check_vma=False
    )
```

```python
import functools
import math

import jax
import jax.numpy as jnp
from jax import lax
from jax.experimental import pallas as pl
from jax.experimental.pallas import tpu as pltpu
from jax.sharding import Mesh
from jax.sharding import PartitionSpec as P

BLK = 128
EPSILON = 1e-06
NEGATIVE = -1e30
FRAME = ("yh", "x")
HEAD = ("yl", "z", "core")
MIB = 1 << 20
PAIRS = 8
CUTS = ((0, 256), (256, 512), (512, 640))


DEEP = CUTS[-1][1]


def shift(value, axis, steps):
    count = lax.axis_size(axis)
    return lax.ppermute(value, axis, [(i, (i + steps) % count) for i in range(count)])


def swap(value, axis):
    return shift(value, axis, 1)


def lay_kernel(core, mine, other, out):
    first = core[0] == 0
    mine, other = mine[...].astype(jnp.float32), other[...].astype(jnp.float32)
    half = mine.shape[0]
    upper = jnp.where(first, mine, other)
    lower = jnp.where(first, other, mine)
    out[...] = jnp.concatenate([upper, lower], axis=0).T.astype(out.dtype)


def lay(core, mine, other):
    half, count = mine.shape
    return pl.pallas_call(
        lay_kernel,
        in_specs=[pl.BlockSpec(memory_space=pltpu.SMEM)]
        + [pl.BlockSpec(memory_space=pltpu.VMEM)] * 2,
        out_specs=pl.BlockSpec(memory_space=pltpu.VMEM),
        out_shape=jax.ShapeDtypeStruct((count, 2 * half), mine.dtype),
        compiler_params=pltpu.CompilerParams(vmem_limit_bytes=12 * MIB),
        cost_estimate=pl.CostEstimate(
            flops=0, bytes_accessed=8 * half * count, transcendentals=0
        ),
        name="lay",
    )(jnp.reshape(core, (1,)).astype(jnp.int32), mine, other)


def together(arrays, others=()):
    return lax.optimization_barrier((*arrays, *others))[: len(arrays)]


ROWS = 32


def project_kernel(chips, heads, *refs):
    xs, weights, modulation, rest = refs[:10], refs[10:14], refs[14], refs[15:]
    (kv0, q0, *packed), (normed, total) = rest[:-2], rest[-2:]
    step = pl.program_id(0)
    features = 8 * DEEP
    count = normed.shape[1]
    lay = [(piece, 0, x) for piece, x in enumerate(xs[:7])]
    lay += [(7, cut[0], x) for cut, x in zip(CUTS, xs[7:])]
    tiles = [
        (piece, first + at, x, at) for piece, first, x in lay for at in range(0, x.shape[1], BLK)
    ]

    @pl.when(step == 0)
    def _():
        total[...] = jnp.zeros_like(total)

        def norm(i, _):
            rows = pl.ds(pl.multiple_of(i * ROWS, ROWS), ROWS)

            def load(x, at):
                return x[rows, at : at + BLK].astype(jnp.float32)

            summed = jnp.zeros((ROWS, BLK), jnp.float32)
            for _, _, x, at in tiles:
                summed = summed + load(x, at)
            center = jnp.sum(summed, axis=1, keepdims=True) / features
            center = jnp.broadcast_to(center, (ROWS, BLK))
            summed = jnp.zeros((ROWS, BLK), jnp.float32)
            for _, _, x, at in tiles:
                summed = summed + jnp.square(load(x, at) - center)
            spread = jnp.sum(summed, axis=1, keepdims=True) / features
            rate = jnp.broadcast_to(lax.rsqrt(spread + EPSILON), (ROWS, BLK))
            for piece, first, x, at in tiles:
                place = pl.ds(pl.multiple_of(chips[piece] * DEEP + first, BLK), BLK)
                gain = 1.0 + modulation[1:2, place]
                value = (load(x, at) - center) * rate * gain + modulation[0:1, place]
                column = piece % 2 * DEEP + first
                normed[piece // 2, rows, column : column + BLK] = value.astype(jnp.bfloat16)
            return 0

        lax.fori_loop(0, count // ROWS, norm, 0)

    held = normed[step]
    for side in range(2):
        for part in range(3):
            weight = jnp.concatenate([w[part] for w in weights[2 * side : 2 * side + 2]], axis=0)
            made = jnp.dot(held, weight, preferred_element_type=jnp.float32)
            for slot in range(2):
                total[side * 6 + part * 2 + slot] += made[:, slot * BLK : (slot + 1) * BLK]

    @pl.when(step == pl.num_programs(0) - 1)
    def _():
        for index in range(4):
            if index:
                kv, q = packed[index - 1], packed[index - 1].at[2 * BLK :]
            else:
                kv, q = kv0, q0
            base = heads[index]
            q[...] = total[base].T.astype(jnp.bfloat16)
            keys = total[base + 2]
            for part in range(count // BLK):
                rows = slice(part * BLK, (part + 1) * BLK)
                kv[:BLK, rows] = keys[rows].astype(jnp.bfloat16)
            kv[BLK : 2 * BLK, :] = total[base + 4].T.astype(jnp.bfloat16)


def project(chips, heads, xs, own, other, modulation):
    parts, features, inner = own.shape
    count, deep = xs[0].shape
    whole = lambda shape: pl.BlockSpec(shape, lambda k, *_: (0, 0))
    blocks = [
        pl.BlockSpec((parts, deep, inner), lambda k, chips, heads, i=i: (0, chips[2 * k + i], 0))
        for i in range(2)
    ]
    shapes = [(2 * BLK, count), (BLK, count)] + [(3 * BLK, count)] * 3
    return pl.pallas_call(
        project_kernel,
        grid_spec=pltpu.PrefetchScalarGridSpec(
            num_scalar_prefetch=2,
            grid=(features // deep // 2,),
            in_specs=[whole(x.shape) for x in xs]
            + [*blocks, *blocks, whole(modulation.shape)],
            out_specs=[whole(s) for s in shapes],
            scratch_shapes=[
                pltpu.VMEM((features // deep // 2, count, 2 * deep), jnp.bfloat16),
                pltpu.VMEM((2 * parts * inner // BLK, count, BLK), jnp.float32),
            ],
        ),
        out_shape=[jax.ShapeDtypeStruct(s, jnp.bfloat16) for s in shapes],
        compiler_params=pltpu.CompilerParams(vmem_limit_bytes=44 * MIB),
        cost_estimate=pl.CostEstimate(
            flops=4 * parts * inner * features * count,
            bytes_accessed=2 * features * (count + 2 * parts * inner),
            transcendentals=0,
        ),
        name="project",
    )(chips, heads, *xs, own, own, other, other, modulation)


def attend_kernel(factor, unroll, plan, places, counts, first, owner, *refs):
    arrays, outs, rest = refs[: -4 - 8], refs[-4 - 8 : -8], refs[-8:]
    kv, query, asked, scores, tops, totals, sums, arrived = rest
    copies = []
    for kind, index, array, start in plan:
        to = (kv if kind == "kv" else query).at[index]
        rows = to.shape[0]
        copies.append(
            pltpu.make_async_copy(
                arrays[array].at[start : start + rows], to, arrived.at[len(copies)]
            )
        )
    for copy in copies:
        copy.start()
    per_piece = kv.shape[2] // BLK
    rows = len(outs) * per_piece
    tops[...] = jnp.full_like(tops, NEGATIVE)
    totals[...] = jnp.zeros_like(totals)
    sums[...] = jnp.zeros_like(sums)
    for copy in copies:
        copy.wait()
    for index in range(len(outs)):
        for part in range(per_piece):
            asked[index * per_piece + part] = query[index, :, part * BLK : (part + 1) * BLK]

    def find(pair, low, high):
        live = pair < high
        pair = jnp.where(live, pair, low)
        row = owner[pair]
        place = 2 * (pair - first[row])
        wheres = [places[row, place], places[row, place + 1]]
        offsets = [
            jnp.where(live, 0.0, NEGATIVE),
            jnp.where(live & (place + 1 < counts[row]), 0.0, NEGATIVE),
        ]
        return row, wheres, offsets

    def held(where, part):
        start = pl.multiple_of((where & (per_piece - 1)) * BLK, BLK)
        return kv[where >> 2, part * BLK : (part + 1) * BLK, pl.ds(start, BLK)]

    def fold(op, value):
        return op(value.reshape(BLK // 8, 8, BLK), axis=0)

    def rate(low, high, step, _):
        found = []
        for item in range(unroll):
            pair = step * unroll + item
            row, wheres, offsets = find(low + pair, low, high)
            keys = jnp.concatenate([held(where, 0) for where in wheres], axis=0)
            score = jnp.dot(keys, asked[row], preferred_element_type=jnp.float32)
            scores[pair] = score
            best = jnp.maximum(
                fold(jnp.max, score[:BLK]) + offsets[0], fold(jnp.max, score[BLK:]) + offsets[1]
            )
            found.append((row, best))
        for row, best in found:
            tops[row] = jnp.maximum(tops[row], best)
        return 0

    def gather(low, high, step, _):
        found = []
        for item in range(unroll):
            pair = step * unroll + item
            row, wheres, offsets = find(low + pair, low, high)
            top = tops[row][:1]
            score = scores[pair]
            halves = [
                jnp.exp2(score[part * BLK : (part + 1) * BLK] * factor - (top - offsets[part]))
                for part in range(2)
            ]
            total = fold(jnp.sum, halves[0]) + fold(jnp.sum, halves[1])
            weights = jnp.concatenate([half.astype(jnp.bfloat16) for half in halves], axis=0)
            values = jnp.concatenate([held(where, 1) for where in wheres], axis=1)
            summed = jnp.dot(values, weights, preferred_element_type=jnp.float32)
            found.append((row, total, summed))
        for row, total, summed in found:
            totals[row] += total
            sums[row] += summed
        return 0

    for index in range(len(outs)):
        low, high = first[index * per_piece], first[(index + 1) * per_piece]
        steps = (high - low + unroll - 1) // unroll
        lax.fori_loop(0, steps, functools.partial(rate, low, high), 0)
        for row in range(index * per_piece, (index + 1) * per_piece):
            top = jnp.max(tops[row], axis=0, keepdims=True) * factor
            tops[row] = jnp.broadcast_to(top, tops.shape[1:])
        lax.fori_loop(0, steps, functools.partial(gather, low, high), 0)

    for index, out in enumerate(outs):
        for part in range(per_piece):
            row = index * per_piece + part
            total = jnp.sum(totals[row], axis=0, keepdims=True)
            value = (sums[row] / total).T.astype(jnp.bfloat16)
            out[part * BLK : (part + 1) * BLK, :] = value


def pair_lists(counts, most):
    twos = (counts + 1) // 2
    rows = counts.shape[0]
    order = jnp.arange(rows + 1, dtype=jnp.int32)
    first = jnp.sum(jnp.where(order[None, :rows] < order[:, None], twos[None, :], 0), axis=1)
    slots = jnp.arange(rows * most // 2, dtype=jnp.int32)
    return first, jnp.sum(jnp.where(first[None, 1:] <= slots[:, None], 1, 0), axis=1)


def attend(factor, lists, plan, arrays, count):
    rows, most = lists[0].shape
    pieces = most * BLK // count
    asking = rows * BLK // count

    def kernel(*refs):
        attend_kernel(factor, PAIRS, plan, *refs)

    shape = (BLK, count)
    return pl.pallas_call(
        kernel,
        in_specs=[pl.BlockSpec(memory_space=pltpu.SMEM)] * len(lists)
        + [pl.BlockSpec(memory_space=pl.ANY)] * len(arrays),
        out_specs=[pl.BlockSpec(memory_space=pltpu.VMEM)] * asking,
        out_shape=[jax.ShapeDtypeStruct((count, BLK), jnp.bfloat16)] * asking,
        scratch_shapes=[
            pltpu.VMEM((pieces, 2 * BLK, count), jnp.bfloat16),
            pltpu.VMEM((asking, *shape), jnp.bfloat16),
            pltpu.VMEM((rows, BLK, BLK), jnp.bfloat16),
            pltpu.VMEM((rows * most // 2 // asking + PAIRS, 2 * BLK, BLK), jnp.float32),
            pltpu.VMEM((rows, 8, BLK), jnp.float32),
            pltpu.VMEM((rows, 8, BLK), jnp.float32),
            pltpu.VMEM((rows, BLK, BLK), jnp.float32),
            pltpu.SemaphoreType.DMA((len(plan),)),
        ],
        compiler_params=pltpu.CompilerParams(vmem_limit_bytes=32 * MIB),
        cost_estimate=pl.CostEstimate(
            flops=rows * BLK * most * BLK * BLK,
            bytes_accessed=4 * most * BLK * BLK,
            transcendentals=rows * BLK * most * BLK // 4,
        ),
        name="attend",
    )(*lists, *arrays)


def leave_kernel(plan, chips, columns, own, other, *refs):
    heads, outs, ordered = refs[:4], list(refs[4:-1]), refs[-1]
    step = pl.program_id(0)

    @pl.when(step == 0)
    def _():
        for index, head in enumerate(heads):
            ordered[columns[index]] = head[...]

    summed = jnp.dot(
        jnp.concatenate([ordered[index] for index in range(4)], axis=1),
        jnp.concatenate([own[...], other[...]], axis=0),
        preferred_element_type=jnp.float32,
    )
    for index, cuts in enumerate(plan):
        mine = [outs.pop(0) for _ in cuts]

        @pl.when(step == index)
        def _():
            for cut, out in zip(cuts, mine):
                out[...] = summed[:, cut[0] : cut[1]].astype(out.dtype)


def leave(chips, columns, weights, heads, plan):
    count = heads[0].shape[0]
    steps = len(plan)
    inner = weights[0].shape[0]
    block = pl.BlockSpec((inner, DEEP), lambda i, chips, columns: (0, chips[i]))
    whole = lambda shape: pl.BlockSpec(shape, lambda i, *_: (0, 0))
    shapes = [(count, cut[1] - cut[0]) for cuts in plan for cut in cuts]

    def kernel(*refs):
        leave_kernel(plan, *refs)

    return pl.pallas_call(
        kernel,
        grid_spec=pltpu.PrefetchScalarGridSpec(
            num_scalar_prefetch=2,
            grid=(steps,),
            in_specs=[block] * 2 + [whole(h.shape) for h in heads],
            out_specs=[whole(s) for s in shapes],
            scratch_shapes=[pltpu.VMEM((4, count, BLK), jnp.bfloat16)],
        ),
        out_shape=[jax.ShapeDtypeStruct(s, jnp.bfloat16) for s in shapes],
        compiler_params=pltpu.CompilerParams(vmem_limit_bytes=28 * MIB),
        cost_estimate=pl.CostEstimate(
            flops=4 * steps * DEEP * inner * count,
            bytes_accessed=2 * steps * DEEP * (2 * inner + count),
            transcendentals=0,
        ),
        name="leave",
    )(chips, columns, *weights, *heads)


def arrive_kernel(plan, turned, *refs):
    outs = refs[-len(plan) :]
    at = 0
    for cuts, out in zip(plan, outs):
        share, arrived = refs[at], refs[at + 1 : at + 1 + len(cuts)]
        at += 1 + len(cuts)
        edges = sorted({0, share.shape[1], *[edge for cut in cuts for edge in cut]})
        for low, high in zip(edges, edges[1:]):
            value = share[:, low:high].astype(jnp.float32)
            for (first, last), ref in zip(cuts, arrived):
                if first <= low and high <= last:
                    value += ref[:, low - first : high - first].astype(jnp.float32)
            if turned:
                out[low:high, :] = value.T.astype(out.dtype)
            else:
                out[:, low:high] = value.astype(out.dtype)


def arrive(plan, *arrays, turned=False):
    shapes, at = [], 0
    for cuts in plan:
        shapes.append(arrays[at].shape[::-1] if turned else arrays[at].shape)
        at += 1 + len(cuts)

    def kernel(*refs):
        arrive_kernel(plan, turned, *refs)

    return pl.pallas_call(
        kernel,
        in_specs=[pl.BlockSpec(memory_space=pltpu.VMEM)] * len(arrays),
        out_specs=[pl.BlockSpec(memory_space=pltpu.VMEM)] * len(plan),
        out_shape=[jax.ShapeDtypeStruct(shape, arrays[0].dtype) for shape in shapes],
        compiler_params=pltpu.CompilerParams(vmem_limit_bytes=16 * MIB),
        cost_estimate=pl.CostEstimate(
            flops=0, bytes_accessed=8 * arrays[0].size, transcendentals=0
        ),
        name="arrive",
    )(*arrays)


def gather_tokens(own):
    below = shift(own, "z", 1)
    above = shift(own, "z", -1)
    beside = swap(own, "yl")
    below, above, beside = together((below, above, beside))
    far = shift(below, "z", 1)
    beside_below = swap(below, "yl")
    beside_above = shift(beside, "z", -1)
    far, beside_below, beside_above = together((far, beside_below, beside_above))
    first, second, third = [slice(*cut) for cut in CUTS]
    parts = [
        swap(far[:, first], "yl"),
        shift(beside_above[:, second], "z", -1),
        shift(beside_below[:, third], "z", 1),
    ]
    places = [(0, 0), (0, -1), (0, 1), (1, 0), (0, 2), (1, -1), (1, 1), (1, 2)]
    return places, [own, below, above, beside, far, beside_below, beside_above, *parts]


def shards(tokens, qkv_weight, out_weight, modulation, block_mask):
    rows, local = tokens.shape
    features = modulation.shape[1]
    heads_here = block_mask.shape[0]
    inner = qkv_weight.shape[2]
    head_size = inner // heads_here
    factor = math.log2(math.e) / math.sqrt(head_size)
    half = rows // 2
    core = lax.axis_index("core")
    frame_x, frame_y = lax.axis_index("x"), lax.axis_index("yh")
    chip_y, chip_z = lax.axis_index("yl"), lax.axis_index("z")
    across = tokens.T

    def chip(dy, dz):
        return ((chip_y + dy) % 2) * 4 + (chip_z + dz) % 4

    def mine_and_given(value, axis):
        size = value.shape[axis] // 2
        mine = lax.dynamic_slice_in_dim(value, core * size, size, axis)
        return mine, lax.dynamic_slice_in_dim(value, (1 - core) * size, size, axis)

    def head_slot(steps):
        head = (frame_x + steps) % 4
        return jnp.where(head // 2 == core, 0, 1), head % 2

    mine, given = mine_and_given(across, 1)
    other = swap(given, "core")
    own = lay(core, mine, other)
    mask_mine, mask_given = mine_and_given(block_mask, 1)
    mask_other = swap(mask_given, "core")

    raw, *_ = lax.optimization_barrier((qkv_weight, own, mask_other))
    other_weight = swap(raw, "core")
    places, xs = gather_tokens(own)

    chips = jnp.stack([chip(*place) for place in places]).astype(jnp.int32)
    slots = [head_slot(steps) for steps in range(4)]
    bases = jnp.stack([side * 3 * heads_here + slot for side, slot in slots]).astype(jnp.int32)
    kv, query, *packed = project(chips, bases, xs, qkv_weight, other_weight, modulation)
    two, one, three = [shift(packed[i - 1], "x", i) for i in (2, 1, 3)]
    away_kv = swap(kv, "yh")
    out_own, _ = lax.optimization_barrier((out_weight, kv))
    leaving = out_weight, swap(out_own, "core")
    one, three = together((one, three), (away_kv,))
    both = jnp.concatenate([one[: 2 * BLK], three[: 2 * BLK]], axis=0)
    away_both = swap(both, "yh")
    (two,) = together((two,), (away_both,))
    last = two[: 2 * BLK]
    away = [away_kv, away_both, swap(last, "yh")]
    near = jnp.concatenate([kv, both, last], axis=0)
    arrays = [kv, query, one, two, three, *away, swap(near, "core"), *[swap(a, "core") for a in away]]

    mask_mine, mask_other, _ = lax.optimization_barrier((mask_mine, mask_other, one))
    mask_heads = jnp.stack([mask_mine, mask_other])
    mask_rows = []
    for steps in range(4):
        side, slot = head_slot(steps)
        part = lax.dynamic_slice(
            mask_heads, (side, slot, 0, 0), (1, 1, *mask_heads.shape[2:])
        )[0, 0]
        mask_rows.append(shift(part, "x", steps) if steps else part)
    keep = jnp.concatenate(mask_rows, axis=0) != 0
    blocks = jnp.arange(keep.shape[1], dtype=jnp.int32)
    per_core = half // BLK
    piece, inside = blocks // per_core, blocks % per_core
    from_core, from_y = core ^ (piece // 8), frame_y ^ (piece // 4 % 2)
    from_x = (frame_x - piece % 4) % 4
    origin = (from_y * 4 + from_x) * (2 * per_core) + from_core * per_core + inside
    same = origin[:, None] == blocks[None, :]
    keep = jnp.sum(jnp.where(same[None] & keep[:, None, :], 1, 0), axis=2)
    counts = jnp.sum(keep, axis=1)
    earlier = blocks[None, :] < blocks[:, None]
    rank = jnp.sum(jnp.where(earlier[None], keep[:, None, :], 0), axis=2)
    chosen = (keep[:, None, :] != 0) & (rank[:, None, :] == blocks[None, :, None])
    listed = jnp.sum(jnp.where(chosen, blocks[None, None, :], 0), axis=2)
    lists = (listed, counts, *pair_lists(counts, listed.shape[1]))

    step = 2 * BLK
    plan = [("kv", 0, 0, 0), ("q", 0, 1, 0)]
    for steps, array in ((1, 2), (2, 3), (3, 4)):
        plan += [("kv", steps, array, 0), ("q", steps, array, step)]
    for index, array in ((4, 5), (12, 9)):
        plan += [("kv", index, array, 0), ("kv", index + 1, array + 1, 0)]
        plan += [("kv", index + 3, array + 1, step), ("kv", index + 2, array + 2, 0)]
    plan += [("kv", 8 + steps, 8, at * step) for at, steps in enumerate((0, 1, 3, 2))]
    heads = attend(factor, lists, plan, arrays, half)
    heads = [heads[0]] + [shift(heads[steps], "x", -steps) for steps in (1, 2, 3)]

    columns = jnp.stack([side * heads_here + slot for side, slot in slots]).astype(jnp.int32)
    whole = CUTS[0][0], CUTS[-1][1]

    def shares(targets, cuts):
        chips = jnp.stack([chip(*target) for target in targets]).astype(jnp.int32)
        return leave(chips, columns, leaving, heads, [cuts] * len(targets))

    parts = shares([(1, 2)], CUTS)
    near = [(0, 2), (1, 1), (1, -1), (0, -1), (0, 1), (1, 0), (0, 0)]
    share = dict(zip(near, shares(near, (whole,))))
    first = swap(parts[0], "yl")
    second = shift(parts[1], "z", 1)
    third = shift(parts[2], "z", -1)
    down, up, side = arrive(
        [(CUTS[0],), (CUTS[1],), (CUTS[2],)],
        *[share[0, 2], first, share[1, 1], second, share[1, -1], third],
    )
    down, up, side = shift(down, "z", -1), shift(up, "z", 1), swap(side, "yl")
    down, side = arrive(
        [(whole, whole), (whole,)], share[0, -1], down, side, share[1, 0], up
    )
    down, up, side = shift(down, "z", -1), shift(share[0, 1], "z", 1), swap(side, "yl")
    (summed,) = arrive([(whole, whole, whole)], share[0, 0], down, up, side, turned=True)

    kept, given = mine_and_given(summed, 0)
    other = swap(given, "core")
    projected = jnp.concatenate(
        [jnp.where(core == 0, kept, other), jnp.where(core == 0, other, kept)], axis=1
    ).astype(jnp.float32)
    start = lax.axis_index(HEAD) * local
    gate = lax.dynamic_slice_in_dim(modulation, start, local, 1)[2][:, None]
    return (across.astype(jnp.float32) + gate * projected).astype(jnp.bfloat16).T


def solution(mesh):
    fine = Mesh(mesh.devices.reshape(2, 4, 2, 4, 2), ("yh", "x", "yl", "z", "core"))
    placed = (
        P(FRAME, HEAD),
        P(None, None, HEAD),
        P(HEAD, None),
        P(),
        P(HEAD, FRAME, None),
    )
    return jax.shard_map(
        shards, mesh=fine, in_specs=placed, out_specs=P(FRAME, HEAD), check_vma=False
    )
```

```python
import functools
import math

import jax
import jax.numpy as jnp
from jax import lax
from jax.experimental import pallas as pl
from jax.experimental.pallas import tpu as pltpu
from jax.sharding import Mesh
from jax.sharding import PartitionSpec as P

BLK = 128
EPSILON = 1e-06
NEGATIVE = -1e30
FRAME = ("yh", "x")
HEAD = ("yl", "z", "core")
MIB = 1 << 20
PAIRS = 8
CUTS = ((0, 256), (256, 512), (512, 640))


DEEP = CUTS[-1][1]


def shift(value, axis, steps):
    count = lax.axis_size(axis)
    return lax.ppermute(value, axis, [(i, (i + steps) % count) for i in range(count)])


def swap(value, axis):
    return shift(value, axis, 1)


def lay_kernel(core, mine, other, out):
    first = core[0] == 0
    mine, other = mine[...].astype(jnp.float32), other[...].astype(jnp.float32)
    half = mine.shape[0]
    upper = jnp.where(first, mine, other)
    lower = jnp.where(first, other, mine)
    out[...] = jnp.concatenate([upper, lower], axis=0).T.astype(out.dtype)


def lay(core, mine, other):
    half, count = mine.shape
    return pl.pallas_call(
        lay_kernel,
        in_specs=[pl.BlockSpec(memory_space=pltpu.SMEM)]
        + [pl.BlockSpec(memory_space=pltpu.VMEM)] * 2,
        out_specs=pl.BlockSpec(memory_space=pltpu.VMEM),
        out_shape=jax.ShapeDtypeStruct((count, 2 * half), mine.dtype),
        compiler_params=pltpu.CompilerParams(vmem_limit_bytes=12 * MIB),
        cost_estimate=pl.CostEstimate(
            flops=0, bytes_accessed=8 * half * count, transcendentals=0
        ),
        name="lay",
    )(jnp.reshape(core, (1,)).astype(jnp.int32), mine, other)


def together(arrays, others=()):
    return lax.optimization_barrier((*arrays, *others))[: len(arrays)]


ROWS = 32


def project_kernel(chips, heads, *refs):
    xs, weights, modulation, rest = refs[:10], refs[10:14], refs[14], refs[15:]
    outs, (held_x, normed, total, arrived) = rest[:-4], rest[-4:]
    step = pl.program_id(0)
    features = 8 * DEEP
    count = normed.shape[1]
    tiles = [(piece, at) for piece in range(8) for at in range(0, DEEP, BLK)]

    @pl.when(step == 0)
    def _():
        places = [held_x.at[piece] for piece in range(7)]
        places += [held_x.at[7, :, cut[0] : cut[1]] for cut in CUTS]
        copies = [
            pltpu.make_async_copy(x, place, arrived.at[index])
            for index, (x, place) in enumerate(zip(xs, places))
        ]
        for copy in copies:
            copy.start()
        for copy in copies:
            copy.wait()
        total[...] = jnp.zeros_like(total)

        def norm(i, _):
            rows = pl.ds(pl.multiple_of(i * ROWS, ROWS), ROWS)

            def load(piece, at):
                return held_x[piece, rows, at : at + BLK].astype(jnp.float32)

            summed = jnp.zeros((ROWS, BLK), jnp.float32)
            for tile in tiles:
                summed = summed + load(*tile)
            center = jnp.sum(summed, axis=1, keepdims=True) / features
            center = jnp.broadcast_to(center, (ROWS, BLK))
            summed = jnp.zeros((ROWS, BLK), jnp.float32)
            for tile in tiles:
                summed = summed + jnp.square(load(*tile) - center)
            spread = jnp.sum(summed, axis=1, keepdims=True) / features
            rate = jnp.broadcast_to(lax.rsqrt(spread + EPSILON), (ROWS, BLK))
            for piece, at in tiles:
                place = pl.ds(pl.multiple_of(chips[piece] * DEEP + at, BLK), BLK)
                gain = 1.0 + modulation[1:2, place]
                value = (load(piece, at) - center) * rate * gain + modulation[0:1, place]
                column = piece % 2 * DEEP + at
                normed[piece // 2, rows, column : column + BLK] = value.astype(jnp.bfloat16)
            return 0

        lax.fori_loop(0, count // ROWS, norm, 0)

    held = normed[step]
    for side in range(2):
        for part in range(3):
            weight = jnp.concatenate([w[part] for w in weights[2 * side : 2 * side + 2]], axis=0)
            made = jnp.dot(held, weight, preferred_element_type=jnp.float32)
            for slot in range(2):
                total[side * 6 + part * 2 + slot] += made[:, slot * BLK : (slot + 1) * BLK]

    @pl.when(step == pl.num_programs(0) - 1)
    def _():
        for index in range(4):
            kv, q = outs[2 * index], outs[2 * index + 1]
            base = heads[index]
            q[...] = total[base].T.astype(jnp.bfloat16)
            keys = total[base + 2]
            for part in range(count // BLK):
                rows = slice(part * BLK, (part + 1) * BLK)
                kv[:BLK, rows] = keys[rows].astype(jnp.bfloat16)
            kv[BLK : 2 * BLK, :] = total[base + 4].T.astype(jnp.bfloat16)


def project(chips, heads, xs, own, other, modulation):
    parts, features, inner = own.shape
    count, deep = xs[0].shape
    whole = lambda shape: pl.BlockSpec(shape, lambda k, *_: (0, 0))
    blocks = [
        pl.BlockSpec((parts, deep, inner), lambda k, chips, heads, i=i: (0, chips[2 * k + i], 0))
        for i in range(2)
    ]
    shapes = [(2 * BLK, count), (BLK, count)] * 4
    return pl.pallas_call(
        project_kernel,
        grid_spec=pltpu.PrefetchScalarGridSpec(
            num_scalar_prefetch=2,
            grid=(features // deep // 2,),
            in_specs=[pl.BlockSpec(memory_space=pl.ANY)] * len(xs)
            + [*blocks, *blocks, whole(modulation.shape)],
            out_specs=[whole(s) for s in shapes],
            scratch_shapes=[
                pltpu.VMEM((features // deep, count, deep), jnp.bfloat16),
                pltpu.VMEM((features // deep // 2, count, 2 * deep), jnp.bfloat16),
                pltpu.VMEM((2 * parts * inner // BLK, count, BLK), jnp.float32),
                pltpu.SemaphoreType.DMA((len(xs),)),
            ],
        ),
        out_shape=[jax.ShapeDtypeStruct(s, jnp.bfloat16) for s in shapes],
        compiler_params=pltpu.CompilerParams(vmem_limit_bytes=56 * MIB),
        cost_estimate=pl.CostEstimate(
            flops=4 * parts * inner * features * count,
            bytes_accessed=2 * features * (count + 2 * parts * inner),
            transcendentals=0,
        ),
        name="project",
    )(chips, heads, *xs, own, own, other, other, modulation)


def attend_kernel(factor, unroll, plan, places, counts, first, owner, *refs):
    arrays, outs, rest = refs[: -4 - 8], refs[-4 - 8 : -8], refs[-8:]
    kv, query, asked, scores, tops, totals, sums, arrived = rest
    copies = []
    for kind, index, array, start in plan:
        to = (kv if kind == "kv" else query).at[index]
        rows = to.shape[0]
        copies.append(
            pltpu.make_async_copy(
                arrays[array].at[start : start + rows], to, arrived.at[len(copies)]
            )
        )
    for copy in copies:
        copy.start()
    per_piece = kv.shape[2] // BLK
    rows = len(outs) * per_piece
    tops[...] = jnp.full_like(tops, NEGATIVE)
    totals[...] = jnp.zeros_like(totals)
    sums[...] = jnp.zeros_like(sums)
    for copy in copies:
        copy.wait()
    for index in range(len(outs)):
        for part in range(per_piece):
            asked[index * per_piece + part] = query[index, :, part * BLK : (part + 1) * BLK]

    def find(pair, low, high):
        live = pair < high
        pair = jnp.where(live, pair, low)
        row = owner[pair]
        place = 2 * (pair - first[row])
        wheres = [places[row, place], places[row, place + 1]]
        offsets = [
            jnp.where(live, 0.0, NEGATIVE),
            jnp.where(live & (place + 1 < counts[row]), 0.0, NEGATIVE),
        ]
        return row, wheres, offsets

    def held(where, part):
        start = pl.multiple_of((where & (per_piece - 1)) * BLK, BLK)
        return kv[where >> 2, part * BLK : (part + 1) * BLK, pl.ds(start, BLK)]

    def fold(op, value):
        return op(value.reshape(BLK // 8, 8, BLK), axis=0)

    def rate(low, high, step, _):
        found = []
        for item in range(unroll):
            pair = step * unroll + item
            row, wheres, offsets = find(low + pair, low, high)
            keys = jnp.concatenate([held(where, 0) for where in wheres], axis=0)
            score = jnp.dot(keys, asked[row], preferred_element_type=jnp.float32)
            scores[pair] = score
            best = jnp.maximum(
                fold(jnp.max, score[:BLK]) + offsets[0], fold(jnp.max, score[BLK:]) + offsets[1]
            )
            found.append((row, best))
        for row, best in found:
            tops[row] = jnp.maximum(tops[row], best)
        return 0

    def gather(low, high, step, _):
        found = []
        for item in range(unroll):
            pair = step * unroll + item
            row, wheres, offsets = find(low + pair, low, high)
            top = tops[row][:1]
            score = scores[pair]
            halves = [
                jnp.exp2(score[part * BLK : (part + 1) * BLK] * factor - (top - offsets[part]))
                for part in range(2)
            ]
            total = fold(jnp.sum, halves[0]) + fold(jnp.sum, halves[1])
            weights = jnp.concatenate([half.astype(jnp.bfloat16) for half in halves], axis=0)
            values = jnp.concatenate([held(where, 1) for where in wheres], axis=1)
            summed = jnp.dot(values, weights, preferred_element_type=jnp.float32)
            found.append((row, total, summed))
        for row, total, summed in found:
            totals[row] += total
            sums[row] += summed
        return 0

    for index in range(len(outs)):
        low, high = first[index * per_piece], first[(index + 1) * per_piece]
        steps = (high - low + unroll - 1) // unroll
        lax.fori_loop(0, steps, functools.partial(rate, low, high), 0)
        for row in range(index * per_piece, (index + 1) * per_piece):
            top = jnp.max(tops[row], axis=0, keepdims=True) * factor
            tops[row] = jnp.broadcast_to(top, tops.shape[1:])
        lax.fori_loop(0, steps, functools.partial(gather, low, high), 0)

    for index, out in enumerate(outs):
        for part in range(per_piece):
            row = index * per_piece + part
            total = jnp.sum(totals[row], axis=0, keepdims=True)
            value = (sums[row] / total).T.astype(jnp.bfloat16)
            out[part * BLK : (part + 1) * BLK, :] = value


def pair_lists(counts, most):
    twos = (counts + 1) // 2
    rows = counts.shape[0]
    order = jnp.arange(rows + 1, dtype=jnp.int32)
    first = jnp.sum(jnp.where(order[None, :rows] < order[:, None], twos[None, :], 0), axis=1)
    slots = jnp.arange(rows * most // 2, dtype=jnp.int32)
    return first, jnp.sum(jnp.where(first[None, 1:] <= slots[:, None], 1, 0), axis=1)


def attend(factor, lists, plan, arrays, count):
    rows, most = lists[0].shape
    pieces = most * BLK // count
    asking = rows * BLK // count

    def kernel(*refs):
        attend_kernel(factor, PAIRS, plan, *refs)

    shape = (BLK, count)
    return pl.pallas_call(
        kernel,
        in_specs=[pl.BlockSpec(memory_space=pltpu.SMEM)] * len(lists)
        + [pl.BlockSpec(memory_space=pl.ANY)] * len(arrays),
        out_specs=[pl.BlockSpec(memory_space=pltpu.VMEM)] * asking,
        out_shape=[jax.ShapeDtypeStruct((count, BLK), jnp.bfloat16)] * asking,
        scratch_shapes=[
            pltpu.VMEM((pieces, 2 * BLK, count), jnp.bfloat16),
            pltpu.VMEM((asking, *shape), jnp.bfloat16),
            pltpu.VMEM((rows, BLK, BLK), jnp.bfloat16),
            pltpu.VMEM((rows * most // 2 // asking + PAIRS, 2 * BLK, BLK), jnp.float32),
            pltpu.VMEM((rows, 8, BLK), jnp.float32),
            pltpu.VMEM((rows, 8, BLK), jnp.float32),
            pltpu.VMEM((rows, BLK, BLK), jnp.float32),
            pltpu.SemaphoreType.DMA((len(plan),)),
        ],
        compiler_params=pltpu.CompilerParams(vmem_limit_bytes=32 * MIB),
        cost_estimate=pl.CostEstimate(
            flops=rows * BLK * most * BLK * BLK,
            bytes_accessed=4 * most * BLK * BLK,
            transcendentals=rows * BLK * most * BLK // 4,
        ),
        name="attend",
    )(*lists, *arrays)


def leave_kernel(plan, chips, columns, own, other, *refs):
    heads, outs, ordered, arrived = refs[:4], list(refs[4:-2]), *refs[-2:]
    step = pl.program_id(0)

    @pl.when(step == 0)
    def _():
        copies = [
            pltpu.make_async_copy(head, ordered.at[columns[index]], arrived.at[index])
            for index, head in enumerate(heads)
        ]
        for copy in copies:
            copy.start()
        for copy in copies:
            copy.wait()

    summed = jnp.dot(
        jnp.concatenate([ordered[index] for index in range(4)], axis=1),
        jnp.concatenate([own[...], other[...]], axis=0),
        preferred_element_type=jnp.float32,
    )
    for index, cuts in enumerate(plan):
        mine = [outs.pop(0) for _ in cuts]

        @pl.when(step == index)
        def _():
            for cut, out in zip(cuts, mine):
                out[...] = summed[:, cut[0] : cut[1]].astype(out.dtype)


def leave(chips, columns, weights, heads, plan):
    count = heads[0].shape[0]
    steps = len(plan)
    inner = weights[0].shape[0]
    block = pl.BlockSpec((inner, DEEP), lambda i, chips, columns: (0, chips[i]))
    whole = lambda shape: pl.BlockSpec(shape, lambda i, *_: (0, 0))
    shapes = [(count, cut[1] - cut[0]) for cuts in plan for cut in cuts]

    def kernel(*refs):
        leave_kernel(plan, *refs)

    return pl.pallas_call(
        kernel,
        grid_spec=pltpu.PrefetchScalarGridSpec(
            num_scalar_prefetch=2,
            grid=(steps,),
            in_specs=[block] * 2 + [pl.BlockSpec(memory_space=pl.ANY)] * 4,
            out_specs=[whole(s) for s in shapes],
            scratch_shapes=[
                pltpu.VMEM((4, count, BLK), jnp.bfloat16),
                pltpu.SemaphoreType.DMA((4,)),
            ],
        ),
        out_shape=[jax.ShapeDtypeStruct(s, jnp.bfloat16) for s in shapes],
        compiler_params=pltpu.CompilerParams(vmem_limit_bytes=28 * MIB),
        cost_estimate=pl.CostEstimate(
            flops=4 * steps * DEEP * inner * count,
            bytes_accessed=2 * steps * DEEP * (2 * inner + count),
            transcendentals=0,
        ),
        name="leave",
    )(chips, columns, *weights, *heads)


def arrive_kernel(plan, turned, *refs):
    outs = refs[-len(plan) :]
    at = 0
    for cuts, out in zip(plan, outs):
        share, arrived = refs[at], refs[at + 1 : at + 1 + len(cuts)]
        at += 1 + len(cuts)
        edges = sorted({0, share.shape[1], *[edge for cut in cuts for edge in cut]})
        for low, high in zip(edges, edges[1:]):
            value = share[:, low:high].astype(jnp.float32)
            for (first, last), ref in zip(cuts, arrived):
                if first <= low and high <= last:
                    value += ref[:, low - first : high - first].astype(jnp.float32)
            if turned:
                out[low:high, :] = value.T.astype(out.dtype)
            else:
                out[:, low:high] = value.astype(out.dtype)


def arrive(plan, *arrays, turned=False):
    shapes, at = [], 0
    for cuts in plan:
        shapes.append(arrays[at].shape[::-1] if turned else arrays[at].shape)
        at += 1 + len(cuts)

    def kernel(*refs):
        arrive_kernel(plan, turned, *refs)

    return pl.pallas_call(
        kernel,
        in_specs=[pl.BlockSpec(memory_space=pltpu.VMEM)] * len(arrays),
        out_specs=[pl.BlockSpec(memory_space=pltpu.VMEM)] * len(plan),
        out_shape=[jax.ShapeDtypeStruct(shape, arrays[0].dtype) for shape in shapes],
        compiler_params=pltpu.CompilerParams(vmem_limit_bytes=16 * MIB),
        cost_estimate=pl.CostEstimate(
            flops=0, bytes_accessed=8 * arrays[0].size, transcendentals=0
        ),
        name="arrive",
    )(*arrays)


def gather_tokens(own, first_others, second_others):
    below = shift(own, "z", 1)
    above = shift(own, "z", -1)
    beside = swap(own, "yl")
    below, above, beside = together((below, above, beside), first_others)
    far = shift(below, "z", 1)
    beside_below = swap(below, "yl")
    beside_above = shift(beside, "z", -1)
    far, beside_below, beside_above = together((far, beside_below, beside_above), second_others)
    first, second, third = [slice(*cut) for cut in CUTS]
    parts = [
        swap(far[:, first], "yl"),
        shift(beside_above[:, second], "z", -1),
        shift(beside_below[:, third], "z", 1),
    ]
    places = [(0, 0), (0, -1), (0, 1), (1, 0), (0, 2), (1, -1), (1, 1), (1, 2)]
    return places, [own, below, above, beside, far, beside_below, beside_above, *parts]


def shards(tokens, qkv_weight, out_weight, modulation, block_mask):
    rows, local = tokens.shape
    features = modulation.shape[1]
    heads_here = block_mask.shape[0]
    inner = qkv_weight.shape[2]
    head_size = inner // heads_here
    factor = math.log2(math.e) / math.sqrt(head_size)
    half = rows // 2
    core = lax.axis_index("core")
    frame_x, frame_y = lax.axis_index("x"), lax.axis_index("yh")
    chip_y, chip_z = lax.axis_index("yl"), lax.axis_index("z")
    across = tokens.T

    def chip(dy, dz):
        return ((chip_y + dy) % 2) * 4 + (chip_z + dz) % 4

    def mine_and_given(value, axis):
        size = value.shape[axis] // 2
        mine = lax.dynamic_slice_in_dim(value, core * size, size, axis)
        return mine, lax.dynamic_slice_in_dim(value, (1 - core) * size, size, axis)

    def head_slot(steps):
        head = (frame_x + steps) % 4
        return jnp.where(head // 2 == core, 0, 1), head % 2

    mine, given = mine_and_given(across, 1)
    other = swap(given, "core")
    own = lay(core, mine, other)
    mask_mine, mask_given = mine_and_given(block_mask, 1)
    mask_other = swap(mask_given, "core")

    raw, *_ = lax.optimization_barrier((qkv_weight, own, mask_other))
    other_weight = swap(raw, "core")
    mask_heads = jnp.stack([mask_mine, mask_other])
    mask_rows = []
    for steps in range(4):
        side, slot = head_slot(steps)
        part = lax.dynamic_slice(
            mask_heads, (side, slot, 0, 0), (1, 1, *mask_heads.shape[2:])
        )[0, 0]
        mask_rows.append(shift(part, "x", steps) if steps else part)
    keep = jnp.concatenate(mask_rows, axis=0) != 0
    blocks = jnp.arange(keep.shape[1], dtype=jnp.int32)
    per_core = half // BLK
    piece, inside = blocks // per_core, blocks % per_core
    from_core, from_y = core ^ (piece // 8), frame_y ^ (piece // 4 % 2)
    from_x = (frame_x - piece % 4) % 4
    origin = (from_y * 4 + from_x) * (2 * per_core) + from_core * per_core + inside
    same = origin[:, None] == blocks[None, :]
    keep = jnp.sum(jnp.where(same[None] & keep[:, None, :], 1, 0), axis=2)
    counts = jnp.sum(keep, axis=1)
    earlier = blocks[None, :] < blocks[:, None]
    rank = jnp.sum(jnp.where(earlier[None], keep[:, None, :], 0), axis=2)
    chosen = (keep[:, None, :] != 0) & (rank[:, None, :] == blocks[None, :, None])
    listed = jnp.sum(jnp.where(chosen, blocks[None, None, :], 0), axis=2)
    lists = (listed, counts, *pair_lists(counts, listed.shape[1]))
    places, xs = gather_tokens(own, (), mask_rows[1:])

    chips = jnp.stack([chip(*place) for place in places]).astype(jnp.int32)
    slots = [head_slot(steps) for steps in range(4)]
    bases = jnp.stack([side * 3 * heads_here + slot for side, slot in slots]).astype(jnp.int32)
    made = project(chips, bases, xs, qkv_weight, other_weight, modulation)
    kv, queries = made[::2], made[1::2]
    one, three = shift(kv[1], "x", 1), shift(kv[3], "x", 3)
    away_kv = swap(kv[0], "yh")
    one, three = together((one, three), (away_kv,))
    both = jnp.concatenate([one, three], axis=0)
    away_both = swap(both, "yh")
    kv_two, *asked = together((kv[2], *queries[1:]), (one,))
    two = shift(kv_two, "x", 2)
    queries = [queries[0]] + [shift(asked[i - 1], "x", i) for i in (1, 2, 3)]
    near = swap(jnp.concatenate([kv[0], both], axis=0), "core")
    away_kv_other = swap(away_kv, "core")
    two, out_own = together(
        (two, out_weight), (away_both, *queries[1:], *lists, near, away_kv_other)
    )
    away_two = swap(two, "yh")
    arrays = [kv[0], both, two, away_kv, away_both, away_two, near, swap(two, "core")]
    arrays += [away_kv_other, swap(away_both, "core"), swap(away_two, "core")] + queries
    leaving = out_weight, swap(out_own, "core")
    step = 2 * BLK
    plan = []
    for index, array in ((0, 0), (4, 3), (12, 8)):
        plan += [("kv", index, array, 0), ("kv", index + 1, array + 1, 0)]
        plan += [("kv", index + 3, array + 1, step), ("kv", index + 2, array + 2, 0)]
    plan += [("kv", 8, 6, 0), ("kv", 9, 6, step), ("kv", 11, 6, 2 * step), ("kv", 10, 7, 0)]
    plan += [("q", index, 11 + index, 0) for index in range(4)]
    heads = attend(factor, lists, plan, arrays, half)
    heads = [heads[0]] + [shift(heads[steps], "x", -steps) for steps in (1, 2, 3)]

    columns = jnp.stack([side * heads_here + slot for side, slot in slots]).astype(jnp.int32)
    whole = CUTS[0][0], CUTS[-1][1]

    def shares(targets, cuts, heads):
        chips = jnp.stack([chip(*target) for target in targets]).astype(jnp.int32)
        return leave(chips, columns, leaving, heads, [cuts] * len(targets))

    parts = shares([(1, 2)], CUTS, heads)
    middle = [(0, 2), (1, 1), (1, -1)]
    share = dict(zip(middle, shares(middle, (whole,), heads)))
    first = swap(parts[0], "yl")
    second = shift(parts[1], "z", 1)
    third = shift(parts[2], "z", -1)
    heads = together(heads, (first, second, third))
    near = [(0, -1), (0, 1), (1, 0), (0, 0)]
    share |= dict(zip(near, shares(near, (whole,), heads)))
    down, up, side = arrive(
        [(CUTS[0],), (CUTS[1],), (CUTS[2],)],
        *[share[0, 2], first, share[1, 1], second, share[1, -1], third],
    )
    down, up, side = shift(down, "z", -1), shift(up, "z", 1), swap(side, "yl")
    down, side = arrive(
        [(whole, whole), (whole,)], share[0, -1], down, side, share[1, 0], up
    )
    down, up, side = shift(down, "z", -1), shift(share[0, 1], "z", 1), swap(side, "yl")
    (summed,) = arrive([(whole, whole, whole)], share[0, 0], down, up, side, turned=True)

    kept, given = mine_and_given(summed, 0)
    other = swap(given, "core")
    projected = jnp.concatenate(
        [jnp.where(core == 0, kept, other), jnp.where(core == 0, other, kept)], axis=1
    ).astype(jnp.float32)
    start = lax.axis_index(HEAD) * local
    gate = lax.dynamic_slice_in_dim(modulation, start, local, 1)[2][:, None]
    return (across.astype(jnp.float32) + gate * projected).astype(jnp.bfloat16).T


def solution(mesh):
    fine = Mesh(mesh.devices.reshape(2, 4, 2, 4, 2), ("yh", "x", "yl", "z", "core"))
    placed = (
        P(FRAME, HEAD),
        P(None, None, HEAD),
        P(HEAD, None),
        P(),
        P(HEAD, FRAME, None),
    )
    return jax.shard_map(
        shards, mesh=fine, in_specs=placed, out_specs=P(FRAME, HEAD), check_vma=False
    )
```

```python
import functools
import math

import jax
import jax.numpy as jnp
from jax import lax
from jax.experimental import pallas as pl
from jax.experimental.pallas import tpu as pltpu
from jax.sharding import Mesh
from jax.sharding import PartitionSpec as P

BLK = 128
EPSILON = 1e-06
NEGATIVE = -1e30
FRAME = ("yh", "x")
HEAD = ("yl", "z", "core")
MIB = 1 << 20
PAIRS = 8
CUTS = ((0, 256), (256, 512), (512, 640))


DEEP = CUTS[-1][1]


def shift(value, axis, steps):
    count = lax.axis_size(axis)
    return lax.ppermute(value, axis, [(i, (i + steps) % count) for i in range(count)])


def swap(value, axis):
    return shift(value, axis, 1)


def lay_kernel(core, mine, other, out):
    first = core[0] == 0
    mine, other = mine[...].astype(jnp.float32), other[...].astype(jnp.float32)
    half = mine.shape[0]
    upper = jnp.where(first, mine, other)
    lower = jnp.where(first, other, mine)
    out[...] = jnp.concatenate([upper, lower], axis=0).T.astype(out.dtype)


def lay(core, mine, other):
    half, count = mine.shape
    return pl.pallas_call(
        lay_kernel,
        in_specs=[pl.BlockSpec(memory_space=pltpu.SMEM)]
        + [pl.BlockSpec(memory_space=pltpu.VMEM)] * 2,
        out_specs=pl.BlockSpec(memory_space=pltpu.VMEM),
        out_shape=jax.ShapeDtypeStruct((count, 2 * half), mine.dtype),
        compiler_params=pltpu.CompilerParams(vmem_limit_bytes=12 * MIB),
        cost_estimate=pl.CostEstimate(
            flops=0, bytes_accessed=8 * half * count, transcendentals=0
        ),
        name="lay",
    )(jnp.reshape(core, (1,)).astype(jnp.int32), mine, other)


def together(arrays, others=()):
    return lax.optimization_barrier((*arrays, *others))[: len(arrays)]


ROWS = 64


def project_kernel(chips, heads, *refs):
    xs, weights, modulation, rest = refs[:10], refs[10:14], refs[14], refs[15:]
    outs, (held_x, normed, total, arrived) = rest[:-4], rest[-4:]
    step = pl.program_id(0)
    features = 8 * DEEP
    count = normed.shape[1]
    tiles = [(piece, at) for piece in range(8) for at in range(0, DEEP, BLK)]

    @pl.when(step == 0)
    def _():
        places = [held_x.at[piece] for piece in range(7)]
        places += [held_x.at[7, :, cut[0] : cut[1]] for cut in CUTS]
        copies = [
            pltpu.make_async_copy(x, place, arrived.at[index])
            for index, (x, place) in enumerate(zip(xs, places))
        ]
        for copy in copies:
            copy.start()
        for copy in copies:
            copy.wait()
        total[...] = jnp.zeros_like(total)

        def norm(i, _):
            rows = pl.ds(pl.multiple_of(i * ROWS, ROWS), ROWS)

            def load(piece, at):
                return held_x[piece, rows, at : at + BLK].astype(jnp.float32)

            summed = jnp.zeros((ROWS, BLK), jnp.float32)
            for tile in tiles:
                summed = summed + load(*tile)
            center = jnp.sum(summed, axis=1, keepdims=True) / features
            center = jnp.broadcast_to(center, (ROWS, BLK))
            summed = jnp.zeros((ROWS, BLK), jnp.float32)
            for tile in tiles:
                summed = summed + jnp.square(load(*tile) - center)
            spread = jnp.sum(summed, axis=1, keepdims=True) / features
            rate = jnp.broadcast_to(lax.rsqrt(spread + EPSILON), (ROWS, BLK))
            for piece, at in tiles:
                place = pl.ds(pl.multiple_of(chips[piece] * DEEP + at, BLK), BLK)
                gain = 1.0 + modulation[1:2, place]
                value = (load(piece, at) - center) * rate * gain + modulation[0:1, place]
                column = piece % 2 * DEEP + at
                normed[piece // 2, rows, column : column + BLK] = value.astype(jnp.bfloat16)
            return 0

        lax.fori_loop(0, count // ROWS, norm, 0)

    held = normed[step]
    for side in range(2):
        for part in range(3):
            weight = jnp.concatenate([w[part] for w in weights[2 * side : 2 * side + 2]], axis=0)
            made = jnp.dot(held, weight, preferred_element_type=jnp.float32)
            for slot in range(2):
                total[side * 6 + part * 2 + slot] += made[:, slot * BLK : (slot + 1) * BLK]

    @pl.when(step == pl.num_programs(0) - 1)
    def _():
        for index in range(4):
            kv, q = outs[2 * index], outs[2 * index + 1]
            base = heads[index]
            q[...] = total[base].T.astype(jnp.bfloat16)
            keys = total[base + 2]
            for part in range(count // BLK):
                rows = slice(part * BLK, (part + 1) * BLK)
                kv[:BLK, rows] = keys[rows].astype(jnp.bfloat16)
            kv[BLK : 2 * BLK, :] = total[base + 4].T.astype(jnp.bfloat16)


def project(chips, heads, xs, own, other, modulation):
    parts, features, inner = own.shape
    count, deep = xs[0].shape
    whole = lambda shape: pl.BlockSpec(shape, lambda k, *_: (0, 0))
    blocks = [
        pl.BlockSpec((parts, deep, inner), lambda k, chips, heads, i=i: (0, chips[2 * k + i], 0))
        for i in range(2)
    ]
    shapes = [(2 * BLK, count), (BLK, count)] * 4
    return pl.pallas_call(
        project_kernel,
        grid_spec=pltpu.PrefetchScalarGridSpec(
            num_scalar_prefetch=2,
            grid=(features // deep // 2,),
            in_specs=[pl.BlockSpec(memory_space=pl.ANY)] * len(xs)
            + [*blocks, *blocks, whole(modulation.shape)],
            out_specs=[whole(s) for s in shapes],
            scratch_shapes=[
                pltpu.VMEM((features // deep, count, deep), jnp.bfloat16),
                pltpu.VMEM((features // deep // 2, count, 2 * deep), jnp.bfloat16),
                pltpu.VMEM((2 * parts * inner // BLK, count, BLK), jnp.float32),
                pltpu.SemaphoreType.DMA((len(xs),)),
            ],
        ),
        out_shape=[jax.ShapeDtypeStruct(s, jnp.bfloat16) for s in shapes],
        compiler_params=pltpu.CompilerParams(vmem_limit_bytes=56 * MIB),
        cost_estimate=pl.CostEstimate(
            flops=4 * parts * inner * features * count,
            bytes_accessed=2 * features * (count + 2 * parts * inner),
            transcendentals=0,
        ),
        name="project",
    )(chips, heads, *xs, own, own, other, other, modulation)


def attend_kernel(factor, unroll, plan, places, counts, first, owner, *refs):
    arrays, outs, rest = refs[: -4 - 8], refs[-4 - 8 : -8], refs[-8:]
    kv, query, asked, scores, tops, totals, sums, arrived = rest
    copies = []
    for kind, index, array, start in plan:
        to = (kv if kind == "kv" else query).at[index]
        rows = to.shape[0]
        copies.append(
            pltpu.make_async_copy(
                arrays[array].at[start : start + rows], to, arrived.at[len(copies)]
            )
        )
    for copy in copies:
        copy.start()
    per_piece = kv.shape[2] // BLK
    rows = len(outs) * per_piece
    tops[...] = jnp.full_like(tops, NEGATIVE)
    totals[...] = jnp.zeros_like(totals)
    sums[...] = jnp.zeros_like(sums)
    for copy in copies:
        copy.wait()
    for index in range(len(outs)):
        for part in range(per_piece):
            asked[index * per_piece + part] = query[index, :, part * BLK : (part + 1) * BLK]

    def find(pair, low, high):
        live = pair < high
        pair = jnp.where(live, pair, low)
        row = owner[pair]
        place = 2 * (pair - first[row])
        wheres = [places[row, place], places[row, place + 1]]
        offsets = [
            jnp.where(live, 0.0, NEGATIVE),
            jnp.where(live & (place + 1 < counts[row]), 0.0, NEGATIVE),
        ]
        return row, wheres, offsets

    def held(where, part):
        start = pl.multiple_of((where & (per_piece - 1)) * BLK, BLK)
        return kv[where >> 2, part * BLK : (part + 1) * BLK, pl.ds(start, BLK)]

    def fold(op, value):
        return op(value.reshape(BLK // 8, 8, BLK), axis=0)

    def rate(low, high, step, _):
        found = []
        for item in range(unroll):
            pair = step * unroll + item
            row, wheres, offsets = find(low + pair, low, high)
            keys = jnp.concatenate([held(where, 0) for where in wheres], axis=0)
            score = jnp.dot(keys, asked[row], preferred_element_type=jnp.float32)
            scores[pair] = score
            best = jnp.maximum(
                fold(jnp.max, score[:BLK]) + offsets[0], fold(jnp.max, score[BLK:]) + offsets[1]
            )
            found.append((row, best))
        for row, best in found:
            tops[row] = jnp.maximum(tops[row], best)
        return 0

    def gather(low, high, step, _):
        found = []
        for item in range(unroll):
            pair = step * unroll + item
            row, wheres, offsets = find(low + pair, low, high)
            top = tops[row][:1]
            score = scores[pair]
            halves = [
                jnp.exp2(score[part * BLK : (part + 1) * BLK] * factor - (top - offsets[part]))
                for part in range(2)
            ]
            total = fold(jnp.sum, halves[0]) + fold(jnp.sum, halves[1])
            weights = jnp.concatenate([half.astype(jnp.bfloat16) for half in halves], axis=0)
            values = jnp.concatenate([held(where, 1) for where in wheres], axis=1)
            summed = jnp.dot(values, weights, preferred_element_type=jnp.float32)
            found.append((row, total, summed))
        for row, total, summed in found:
            totals[row] += total
            sums[row] += summed
        return 0

    for index in range(len(outs)):
        low, high = first[index * per_piece], first[(index + 1) * per_piece]
        steps = (high - low + unroll - 1) // unroll
        lax.fori_loop(0, steps, functools.partial(rate, low, high), 0)
        for row in range(index * per_piece, (index + 1) * per_piece):
            top = jnp.max(tops[row], axis=0, keepdims=True) * factor
            tops[row] = jnp.broadcast_to(top, tops.shape[1:])
        lax.fori_loop(0, steps, functools.partial(gather, low, high), 0)

    for index, out in enumerate(outs):
        for part in range(per_piece):
            row = index * per_piece + part
            total = jnp.sum(totals[row], axis=0, keepdims=True)
            value = (sums[row] / total).T.astype(jnp.bfloat16)
            out[part * BLK : (part + 1) * BLK, :] = value


def pair_lists(counts, most):
    twos = (counts + 1) // 2
    rows = counts.shape[0]
    order = jnp.arange(rows + 1, dtype=jnp.int32)
    first = jnp.sum(jnp.where(order[None, :rows] < order[:, None], twos[None, :], 0), axis=1)
    slots = jnp.arange(rows * most // 2, dtype=jnp.int32)
    return first, jnp.sum(jnp.where(first[None, 1:] <= slots[:, None], 1, 0), axis=1)


def attend(factor, lists, plan, arrays, count):
    rows, most = lists[0].shape
    pieces = most * BLK // count
    asking = rows * BLK // count

    def kernel(*refs):
        attend_kernel(factor, PAIRS, plan, *refs)

    shape = (BLK, count)
    return pl.pallas_call(
        kernel,
        in_specs=[pl.BlockSpec(memory_space=pltpu.SMEM)] * len(lists)
        + [pl.BlockSpec(memory_space=pl.ANY)] * len(arrays),
        out_specs=[pl.BlockSpec(memory_space=pltpu.VMEM)] * asking,
        out_shape=[jax.ShapeDtypeStruct((count, BLK), jnp.bfloat16)] * asking,
        scratch_shapes=[
            pltpu.VMEM((pieces, 2 * BLK, count), jnp.bfloat16),
            pltpu.VMEM((asking, *shape), jnp.bfloat16),
            pltpu.VMEM((rows, BLK, BLK), jnp.bfloat16),
            pltpu.VMEM((rows * most // 2 // asking + PAIRS, 2 * BLK, BLK), jnp.float32),
            pltpu.VMEM((rows, 8, BLK), jnp.float32),
            pltpu.VMEM((rows, 8, BLK), jnp.float32),
            pltpu.VMEM((rows, BLK, BLK), jnp.float32),
            pltpu.SemaphoreType.DMA((len(plan),)),
        ],
        compiler_params=pltpu.CompilerParams(vmem_limit_bytes=32 * MIB),
        cost_estimate=pl.CostEstimate(
            flops=rows * BLK * most * BLK * BLK,
            bytes_accessed=4 * most * BLK * BLK,
            transcendentals=rows * BLK * most * BLK // 4,
        ),
        name="attend",
    )(*lists, *arrays)


def leave_kernel(plan, chips, columns, own, other, *refs):
    heads, outs, ordered, arrived = refs[:4], list(refs[4:-2]), *refs[-2:]
    step = pl.program_id(0)

    @pl.when(step == 0)
    def _():
        copies = [
            pltpu.make_async_copy(head, ordered.at[columns[index]], arrived.at[index])
            for index, head in enumerate(heads)
        ]
        for copy in copies:
            copy.start()
        for copy in copies:
            copy.wait()

    summed = jnp.dot(
        jnp.concatenate([ordered[index] for index in range(4)], axis=1),
        jnp.concatenate([own[...], other[...]], axis=0),
        preferred_element_type=jnp.float32,
    )
    for index, cuts in enumerate(plan):
        mine = [outs.pop(0) for _ in cuts]

        @pl.when(step == index)
        def _():
            for cut, out in zip(cuts, mine):
                out[...] = summed[:, cut[0] : cut[1]].astype(out.dtype)


def leave(chips, columns, weights, heads, plan):
    count = heads[0].shape[0]
    steps = len(plan)
    inner = weights[0].shape[0]
    block = pl.BlockSpec((inner, DEEP), lambda i, chips, columns: (0, chips[i]))
    whole = lambda shape: pl.BlockSpec(shape, lambda i, *_: (0, 0))
    shapes = [(count, cut[1] - cut[0]) for cuts in plan for cut in cuts]

    def kernel(*refs):
        leave_kernel(plan, *refs)

    return pl.pallas_call(
        kernel,
        grid_spec=pltpu.PrefetchScalarGridSpec(
            num_scalar_prefetch=2,
            grid=(steps,),
            in_specs=[block] * 2 + [pl.BlockSpec(memory_space=pl.ANY)] * 4,
            out_specs=[whole(s) for s in shapes],
            scratch_shapes=[
                pltpu.VMEM((4, count, BLK), jnp.bfloat16),
                pltpu.SemaphoreType.DMA((4,)),
            ],
        ),
        out_shape=[jax.ShapeDtypeStruct(s, jnp.bfloat16) for s in shapes],
        compiler_params=pltpu.CompilerParams(vmem_limit_bytes=28 * MIB),
        cost_estimate=pl.CostEstimate(
            flops=4 * steps * DEEP * inner * count,
            bytes_accessed=2 * steps * DEEP * (2 * inner + count),
            transcendentals=0,
        ),
        name="leave",
    )(chips, columns, *weights, *heads)


def arrive_kernel(plan, turned, *refs):
    outs = refs[-len(plan) :]
    at = 0
    for cuts, out in zip(plan, outs):
        share, arrived = refs[at], refs[at + 1 : at + 1 + len(cuts)]
        at += 1 + len(cuts)
        edges = sorted({0, share.shape[1], *[edge for cut in cuts for edge in cut]})
        for low, high in zip(edges, edges[1:]):
            value = share[:, low:high].astype(jnp.float32)
            for (first, last), ref in zip(cuts, arrived):
                if first <= low and high <= last:
                    value += ref[:, low - first : high - first].astype(jnp.float32)
            if turned:
                out[low:high, :] = value.T.astype(out.dtype)
            else:
                out[:, low:high] = value.astype(out.dtype)


def arrive(plan, *arrays, turned=False):
    shapes, at = [], 0
    for cuts in plan:
        shapes.append(arrays[at].shape[::-1] if turned else arrays[at].shape)
        at += 1 + len(cuts)

    def kernel(*refs):
        arrive_kernel(plan, turned, *refs)

    return pl.pallas_call(
        kernel,
        in_specs=[pl.BlockSpec(memory_space=pltpu.VMEM)] * len(arrays),
        out_specs=[pl.BlockSpec(memory_space=pltpu.VMEM)] * len(plan),
        out_shape=[jax.ShapeDtypeStruct(shape, arrays[0].dtype) for shape in shapes],
        compiler_params=pltpu.CompilerParams(vmem_limit_bytes=16 * MIB),
        cost_estimate=pl.CostEstimate(
            flops=0, bytes_accessed=8 * arrays[0].size, transcendentals=0
        ),
        name="arrive",
    )(*arrays)


def gather_tokens(own, first_others, second_others):
    below = shift(own, "z", 1)
    above = shift(own, "z", -1)
    beside = swap(own, "yl")
    below, above, beside = together((below, above, beside), first_others)
    far = shift(below, "z", 1)
    beside_below = swap(below, "yl")
    beside_above = shift(beside, "z", -1)
    far, beside_below, beside_above = together((far, beside_below, beside_above), second_others)
    first, second, third = [slice(*cut) for cut in CUTS]
    parts = [
        swap(far[:, first], "yl"),
        shift(beside_above[:, second], "z", -1),
        shift(beside_below[:, third], "z", 1),
    ]
    places = [(0, 0), (0, -1), (0, 1), (1, 0), (0, 2), (1, -1), (1, 1), (1, 2)]
    return places, [own, below, above, beside, far, beside_below, beside_above, *parts]


def shards(tokens, qkv_weight, out_weight, modulation, block_mask):
    rows, local = tokens.shape
    features = modulation.shape[1]
    heads_here = block_mask.shape[0]
    inner = qkv_weight.shape[2]
    head_size = inner // heads_here
    factor = math.log2(math.e) / math.sqrt(head_size)
    half = rows // 2
    core = lax.axis_index("core")
    frame_x, frame_y = lax.axis_index("x"), lax.axis_index("yh")
    chip_y, chip_z = lax.axis_index("yl"), lax.axis_index("z")
    across = tokens.T

    def chip(dy, dz):
        return ((chip_y + dy) % 2) * 4 + (chip_z + dz) % 4

    def mine_and_given(value, axis):
        size = value.shape[axis] // 2
        mine = lax.dynamic_slice_in_dim(value, core * size, size, axis)
        return mine, lax.dynamic_slice_in_dim(value, (1 - core) * size, size, axis)

    def head_slot(steps):
        head = (frame_x + steps) % 4
        return jnp.where(head // 2 == core, 0, 1), head % 2

    mine, given = mine_and_given(across, 1)
    other = swap(given, "core")
    own = lay(core, mine, other)
    mask_mine, mask_given = mine_and_given(block_mask, 1)
    mask_other = swap(mask_given, "core")

    raw, *_ = lax.optimization_barrier((qkv_weight, own, mask_other))
    other_weight = swap(raw, "core")
    mask_heads = jnp.stack([mask_mine, mask_other])
    mask_rows = []
    for steps in range(4):
        side, slot = head_slot(steps)
        part = lax.dynamic_slice(
            mask_heads, (side, slot, 0, 0), (1, 1, *mask_heads.shape[2:])
        )[0, 0]
        mask_rows.append(shift(part, "x", steps) if steps else part)
    keep = jnp.concatenate(mask_rows, axis=0) != 0
    blocks = jnp.arange(keep.shape[1], dtype=jnp.int32)
    per_core = half // BLK
    piece, inside = blocks // per_core, blocks % per_core
    from_core, from_y = core ^ (piece // 8), frame_y ^ (piece // 4 % 2)
    from_x = (frame_x - piece % 4) % 4
    origin = (from_y * 4 + from_x) * (2 * per_core) + from_core * per_core + inside
    same = origin[:, None] == blocks[None, :]
    keep = jnp.sum(jnp.where(same[None] & keep[:, None, :], 1, 0), axis=2)
    counts = jnp.sum(keep, axis=1)
    earlier = blocks[None, :] < blocks[:, None]
    rank = jnp.sum(jnp.where(earlier[None], keep[:, None, :], 0), axis=2)
    chosen = (keep[:, None, :] != 0) & (rank[:, None, :] == blocks[None, :, None])
    listed = jnp.sum(jnp.where(chosen, blocks[None, None, :], 0), axis=2)
    lists = (listed, counts, *pair_lists(counts, listed.shape[1]))
    places, xs = gather_tokens(own, (), mask_rows[1:])

    chips = jnp.stack([chip(*place) for place in places]).astype(jnp.int32)
    slots = [head_slot(steps) for steps in range(4)]
    bases = jnp.stack([side * 3 * heads_here + slot for side, slot in slots]).astype(jnp.int32)
    made = project(chips, bases, xs, qkv_weight, other_weight, modulation)
    kv, queries = made[::2], made[1::2]
    one, three = shift(kv[1], "x", 1), shift(kv[3], "x", 3)
    away_kv = swap(kv[0], "yh")
    q_one, q_three = shift(queries[1], "x", 1), shift(queries[3], "x", 3)
    one, three = together((one, three), (away_kv, q_one, q_three))
    both = jnp.concatenate([one, three], axis=0)
    away_both = swap(both, "yh")
    kv_two, q_two = together((kv[2], queries[2]), (one,))
    two, q_two = shift(kv_two, "x", 2), shift(q_two, "x", 2)
    near = swap(jnp.concatenate([kv[0], both], axis=0), "core")
    away_kv_other = swap(away_kv, "core")
    (two,) = together((two,), (away_both, q_two, *lists, near, away_kv_other))
    away_two = swap(two, "yh")
    (out_own,) = together((out_weight,), (away_two,))
    leaving = out_weight, swap(out_own, "core")
    arrays = [kv[0], both, two, away_kv, away_both, away_two, near, swap(two, "core")]
    arrays += [away_kv_other, swap(away_both, "core"), swap(away_two, "core")]
    arrays += [queries[0], q_one, q_two, q_three]
    step = 2 * BLK
    plan = []
    for index, array in ((0, 0), (4, 3), (12, 8)):
        plan += [("kv", index, array, 0), ("kv", index + 1, array + 1, 0)]
        plan += [("kv", index + 3, array + 1, step), ("kv", index + 2, array + 2, 0)]
    plan += [("kv", 8, 6, 0), ("kv", 9, 6, step), ("kv", 11, 6, 2 * step), ("kv", 10, 7, 0)]
    plan += [("q", index, 11 + index, 0) for index in range(4)]
    heads = attend(factor, lists, plan, arrays, half)
    heads = [heads[0]] + [shift(heads[steps], "x", -steps) for steps in (1, 2, 3)]

    columns = jnp.stack([side * heads_here + slot for side, slot in slots]).astype(jnp.int32)
    whole = CUTS[0][0], CUTS[-1][1]

    def shares(targets, cuts, heads):
        chips = jnp.stack([chip(*target) for target in targets]).astype(jnp.int32)
        return leave(chips, columns, leaving, heads, [cuts] * len(targets))

    parts = shares([(1, 2)], CUTS, heads)
    middle = [(0, 2), (1, 1), (1, -1)]
    share = dict(zip(middle, shares(middle, (whole,), heads)))
    first = swap(parts[0], "yl")
    second = shift(parts[1], "z", 1)
    third = shift(parts[2], "z", -1)
    heads = together(heads, (first, second, third))
    near = [(0, -1), (0, 1), (1, 0), (0, 0)]
    share |= dict(zip(near, shares(near, (whole,), heads)))
    down, up, side = arrive(
        [(CUTS[0],), (CUTS[1],), (CUTS[2],)],
        *[share[0, 2], first, share[1, 1], second, share[1, -1], third],
    )
    down, up, side = shift(down, "z", -1), shift(up, "z", 1), swap(side, "yl")
    down, side = arrive(
        [(whole, whole), (whole,)], share[0, -1], down, side, share[1, 0], up
    )
    down, up, side = shift(down, "z", -1), shift(share[0, 1], "z", 1), swap(side, "yl")
    (summed,) = arrive([(whole, whole, whole)], share[0, 0], down, up, side, turned=True)

    kept, given = mine_and_given(summed, 0)
    other = swap(given, "core")
    projected = jnp.concatenate(
        [jnp.where(core == 0, kept, other), jnp.where(core == 0, other, kept)], axis=1
    ).astype(jnp.float32)
    start = lax.axis_index(HEAD) * local
    gate = lax.dynamic_slice_in_dim(modulation, start, local, 1)[2][:, None]
    return (across.astype(jnp.float32) + gate * projected).astype(jnp.bfloat16).T


def solution(mesh):
    fine = Mesh(mesh.devices.reshape(2, 4, 2, 4, 2), ("yh", "x", "yl", "z", "core"))
    placed = (
        P(FRAME, HEAD),
        P(None, None, HEAD),
        P(HEAD, None),
        P(),
        P(HEAD, FRAME, None),
    )
    return jax.shard_map(
        shards, mesh=fine, in_specs=placed, out_specs=P(FRAME, HEAD), check_vma=False
    )
```

```python
import functools
import math

import jax
import jax.numpy as jnp
from jax import lax
from jax.experimental import pallas as pl
from jax.experimental.pallas import tpu as pltpu
from jax.sharding import Mesh
from jax.sharding import PartitionSpec as P

BLK = 128
EPSILON = 1e-06
NEGATIVE = -1e30
FRAME = ("yh", "x")
HEAD = ("yl", "z", "core")
MIB = 1 << 20
PAIRS = 12
CUTS = ((0, 256), (256, 512), (512, 640))


DEEP = CUTS[-1][1]


def shift(value, axis, steps):
    count = lax.axis_size(axis)
    return lax.ppermute(value, axis, [(i, (i + steps) % count) for i in range(count)])


def swap(value, axis):
    return shift(value, axis, 1)


def lay_kernel(core, mine, other, out):
    first = core[0] == 0
    mine, other = mine[...].astype(jnp.float32), other[...].astype(jnp.float32)
    half = mine.shape[0]
    upper = jnp.where(first, mine, other)
    lower = jnp.where(first, other, mine)
    out[...] = jnp.concatenate([upper, lower], axis=0).T.astype(out.dtype)


def lay(core, mine, other):
    half, count = mine.shape
    return pl.pallas_call(
        lay_kernel,
        in_specs=[pl.BlockSpec(memory_space=pltpu.SMEM)]
        + [pl.BlockSpec(memory_space=pltpu.VMEM)] * 2,
        out_specs=pl.BlockSpec(memory_space=pltpu.VMEM),
        out_shape=jax.ShapeDtypeStruct((count, 2 * half), mine.dtype),
        compiler_params=pltpu.CompilerParams(vmem_limit_bytes=12 * MIB),
        cost_estimate=pl.CostEstimate(
            flops=0, bytes_accessed=8 * half * count, transcendentals=0
        ),
        name="lay",
    )(jnp.reshape(core, (1,)).astype(jnp.int32), mine, other)


def together(arrays, others=()):
    return lax.optimization_barrier((*arrays, *others))[: len(arrays)]


ROWS = 64
NEAR = {1: 4, 3: 5}


def project_kernel(chips, heads, *refs):
    xs, weights, modulation, rest = refs[:10], refs[10:14], refs[14], refs[15:]
    outs, (held_x, normed, total, arrived) = rest[:-4], rest[-4:]
    step = pl.program_id(0)
    features = 8 * DEEP
    count = normed.shape[1]
    tiles = [(piece, at) for piece in range(8) for at in range(0, DEEP, BLK)]

    @pl.when(step == 0)
    def _():
        places = [held_x.at[piece] for piece in range(7)]
        places += [held_x.at[7, :, cut[0] : cut[1]] for cut in CUTS]
        copies = [
            pltpu.make_async_copy(x, place, arrived.at[index])
            for index, (x, place) in enumerate(zip(xs, places))
        ]
        for copy in copies:
            copy.start()
        for copy in copies:
            copy.wait()
        total[...] = jnp.zeros_like(total)

        def norm(i, _):
            rows = pl.ds(pl.multiple_of(i * ROWS, ROWS), ROWS)

            def load(piece, at):
                return held_x[piece, rows, at : at + BLK].astype(jnp.float32)

            summed = jnp.zeros((ROWS, BLK), jnp.float32)
            for tile in tiles:
                summed = summed + load(*tile)
            center = jnp.sum(summed, axis=1, keepdims=True) / features
            center = jnp.broadcast_to(center, (ROWS, BLK))
            summed = jnp.zeros((ROWS, BLK), jnp.float32)
            for tile in tiles:
                summed = summed + jnp.square(load(*tile) - center)
            spread = jnp.sum(summed, axis=1, keepdims=True) / features
            rate = jnp.broadcast_to(lax.rsqrt(spread + EPSILON), (ROWS, BLK))
            for piece, at in tiles:
                place = pl.ds(pl.multiple_of(chips[piece] * DEEP + at, BLK), BLK)
                gain = 1.0 + modulation[1:2, place]
                value = (load(piece, at) - center) * rate * gain + modulation[0:1, place]
                column = piece % 2 * DEEP + at
                normed[piece // 2, rows, column : column + BLK] = value.astype(jnp.bfloat16)
            return 0

        lax.fori_loop(0, count // ROWS, norm, 0)

    held = normed[step]
    for side in range(2):
        for part in range(3):
            weight = jnp.concatenate([w[part] for w in weights[2 * side : 2 * side + 2]], axis=0)
            made = jnp.dot(held, weight, preferred_element_type=jnp.float32)
            for slot in range(2):
                total[side * 6 + part * 2 + slot] += made[:, slot * BLK : (slot + 1) * BLK]

    @pl.when(step == pl.num_programs(0) - 1)
    def _():
        for index in range(4):
            if index % 2:
                kv, q = outs[NEAR[index]], outs[NEAR[index]].at[2 * BLK :]
            else:
                kv, q = outs[index : index + 2]
            base = heads[index]
            q[...] = total[base].T.astype(jnp.bfloat16)
            keys = total[base + 2]
            for part in range(count // BLK):
                rows = slice(part * BLK, (part + 1) * BLK)
                kv[:BLK, rows] = keys[rows].astype(jnp.bfloat16)
            kv[BLK : 2 * BLK, :] = total[base + 4].T.astype(jnp.bfloat16)


def project(chips, heads, xs, own, other, modulation):
    parts, features, inner = own.shape
    count, deep = xs[0].shape
    whole = lambda shape: pl.BlockSpec(shape, lambda k, *_: (0, 0))
    blocks = [
        pl.BlockSpec((parts, deep, inner), lambda k, chips, heads, i=i: (0, chips[2 * k + i], 0))
        for i in range(2)
    ]
    shapes = [(2 * BLK, count), (BLK, count)] * 2 + [(3 * BLK, count)] * 2
    return pl.pallas_call(
        project_kernel,
        grid_spec=pltpu.PrefetchScalarGridSpec(
            num_scalar_prefetch=2,
            grid=(features // deep // 2,),
            in_specs=[pl.BlockSpec(memory_space=pl.ANY)] * len(xs)
            + [*blocks, *blocks, whole(modulation.shape)],
            out_specs=[whole(s) for s in shapes],
            scratch_shapes=[
                pltpu.VMEM((features // deep, count, deep), jnp.bfloat16),
                pltpu.VMEM((features // deep // 2, count, 2 * deep), jnp.bfloat16),
                pltpu.VMEM((2 * parts * inner // BLK, count, BLK), jnp.float32),
                pltpu.SemaphoreType.DMA((len(xs),)),
            ],
        ),
        out_shape=[jax.ShapeDtypeStruct(s, jnp.bfloat16) for s in shapes],
        compiler_params=pltpu.CompilerParams(vmem_limit_bytes=56 * MIB),
        cost_estimate=pl.CostEstimate(
            flops=4 * parts * inner * features * count,
            bytes_accessed=2 * features * (count + 2 * parts * inner),
            transcendentals=0,
        ),
        name="project",
    )(chips, heads, *xs, own, own, other, other, modulation)


def attend_kernel(factor, unroll, plan, places, counts, first, owner, *refs):
    arrays, outs, rest = refs[: -4 - 8], refs[-4 - 8 : -8], refs[-8:]
    kv, query, asked, scores, tops, totals, sums, arrived = rest
    copies = []
    for kind, index, array, start in plan:
        to = (kv if kind == "kv" else query).at[index]
        rows = to.shape[0]
        copies.append(
            pltpu.make_async_copy(
                arrays[array].at[start : start + rows], to, arrived.at[len(copies)]
            )
        )
    for copy in copies:
        copy.start()
    per_piece = kv.shape[2] // BLK
    rows = len(outs) * per_piece
    tops[...] = jnp.full_like(tops, NEGATIVE)
    totals[...] = jnp.zeros_like(totals)
    sums[...] = jnp.zeros_like(sums)
    for copy in copies:
        copy.wait()
    for index in range(len(outs)):
        for part in range(per_piece):
            asked[index * per_piece + part] = query[index, :, part * BLK : (part + 1) * BLK]

    def find(pair, low, high):
        live = pair < high
        pair = jnp.where(live, pair, low)
        row = owner[pair]
        place = 2 * (pair - first[row])
        wheres = [places[row, place], places[row, place + 1]]
        offsets = [
            jnp.where(live, 0.0, NEGATIVE),
            jnp.where(live & (place + 1 < counts[row]), 0.0, NEGATIVE),
        ]
        return row, wheres, offsets

    def held(where, part):
        start = pl.multiple_of((where & (per_piece - 1)) * BLK, BLK)
        return kv[where >> 2, part * BLK : (part + 1) * BLK, pl.ds(start, BLK)]

    def fold(op, value):
        return op(value.reshape(BLK // 8, 8, BLK), axis=0)

    def rate(low, high, step, _):
        found = []
        for item in range(unroll):
            pair = step * unroll + item
            row, wheres, offsets = find(low + pair, low, high)
            keys = jnp.concatenate([held(where, 0) for where in wheres], axis=0)
            score = jnp.dot(keys, asked[row], preferred_element_type=jnp.float32)
            scores[pair] = score
            best = jnp.maximum(
                fold(jnp.max, score[:BLK]) + offsets[0], fold(jnp.max, score[BLK:]) + offsets[1]
            )
            found.append((row, best))
        for row, best in found:
            tops[row] = jnp.maximum(tops[row], best)
        return 0

    def gather(low, high, step, _):
        found = []
        for item in range(unroll):
            pair = step * unroll + item
            row, wheres, offsets = find(low + pair, low, high)
            top = tops[row][:1]
            score = scores[pair]
            halves = [
                jnp.exp2(score[part * BLK : (part + 1) * BLK] * factor - (top - offsets[part]))
                for part in range(2)
            ]
            total = fold(jnp.sum, halves[0]) + fold(jnp.sum, halves[1])
            weights = jnp.concatenate([half.astype(jnp.bfloat16) for half in halves], axis=0)
            values = jnp.concatenate([held(where, 1) for where in wheres], axis=1)
            summed = jnp.dot(values, weights, preferred_element_type=jnp.float32)
            found.append((row, total, summed))
        for row, total, summed in found:
            totals[row] += total
            sums[row] += summed
        return 0

    for index in range(len(outs)):
        low, high = first[index * per_piece], first[(index + 1) * per_piece]
        steps = (high - low + unroll - 1) // unroll
        lax.fori_loop(0, steps, functools.partial(rate, low, high), 0)
        for row in range(index * per_piece, (index + 1) * per_piece):
            top = jnp.max(tops[row], axis=0, keepdims=True) * factor
            tops[row] = jnp.broadcast_to(top, tops.shape[1:])
        lax.fori_loop(0, steps, functools.partial(gather, low, high), 0)

    for index, out in enumerate(outs):
        for part in range(per_piece):
            row = index * per_piece + part
            total = jnp.sum(totals[row], axis=0, keepdims=True)
            value = (sums[row] / total).T.astype(jnp.bfloat16)
            out[part * BLK : (part + 1) * BLK, :] = value


def pair_lists(counts, most):
    twos = (counts + 1) // 2
    rows = counts.shape[0]
    order = jnp.arange(rows + 1, dtype=jnp.int32)
    first = jnp.sum(jnp.where(order[None, :rows] < order[:, None], twos[None, :], 0), axis=1)
    slots = jnp.arange(rows * most // 2, dtype=jnp.int32)
    return first, jnp.sum(jnp.where(first[None, 1:] <= slots[:, None], 1, 0), axis=1)


def attend(factor, lists, plan, arrays, count):
    rows, most = lists[0].shape
    pieces = most * BLK // count
    asking = rows * BLK // count

    def kernel(*refs):
        attend_kernel(factor, PAIRS, plan, *refs)

    shape = (BLK, count)
    return pl.pallas_call(
        kernel,
        in_specs=[pl.BlockSpec(memory_space=pltpu.SMEM)] * len(lists)
        + [pl.BlockSpec(memory_space=pl.ANY)] * len(arrays),
        out_specs=[pl.BlockSpec(memory_space=pltpu.VMEM)] * asking,
        out_shape=[jax.ShapeDtypeStruct((count, BLK), jnp.bfloat16)] * asking,
        scratch_shapes=[
            pltpu.VMEM((pieces, 2 * BLK, count), jnp.bfloat16),
            pltpu.VMEM((asking, *shape), jnp.bfloat16),
            pltpu.VMEM((rows, BLK, BLK), jnp.bfloat16),
            pltpu.VMEM((rows * most // 2 // asking + PAIRS, 2 * BLK, BLK), jnp.float32),
            pltpu.VMEM((rows, 8, BLK), jnp.float32),
            pltpu.VMEM((rows, 8, BLK), jnp.float32),
            pltpu.VMEM((rows, BLK, BLK), jnp.float32),
            pltpu.SemaphoreType.DMA((len(plan),)),
        ],
        compiler_params=pltpu.CompilerParams(vmem_limit_bytes=32 * MIB),
        cost_estimate=pl.CostEstimate(
            flops=rows * BLK * most * BLK * BLK,
            bytes_accessed=4 * most * BLK * BLK,
            transcendentals=rows * BLK * most * BLK // 4,
        ),
        name="attend",
    )(*lists, *arrays)


def leave_kernel(plan, chips, columns, own, other, *refs):
    heads, outs, ordered, arrived = refs[:4], list(refs[4:-2]), *refs[-2:]
    step = pl.program_id(0)

    @pl.when(step == 0)
    def _():
        copies = [
            pltpu.make_async_copy(head, ordered.at[columns[index]], arrived.at[index])
            for index, head in enumerate(heads)
        ]
        for copy in copies:
            copy.start()
        for copy in copies:
            copy.wait()

    summed = jnp.dot(
        jnp.concatenate([ordered[index] for index in range(4)], axis=1),
        jnp.concatenate([own[...], other[...]], axis=0),
        preferred_element_type=jnp.float32,
    )
    for index, cuts in enumerate(plan):
        mine = [outs.pop(0) for _ in cuts]

        @pl.when(step == index)
        def _():
            for cut, out in zip(cuts, mine):
                out[...] = summed[:, cut[0] : cut[1]].astype(out.dtype)


def leave(chips, columns, weights, heads, plan):
    count = heads[0].shape[0]
    steps = len(plan)
    inner = weights[0].shape[0]
    block = pl.BlockSpec((inner, DEEP), lambda i, chips, columns: (0, chips[i]))
    whole = lambda shape: pl.BlockSpec(shape, lambda i, *_: (0, 0))
    shapes = [(count, cut[1] - cut[0]) for cuts in plan for cut in cuts]

    def kernel(*refs):
        leave_kernel(plan, *refs)

    return pl.pallas_call(
        kernel,
        grid_spec=pltpu.PrefetchScalarGridSpec(
            num_scalar_prefetch=2,
            grid=(steps,),
            in_specs=[block] * 2 + [pl.BlockSpec(memory_space=pl.ANY)] * 4,
            out_specs=[whole(s) for s in shapes],
            scratch_shapes=[
                pltpu.VMEM((4, count, BLK), jnp.bfloat16),
                pltpu.SemaphoreType.DMA((4,)),
            ],
        ),
        out_shape=[jax.ShapeDtypeStruct(s, jnp.bfloat16) for s in shapes],
        compiler_params=pltpu.CompilerParams(vmem_limit_bytes=28 * MIB),
        cost_estimate=pl.CostEstimate(
            flops=4 * steps * DEEP * inner * count,
            bytes_accessed=2 * steps * DEEP * (2 * inner + count),
            transcendentals=0,
        ),
        name="leave",
    )(chips, columns, *weights, *heads)


def arrive_kernel(plan, turned, *refs):
    outs = refs[-len(plan) :]
    at = 0
    for cuts, out in zip(plan, outs):
        share, arrived = refs[at], refs[at + 1 : at + 1 + len(cuts)]
        at += 1 + len(cuts)
        edges = sorted({0, share.shape[1], *[edge for cut in cuts for edge in cut]})
        for low, high in zip(edges, edges[1:]):
            value = share[:, low:high].astype(jnp.float32)
            for (first, last), ref in zip(cuts, arrived):
                if first <= low and high <= last:
                    value += ref[:, low - first : high - first].astype(jnp.float32)
            if turned:
                out[low:high, :] = value.T.astype(out.dtype)
            else:
                out[:, low:high] = value.astype(out.dtype)


def arrive(plan, *arrays, turned=False):
    shapes, at = [], 0
    for cuts in plan:
        shapes.append(arrays[at].shape[::-1] if turned else arrays[at].shape)
        at += 1 + len(cuts)

    def kernel(*refs):
        arrive_kernel(plan, turned, *refs)

    return pl.pallas_call(
        kernel,
        in_specs=[pl.BlockSpec(memory_space=pltpu.VMEM)] * len(arrays),
        out_specs=[pl.BlockSpec(memory_space=pltpu.VMEM)] * len(plan),
        out_shape=[jax.ShapeDtypeStruct(shape, arrays[0].dtype) for shape in shapes],
        compiler_params=pltpu.CompilerParams(vmem_limit_bytes=16 * MIB),
        cost_estimate=pl.CostEstimate(
            flops=0, bytes_accessed=8 * arrays[0].size, transcendentals=0
        ),
        name="arrive",
    )(*arrays)


def gather_tokens(own, first_others, second_others):
    below = shift(own, "z", 1)
    above = shift(own, "z", -1)
    beside = swap(own, "yl")
    below, above, beside = together((below, above, beside), first_others)
    far = shift(below, "z", 1)
    beside_below = swap(below, "yl")
    beside_above = shift(beside, "z", -1)
    far, beside_below, beside_above = together((far, beside_below, beside_above), second_others)
    first, second, third = [slice(*cut) for cut in CUTS]
    parts = [
        swap(far[:, first], "yl"),
        shift(beside_above[:, second], "z", -1),
        shift(beside_below[:, third], "z", 1),
    ]
    places = [(0, 0), (0, -1), (0, 1), (1, 0), (0, 2), (1, -1), (1, 1), (1, 2)]
    return places, [own, below, above, beside, far, beside_below, beside_above, *parts]


def shards(tokens, qkv_weight, out_weight, modulation, block_mask):
    rows, local = tokens.shape
    features = modulation.shape[1]
    heads_here = block_mask.shape[0]
    inner = qkv_weight.shape[2]
    head_size = inner // heads_here
    factor = math.log2(math.e) / math.sqrt(head_size)
    half = rows // 2
    core = lax.axis_index("core")
    frame_x, frame_y = lax.axis_index("x"), lax.axis_index("yh")
    chip_y, chip_z = lax.axis_index("yl"), lax.axis_index("z")
    across = tokens.T

    def chip(dy, dz):
        return ((chip_y + dy) % 2) * 4 + (chip_z + dz) % 4

    def mine_and_given(value, axis):
        size = value.shape[axis] // 2
        mine = lax.dynamic_slice_in_dim(value, core * size, size, axis)
        return mine, lax.dynamic_slice_in_dim(value, (1 - core) * size, size, axis)

    def head_slot(steps):
        head = (frame_x + steps) % 4
        return jnp.where(head // 2 == core, 0, 1), head % 2

    mine, given = mine_and_given(across, 1)
    other = swap(given, "core")
    own = lay(core, mine, other)
    mask_mine, mask_given = mine_and_given(block_mask, 1)
    mask_other = swap(mask_given, "core")

    raw, *_ = lax.optimization_barrier((qkv_weight, own, mask_other))
    other_weight = swap(raw, "core")
    mask_heads = jnp.stack([mask_mine, mask_other])
    mask_rows = []
    for steps in range(4):
        side, slot = head_slot(steps)
        part = lax.dynamic_slice(
            mask_heads, (side, slot, 0, 0), (1, 1, *mask_heads.shape[2:])
        )[0, 0]
        mask_rows.append(shift(part, "x", steps) if steps else part)
    keep = jnp.concatenate(mask_rows, axis=0) != 0
    blocks = jnp.arange(keep.shape[1], dtype=jnp.int32)
    per_core = half // BLK
    piece, inside = blocks // per_core, blocks % per_core
    from_core, from_y = core ^ (piece // 8), frame_y ^ (piece // 4 % 2)
    from_x = (frame_x - piece % 4) % 4
    origin = (from_y * 4 + from_x) * (2 * per_core) + from_core * per_core + inside
    same = origin[:, None] == blocks[None, :]
    keep = jnp.sum(jnp.where(same[None] & keep[:, None, :], 1, 0), axis=2)
    counts = jnp.sum(keep, axis=1)
    earlier = blocks[None, :] < blocks[:, None]
    rank = jnp.sum(jnp.where(earlier[None], keep[:, None, :], 0), axis=2)
    chosen = (keep[:, None, :] != 0) & (rank[:, None, :] == blocks[None, :, None])
    listed = jnp.sum(jnp.where(chosen, blocks[None, None, :], 0), axis=2)
    lists = (listed, counts, *pair_lists(counts, listed.shape[1]))
    places, xs = gather_tokens(own, (), mask_rows[1:])

    chips = jnp.stack([chip(*place) for place in places]).astype(jnp.int32)
    slots = [head_slot(steps) for steps in range(4)]
    bases = jnp.stack([side * 3 * heads_here + slot for side, slot in slots]).astype(jnp.int32)
    made = project(chips, bases, xs, qkv_weight, other_weight, modulation)
    kv, query, kv_two, q_two, *packed = made
    one, three = shift(packed[0], "x", 1), shift(packed[1], "x", 3)
    away_kv = swap(kv, "yh")
    one, three = together((one, three), (away_kv,))
    both = jnp.concatenate([one[: 2 * BLK], three[: 2 * BLK]], axis=0)
    away_both = swap(both, "yh")
    kv_two, q_two = together((kv_two, q_two), (one,))
    two, q_two = shift(kv_two, "x", 2), shift(q_two, "x", 2)
    away_kv_other = swap(away_kv, "core")
    two, kv, both = together((two, kv, both), (away_both, q_two, *lists, away_kv_other))
    away_two = swap(two, "yh")
    near = swap(jnp.concatenate([kv, both], axis=0), "core")
    arrays = [kv, both, two, away_kv, away_both, away_two, near, swap(two, "core")]
    arrays += [away_kv_other, swap(away_both, "core"), swap(away_two, "core")]
    arrays += [query, one, q_two, three]
    step = 2 * BLK
    plan = []
    for index, array in ((0, 0), (4, 3), (12, 8)):
        plan += [("kv", index, array, 0), ("kv", index + 1, array + 1, 0)]
        plan += [("kv", index + 3, array + 1, step), ("kv", index + 2, array + 2, 0)]
    plan += [("kv", 8, 6, 0), ("kv", 9, 6, step), ("kv", 11, 6, 2 * step), ("kv", 10, 7, 0)]
    plan += [("q", index, 11 + index, index % 2 * step) for index in range(4)]
    heads = attend(factor, lists, plan, arrays, half)
    (out_own,) = together((out_weight,), (heads[0],))
    leaving = out_weight, swap(out_own, "core")
    heads = [heads[0]] + [shift(heads[steps], "x", -steps) for steps in (1, 2, 3)]

    columns = jnp.stack([side * heads_here + slot for side, slot in slots]).astype(jnp.int32)
    whole = CUTS[0][0], CUTS[-1][1]

    def shares(targets, cuts, heads):
        chips = jnp.stack([chip(*target) for target in targets]).astype(jnp.int32)
        return leave(chips, columns, leaving, heads, [cuts] * len(targets))

    parts = shares([(1, 2)], CUTS, heads)
    middle = [(0, 2), (1, 1), (1, -1)]
    share = dict(zip(middle, shares(middle, (whole,), heads)))
    first = swap(parts[0], "yl")
    second = shift(parts[1], "z", 1)
    third = shift(parts[2], "z", -1)
    heads = together(heads, (first, second, third))
    near = [(0, -1), (0, 1), (1, 0), (0, 0)]
    share |= dict(zip(near, shares(near, (whole,), heads)))
    down, up, side = arrive(
        [(CUTS[0],), (CUTS[1],), (CUTS[2],)],
        *[share[0, 2], first, share[1, 1], second, share[1, -1], third],
    )
    down, up, side = shift(down, "z", -1), shift(up, "z", 1), swap(side, "yl")
    down, side = arrive(
        [(whole, whole), (whole,)], share[0, -1], down, side, share[1, 0], up
    )
    down, up, side = shift(down, "z", -1), shift(share[0, 1], "z", 1), swap(side, "yl")
    (summed,) = arrive([(whole, whole, whole)], share[0, 0], down, up, side, turned=True)

    kept, given = mine_and_given(summed, 0)
    other = swap(given, "core")
    projected = jnp.concatenate(
        [jnp.where(core == 0, kept, other), jnp.where(core == 0, other, kept)], axis=1
    ).astype(jnp.float32)
    start = lax.axis_index(HEAD) * local
    gate = lax.dynamic_slice_in_dim(modulation, start, local, 1)[2][:, None]
    return (across.astype(jnp.float32) + gate * projected).astype(jnp.bfloat16).T


def solution(mesh):
    fine = Mesh(mesh.devices.reshape(2, 4, 2, 4, 2), ("yh", "x", "yl", "z", "core"))
    placed = (
        P(FRAME, HEAD),
        P(None, None, HEAD),
        P(HEAD, None),
        P(),
        P(HEAD, FRAME, None),
    )
    return jax.shard_map(
        shards, mesh=fine, in_specs=placed, out_specs=P(FRAME, HEAD), check_vma=False
    )
```

```python
import functools
import math

import jax
import jax.numpy as jnp
from jax import lax
from jax.experimental import pallas as pl
from jax.experimental.pallas import tpu as pltpu
from jax.sharding import Mesh
from jax.sharding import PartitionSpec as P

BLK = 128
EPSILON = 1e-06
NEGATIVE = -1e30
FRAME = ("yh", "x")
HEAD = ("yl", "z", "core")
MIB = 1 << 20
PAIRS = 12
CUTS = ((0, 256), (256, 512), (512, 640))


DEEP = CUTS[-1][1]


def shift(value, axis, steps):
    count = lax.axis_size(axis)
    return lax.ppermute(value, axis, [(i, (i + steps) % count) for i in range(count)])


def swap(value, axis):
    return shift(value, axis, 1)


def lay_kernel(core, mine, other, out):
    first = core[0] == 0
    mine, other = mine[...].astype(jnp.float32), other[...].astype(jnp.float32)
    half = mine.shape[0]
    upper = jnp.where(first, mine, other)
    lower = jnp.where(first, other, mine)
    out[...] = jnp.concatenate([upper, lower], axis=0).T.astype(out.dtype)


def lay(core, mine, other):
    half, count = mine.shape
    return pl.pallas_call(
        lay_kernel,
        in_specs=[pl.BlockSpec(memory_space=pltpu.SMEM)]
        + [pl.BlockSpec(memory_space=pltpu.VMEM)] * 2,
        out_specs=pl.BlockSpec(memory_space=pltpu.VMEM),
        out_shape=jax.ShapeDtypeStruct((count, 2 * half), mine.dtype),
        compiler_params=pltpu.CompilerParams(vmem_limit_bytes=12 * MIB),
        cost_estimate=pl.CostEstimate(
            flops=0, bytes_accessed=8 * half * count, transcendentals=0
        ),
        name="lay",
    )(jnp.reshape(core, (1,)).astype(jnp.int32), mine, other)


def together(arrays, others=()):
    return lax.optimization_barrier((*arrays, *others))[: len(arrays)]


ROWS = 64
NEAR = {1: 4, 3: 5}


def project_kernel(chips, heads, *refs):
    xs, weights, modulation, rest = refs[:10], refs[10:12], refs[12], refs[13:]
    outs, (held_x, held_weight, normed, total, arrived, loaded) = rest[:-6], rest[-6:]
    count, features = normed.shape
    tiles = [(piece, at) for piece in range(8) for at in range(0, DEEP, BLK)]

    places = [held_x.at[piece] for piece in range(7)]
    places += [held_x.at[7, :, cut[0] : cut[1]] for cut in CUTS]
    copies = [
        pltpu.make_async_copy(x, place, arrived.at[index])
        for index, (x, place) in enumerate(zip(xs, places))
    ]
    for copy in copies:
        copy.start()
    loads = []
    for side, weight in enumerate(weights):
        for piece in range(8):
            rows = pl.ds(pl.multiple_of(chips[piece] * DEEP, BLK), DEEP)
            loads.append(
                pltpu.make_async_copy(
                    weight.at[:, rows, :],
                    held_weight.at[side, :, piece * DEEP : (piece + 1) * DEEP, :],
                    loaded.at[side * 8 + piece],
                )
            )
    for copy in copies:
        copy.wait()
    for copy in loads:
        copy.start()

    def norm(i, _):
        rows = pl.ds(pl.multiple_of(i * ROWS, ROWS), ROWS)

        def load(piece, at):
            return held_x[piece, rows, at : at + BLK].astype(jnp.float32)

        summed = jnp.zeros((ROWS, BLK), jnp.float32)
        for tile in tiles:
            summed = summed + load(*tile)
        center = jnp.sum(summed, axis=1, keepdims=True) / features
        center = jnp.broadcast_to(center, (ROWS, BLK))
        summed = jnp.zeros((ROWS, BLK), jnp.float32)
        for tile in tiles:
            summed = summed + jnp.square(load(*tile) - center)
        spread = jnp.sum(summed, axis=1, keepdims=True) / features
        rate = jnp.broadcast_to(lax.rsqrt(spread + EPSILON), (ROWS, BLK))
        for piece, at in tiles:
            place = pl.ds(pl.multiple_of(chips[piece] * DEEP + at, BLK), BLK)
            gain = 1.0 + modulation[1:2, place]
            value = (load(piece, at) - center) * rate * gain + modulation[0:1, place]
            column = piece * DEEP + at
            normed[rows, column : column + BLK] = value.astype(jnp.bfloat16)
        return 0

    lax.fori_loop(0, count // ROWS, norm, 0)
    for copy in loads:
        copy.wait()
    for side in range(2):
        for part in range(3):
            made = jnp.dot(
                normed[...], held_weight[side, part], preferred_element_type=jnp.float32
            )
            for slot in range(2):
                total[side * 6 + part * 2 + slot] = made[:, slot * BLK : (slot + 1) * BLK]
    for index in range(4):
        if index % 2:
            kv, q = outs[NEAR[index]], outs[NEAR[index]].at[2 * BLK :]
        else:
            kv, q = outs[index : index + 2]
        base = heads[index]
        q[...] = total[base].T.astype(jnp.bfloat16)
        for part in range(count // BLK):
            rows = slice(part * BLK, (part + 1) * BLK)
            kv[:BLK, rows] = total[base + 2, rows].astype(jnp.bfloat16)
        kv[BLK : 2 * BLK, :] = total[base + 4].T.astype(jnp.bfloat16)


def project(chips, heads, xs, own, other, modulation):
    parts, features, inner = own.shape
    count, deep = xs[0].shape
    shapes = [(2 * BLK, count), (BLK, count)] * 2 + [(3 * BLK, count)] * 2
    return pl.pallas_call(
        project_kernel,
        in_specs=[pl.BlockSpec(memory_space=pltpu.SMEM)] * 2
        + [pl.BlockSpec(memory_space=pl.ANY)] * (len(xs) + 2)
        + [pl.BlockSpec(memory_space=pltpu.VMEM)],
        out_specs=[pl.BlockSpec(memory_space=pltpu.VMEM)] * len(shapes),
        scratch_shapes=[
            pltpu.VMEM((features // deep, count, deep), jnp.bfloat16),
            pltpu.VMEM((2, parts, features, inner), jnp.bfloat16),
            pltpu.VMEM((count, features), jnp.bfloat16),
            pltpu.VMEM((2 * parts * inner // BLK, count, BLK), jnp.float32),
            pltpu.SemaphoreType.DMA((len(xs),)),
            pltpu.SemaphoreType.DMA((2 * features // deep,)),
        ],
        out_shape=[jax.ShapeDtypeStruct(s, jnp.bfloat16) for s in shapes],
        compiler_params=pltpu.CompilerParams(vmem_limit_bytes=56 * MIB),
        cost_estimate=pl.CostEstimate(
            flops=4 * parts * inner * features * count,
            bytes_accessed=2 * features * (count + 2 * parts * inner),
            transcendentals=0,
        ),
        name="project",
    )(chips, heads, *xs, own, other, modulation)


def attend_kernel(factor, unroll, plan, places, counts, first, owner, *refs):
    arrays, outs, rest = refs[: -4 - 8], refs[-4 - 8 : -8], refs[-8:]
    kv, query, asked, scores, tops, totals, sums, arrived = rest
    copies = []
    for kind, index, array, start in plan:
        to = (kv if kind == "kv" else query).at[index]
        rows = to.shape[0]
        copies.append(
            pltpu.make_async_copy(
                arrays[array].at[start : start + rows], to, arrived.at[len(copies)]
            )
        )
    for copy in copies:
        copy.start()
    per_piece = kv.shape[2] // BLK
    rows = len(outs) * per_piece
    tops[...] = jnp.full_like(tops, NEGATIVE)
    totals[...] = jnp.zeros_like(totals)
    sums[...] = jnp.zeros_like(sums)
    for copy in copies:
        copy.wait()
    for index in range(len(outs)):
        for part in range(per_piece):
            asked[index * per_piece + part] = query[index, :, part * BLK : (part + 1) * BLK]

    def find(pair, low, high):
        live = pair < high
        pair = jnp.where(live, pair, low)
        row = owner[pair]
        place = 2 * (pair - first[row])
        wheres = [places[row, place], places[row, place + 1]]
        offsets = [
            jnp.where(live, 0.0, NEGATIVE),
            jnp.where(live & (place + 1 < counts[row]), 0.0, NEGATIVE),
        ]
        return row, wheres, offsets

    def held(where, part):
        start = pl.multiple_of((where & (per_piece - 1)) * BLK, BLK)
        return kv[where >> 2, part * BLK : (part + 1) * BLK, pl.ds(start, BLK)]

    def fold(op, value):
        return op(value.reshape(BLK // 8, 8, BLK), axis=0)

    def rate(low, high, step, _):
        found = []
        for item in range(unroll):
            pair = step * unroll + item
            row, wheres, offsets = find(low + pair, low, high)
            keys = jnp.concatenate([held(where, 0) for where in wheres], axis=0)
            score = jnp.dot(keys, asked[row], preferred_element_type=jnp.float32)
            scores[pair] = score
            best = jnp.maximum(
                fold(jnp.max, score[:BLK]) + offsets[0], fold(jnp.max, score[BLK:]) + offsets[1]
            )
            found.append((row, best))
        for row, best in found:
            tops[row] = jnp.maximum(tops[row], best)
        return 0

    def gather(low, high, step, _):
        found = []
        for item in range(unroll):
            pair = step * unroll + item
            row, wheres, offsets = find(low + pair, low, high)
            top = tops[row][:1]
            score = scores[pair]
            halves = [
                jnp.exp2(score[part * BLK : (part + 1) * BLK] * factor - (top - offsets[part]))
                for part in range(2)
            ]
            total = fold(jnp.sum, halves[0]) + fold(jnp.sum, halves[1])
            weights = jnp.concatenate([half.astype(jnp.bfloat16) for half in halves], axis=0)
            values = jnp.concatenate([held(where, 1) for where in wheres], axis=1)
            summed = jnp.dot(values, weights, preferred_element_type=jnp.float32)
            found.append((row, total, summed))
        for row, total, summed in found:
            totals[row] += total
            sums[row] += summed
        return 0

    for index in range(len(outs)):
        low, high = first[index * per_piece], first[(index + 1) * per_piece]
        steps = (high - low + unroll - 1) // unroll
        lax.fori_loop(0, steps, functools.partial(rate, low, high), 0)
        for row in range(index * per_piece, (index + 1) * per_piece):
            top = jnp.max(tops[row], axis=0, keepdims=True) * factor
            tops[row] = jnp.broadcast_to(top, tops.shape[1:])
        lax.fori_loop(0, steps, functools.partial(gather, low, high), 0)

    for index, out in enumerate(outs):
        for part in range(per_piece):
            row = index * per_piece + part
            total = jnp.sum(totals[row], axis=0, keepdims=True)
            value = (sums[row] / total).T.astype(jnp.bfloat16)
            out[part * BLK : (part + 1) * BLK, :] = value


def pair_lists(counts, most):
    twos = (counts + 1) // 2
    rows = counts.shape[0]
    order = jnp.arange(rows + 1, dtype=jnp.int32)
    first = jnp.sum(jnp.where(order[None, :rows] < order[:, None], twos[None, :], 0), axis=1)
    slots = jnp.arange(rows * most // 2, dtype=jnp.int32)
    return first, jnp.sum(jnp.where(first[None, 1:] <= slots[:, None], 1, 0), axis=1)


def attend(factor, lists, plan, arrays, count):
    rows, most = lists[0].shape
    pieces = most * BLK // count
    asking = rows * BLK // count

    def kernel(*refs):
        attend_kernel(factor, PAIRS, plan, *refs)

    shape = (BLK, count)
    return pl.pallas_call(
        kernel,
        in_specs=[pl.BlockSpec(memory_space=pltpu.SMEM)] * len(lists)
        + [pl.BlockSpec(memory_space=pl.ANY)] * len(arrays),
        out_specs=[pl.BlockSpec(memory_space=pltpu.VMEM)] * asking,
        out_shape=[jax.ShapeDtypeStruct((count, BLK), jnp.bfloat16)] * asking,
        scratch_shapes=[
            pltpu.VMEM((pieces, 2 * BLK, count), jnp.bfloat16),
            pltpu.VMEM((asking, *shape), jnp.bfloat16),
            pltpu.VMEM((rows, BLK, BLK), jnp.bfloat16),
            pltpu.VMEM((rows * most // 2 // asking + PAIRS, 2 * BLK, BLK), jnp.float32),
            pltpu.VMEM((rows, 8, BLK), jnp.float32),
            pltpu.VMEM((rows, 8, BLK), jnp.float32),
            pltpu.VMEM((rows, BLK, BLK), jnp.float32),
            pltpu.SemaphoreType.DMA((len(plan),)),
        ],
        compiler_params=pltpu.CompilerParams(vmem_limit_bytes=32 * MIB),
        cost_estimate=pl.CostEstimate(
            flops=rows * BLK * most * BLK * BLK,
            bytes_accessed=4 * most * BLK * BLK,
            transcendentals=rows * BLK * most * BLK // 4,
        ),
        name="attend",
    )(*lists, *arrays)


def leave_kernel(plan, chips, columns, own, other, *refs):
    heads, outs, ordered, arrived = refs[:4], list(refs[4:-2]), *refs[-2:]
    step = pl.program_id(0)

    @pl.when(step == 0)
    def _():
        copies = [
            pltpu.make_async_copy(head, ordered.at[columns[index]], arrived.at[index])
            for index, head in enumerate(heads)
        ]
        for copy in copies:
            copy.start()
        for copy in copies:
            copy.wait()

    summed = jnp.dot(
        jnp.concatenate([ordered[index] for index in range(4)], axis=1),
        jnp.concatenate([own[...], other[...]], axis=0),
        preferred_element_type=jnp.float32,
    )
    for index, cuts in enumerate(plan):
        mine = [outs.pop(0) for _ in cuts]

        @pl.when(step == index)
        def _():
            for cut, out in zip(cuts, mine):
                out[...] = summed[:, cut[0] : cut[1]].astype(out.dtype)


def leave(chips, columns, weights, heads, plan):
    count = heads[0].shape[0]
    steps = len(plan)
    inner = weights[0].shape[0]
    block = pl.BlockSpec((inner, DEEP), lambda i, chips, columns: (0, chips[i]))
    whole = lambda shape: pl.BlockSpec(shape, lambda i, *_: (0, 0))
    shapes = [(count, cut[1] - cut[0]) for cuts in plan for cut in cuts]

    def kernel(*refs):
        leave_kernel(plan, *refs)

    return pl.pallas_call(
        kernel,
        grid_spec=pltpu.PrefetchScalarGridSpec(
            num_scalar_prefetch=2,
            grid=(steps,),
            in_specs=[block] * 2 + [pl.BlockSpec(memory_space=pl.ANY)] * 4,
            out_specs=[whole(s) for s in shapes],
            scratch_shapes=[
                pltpu.VMEM((4, count, BLK), jnp.bfloat16),
                pltpu.SemaphoreType.DMA((4,)),
            ],
        ),
        out_shape=[jax.ShapeDtypeStruct(s, jnp.bfloat16) for s in shapes],
        compiler_params=pltpu.CompilerParams(vmem_limit_bytes=28 * MIB),
        cost_estimate=pl.CostEstimate(
            flops=4 * steps * DEEP * inner * count,
            bytes_accessed=2 * steps * DEEP * (2 * inner + count),
            transcendentals=0,
        ),
        name="leave",
    )(chips, columns, *weights, *heads)


def arrive_kernel(plan, turned, *refs):
    outs = refs[-len(plan) :]
    at = 0
    for cuts, out in zip(plan, outs):
        share, arrived = refs[at], refs[at + 1 : at + 1 + len(cuts)]
        at += 1 + len(cuts)
        edges = sorted({0, share.shape[1], *[edge for cut in cuts for edge in cut]})
        for low, high in zip(edges, edges[1:]):
            value = share[:, low:high].astype(jnp.float32)
            for (first, last), ref in zip(cuts, arrived):
                if first <= low and high <= last:
                    value += ref[:, low - first : high - first].astype(jnp.float32)
            if turned:
                out[low:high, :] = value.T.astype(out.dtype)
            else:
                out[:, low:high] = value.astype(out.dtype)


def arrive(plan, *arrays, turned=False):
    shapes, at = [], 0
    for cuts in plan:
        shapes.append(arrays[at].shape[::-1] if turned else arrays[at].shape)
        at += 1 + len(cuts)

    def kernel(*refs):
        arrive_kernel(plan, turned, *refs)

    return pl.pallas_call(
        kernel,
        in_specs=[pl.BlockSpec(memory_space=pltpu.VMEM)] * len(arrays),
        out_specs=[pl.BlockSpec(memory_space=pltpu.VMEM)] * len(plan),
        out_shape=[jax.ShapeDtypeStruct(shape, arrays[0].dtype) for shape in shapes],
        compiler_params=pltpu.CompilerParams(vmem_limit_bytes=16 * MIB),
        cost_estimate=pl.CostEstimate(
            flops=0, bytes_accessed=8 * arrays[0].size, transcendentals=0
        ),
        name="arrive",
    )(*arrays)


def gather_tokens(own, first_others, second_others):
    below = shift(own, "z", 1)
    above = shift(own, "z", -1)
    beside = swap(own, "yl")
    below, above, beside = together((below, above, beside), first_others)
    far = shift(below, "z", 1)
    beside_below = swap(below, "yl")
    beside_above = shift(beside, "z", -1)
    far, beside_below, beside_above = together((far, beside_below, beside_above), second_others)
    first, second, third = [slice(*cut) for cut in CUTS]
    parts = [
        swap(far[:, first], "yl"),
        shift(beside_above[:, second], "z", -1),
        shift(beside_below[:, third], "z", 1),
    ]
    places = [(0, 0), (0, -1), (0, 1), (1, 0), (0, 2), (1, -1), (1, 1), (1, 2)]
    return places, [own, below, above, beside, far, beside_below, beside_above, *parts]


def shards(tokens, qkv_weight, out_weight, modulation, block_mask):
    rows, local = tokens.shape
    features = modulation.shape[1]
    heads_here = block_mask.shape[0]
    inner = qkv_weight.shape[2]
    head_size = inner // heads_here
    factor = math.log2(math.e) / math.sqrt(head_size)
    half = rows // 2
    core = lax.axis_index("core")
    frame_x, frame_y = lax.axis_index("x"), lax.axis_index("yh")
    chip_y, chip_z = lax.axis_index("yl"), lax.axis_index("z")
    across = tokens.T

    def chip(dy, dz):
        return ((chip_y + dy) % 2) * 4 + (chip_z + dz) % 4

    def mine_and_given(value, axis):
        size = value.shape[axis] // 2
        mine = lax.dynamic_slice_in_dim(value, core * size, size, axis)
        return mine, lax.dynamic_slice_in_dim(value, (1 - core) * size, size, axis)

    def head_slot(steps):
        head = (frame_x + steps) % 4
        return jnp.where(head // 2 == core, 0, 1), head % 2

    mine, given = mine_and_given(across, 1)
    other = swap(given, "core")
    own = lay(core, mine, other)
    mask_mine, mask_given = mine_and_given(block_mask, 1)
    mask_other = swap(mask_given, "core")

    raw, *_ = lax.optimization_barrier((qkv_weight, own, mask_other))
    other_weight = swap(raw, "core")
    mask_heads = jnp.stack([mask_mine, mask_other])
    mask_rows = []
    for steps in range(4):
        side, slot = head_slot(steps)
        part = lax.dynamic_slice(
            mask_heads, (side, slot, 0, 0), (1, 1, *mask_heads.shape[2:])
        )[0, 0]
        mask_rows.append(shift(part, "x", steps) if steps else part)
    keep = jnp.concatenate(mask_rows, axis=0) != 0
    blocks = jnp.arange(keep.shape[1], dtype=jnp.int32)
    per_core = half // BLK
    piece, inside = blocks // per_core, blocks % per_core
    from_core, from_y = core ^ (piece // 8), frame_y ^ (piece // 4 % 2)
    from_x = (frame_x - piece % 4) % 4
    origin = (from_y * 4 + from_x) * (2 * per_core) + from_core * per_core + inside
    same = origin[:, None] == blocks[None, :]
    keep = jnp.sum(jnp.where(same[None] & keep[:, None, :], 1, 0), axis=2)
    counts = jnp.sum(keep, axis=1)
    earlier = blocks[None, :] < blocks[:, None]
    rank = jnp.sum(jnp.where(earlier[None], keep[:, None, :], 0), axis=2)
    chosen = (keep[:, None, :] != 0) & (rank[:, None, :] == blocks[None, :, None])
    listed = jnp.sum(jnp.where(chosen, blocks[None, None, :], 0), axis=2)
    lists = (listed, counts, *pair_lists(counts, listed.shape[1]))
    places, xs = gather_tokens(own, (), mask_rows[1:])

    chips = jnp.stack([chip(*place) for place in places]).astype(jnp.int32)
    slots = [head_slot(steps) for steps in range(4)]
    bases = jnp.stack([side * 3 * heads_here + slot for side, slot in slots]).astype(jnp.int32)
    made = project(chips, bases, xs, qkv_weight, other_weight, modulation)
    kv, query, kv_two, q_two, *packed = made
    one, three = shift(packed[0], "x", 1), shift(packed[1], "x", 3)
    away_kv = swap(kv, "yh")
    one, three = together((one, three), (away_kv,))
    both = jnp.concatenate([one[: 2 * BLK], three[: 2 * BLK]], axis=0)
    away_both = swap(both, "yh")
    kv_two, q_two = together((kv_two, q_two), (one,))
    two, q_two = shift(kv_two, "x", 2), shift(q_two, "x", 2)
    away_kv_other = swap(away_kv, "core")
    two, kv, both = together((two, kv, both), (away_both, q_two, *lists, away_kv_other))
    away_two = swap(two, "yh")
    near = swap(jnp.concatenate([kv, both], axis=0), "core")
    arrays = [kv, both, two, away_kv, away_both, away_two, near, swap(two, "core")]
    arrays += [away_kv_other, swap(away_both, "core"), swap(away_two, "core")]
    arrays += [query, one, q_two, three]
    step = 2 * BLK
    plan = []
    for index, array in ((0, 0), (4, 3), (12, 8)):
        plan += [("kv", index, array, 0), ("kv", index + 1, array + 1, 0)]
        plan += [("kv", index + 3, array + 1, step), ("kv", index + 2, array + 2, 0)]
    plan += [("kv", 8, 6, 0), ("kv", 9, 6, step), ("kv", 11, 6, 2 * step), ("kv", 10, 7, 0)]
    plan += [("q", index, 11 + index, index % 2 * step) for index in range(4)]
    heads = attend(factor, lists, plan, arrays, half)
    (out_own,) = together((out_weight,), (heads[0],))
    leaving = out_weight, swap(out_own, "core")
    heads = [heads[0]] + [shift(heads[steps], "x", -steps) for steps in (1, 2, 3)]

    columns = jnp.stack([side * heads_here + slot for side, slot in slots]).astype(jnp.int32)
    whole = CUTS[0][0], CUTS[-1][1]

    def shares(targets, cuts, heads):
        chips = jnp.stack([chip(*target) for target in targets]).astype(jnp.int32)
        return leave(chips, columns, leaving, heads, [cuts] * len(targets))

    parts = shares([(1, 2)], CUTS, heads)
    middle = [(0, 2), (1, 1), (1, -1)]
    share = dict(zip(middle, shares(middle, (whole,), heads)))
    first = swap(parts[0], "yl")
    second = shift(parts[1], "z", 1)
    third = shift(parts[2], "z", -1)
    heads = together(heads, (first, second, third))
    near = [(0, -1), (0, 1), (1, 0), (0, 0)]
    share |= dict(zip(near, shares(near, (whole,), heads)))
    down, up, side = arrive(
        [(CUTS[0],), (CUTS[1],), (CUTS[2],)],
        *[share[0, 2], first, share[1, 1], second, share[1, -1], third],
    )
    down, up, side = shift(down, "z", -1), shift(up, "z", 1), swap(side, "yl")
    down, side = arrive(
        [(whole, whole), (whole,)], share[0, -1], down, side, share[1, 0], up
    )
    down, up, side = shift(down, "z", -1), shift(share[0, 1], "z", 1), swap(side, "yl")
    (summed,) = arrive([(whole, whole, whole)], share[0, 0], down, up, side, turned=True)

    kept, given = mine_and_given(summed, 0)
    other = swap(given, "core")
    projected = jnp.concatenate(
        [jnp.where(core == 0, kept, other), jnp.where(core == 0, other, kept)], axis=1
    ).astype(jnp.float32)
    start = lax.axis_index(HEAD) * local
    gate = lax.dynamic_slice_in_dim(modulation, start, local, 1)[2][:, None]
    return (across.astype(jnp.float32) + gate * projected).astype(jnp.bfloat16).T


def solution(mesh):
    fine = Mesh(mesh.devices.reshape(2, 4, 2, 4, 2), ("yh", "x", "yl", "z", "core"))
    placed = (
        P(FRAME, HEAD),
        P(None, None, HEAD),
        P(HEAD, None),
        P(),
        P(HEAD, FRAME, None),
    )
    return jax.shard_map(
        shards, mesh=fine, in_specs=placed, out_specs=P(FRAME, HEAD), check_vma=False
    )
```

```python
import functools
import math

import jax
import jax.numpy as jnp
from jax import lax
from jax.experimental import pallas as pl
from jax.experimental.pallas import tpu as pltpu
from jax.sharding import Mesh
from jax.sharding import PartitionSpec as P

BLK = 128
EPSILON = 1e-06
NEGATIVE = -1e30
FRAME = ("yh", "x")
HEAD = ("yl", "z", "core")
MIB = 1 << 20
PAIRS = 12
FIT = 192
CUTS = ((0, 256), (256, 512), (512, 640))


DEEP = CUTS[-1][1]


def shift(value, axis, steps):
    count = lax.axis_size(axis)
    return lax.ppermute(value, axis, [(i, (i + steps) % count) for i in range(count)])


def swap(value, axis):
    return shift(value, axis, 1)


def lay_kernel(core, mine, other, out):
    first = core[0] == 0
    mine, other = mine[...].astype(jnp.float32), other[...].astype(jnp.float32)
    half = mine.shape[0]
    upper = jnp.where(first, mine, other)
    lower = jnp.where(first, other, mine)
    out[...] = jnp.concatenate([upper, lower], axis=0).T.astype(out.dtype)


def lay(core, mine, other):
    half, count = mine.shape
    return pl.pallas_call(
        lay_kernel,
        in_specs=[pl.BlockSpec(memory_space=pltpu.SMEM)]
        + [pl.BlockSpec(memory_space=pltpu.VMEM)] * 2,
        out_specs=pl.BlockSpec(memory_space=pltpu.VMEM),
        out_shape=jax.ShapeDtypeStruct((count, 2 * half), mine.dtype),
        compiler_params=pltpu.CompilerParams(vmem_limit_bytes=12 * MIB),
        cost_estimate=pl.CostEstimate(
            flops=0, bytes_accessed=8 * half * count, transcendentals=0
        ),
        name="lay",
    )(jnp.reshape(core, (1,)).astype(jnp.int32), mine, other)


def together(arrays, others=()):
    return lax.optimization_barrier((*arrays, *others))[: len(arrays)]


ROWS = 64
NEAR = {1: 4, 3: 5}


def project_kernel(chips, heads, *refs):
    xs, weights, modulation, rest = refs[:10], refs[10:12], refs[12], refs[13:]
    outs, (held_x, held_weight, normed, total, arrived, loaded) = rest[:-6], rest[-6:]
    count, features = normed.shape
    tiles = [(piece, at) for piece in range(8) for at in range(0, DEEP, BLK)]

    places = [held_x.at[piece] for piece in range(7)]
    places += [held_x.at[7, :, cut[0] : cut[1]] for cut in CUTS]
    copies = [
        pltpu.make_async_copy(x, place, arrived.at[index])
        for index, (x, place) in enumerate(zip(xs, places))
    ]
    for copy in copies:
        copy.start()
    loads = []
    for side, weight in enumerate(weights):
        for piece in range(8):
            rows = pl.ds(pl.multiple_of(chips[piece] * DEEP, BLK), DEEP)
            loads.append(
                pltpu.make_async_copy(
                    weight.at[:, rows, :],
                    held_weight.at[side, :, piece * DEEP : (piece + 1) * DEEP, :],
                    loaded.at[side * 8 + piece],
                )
            )
    for copy in copies:
        copy.wait()
    for copy in loads:
        copy.start()

    def norm(i, _):
        rows = pl.ds(pl.multiple_of(i * ROWS, ROWS), ROWS)

        def load(piece, at):
            return held_x[piece, rows, at : at + BLK].astype(jnp.float32)

        summed = jnp.zeros((ROWS, BLK), jnp.float32)
        for tile in tiles:
            summed = summed + load(*tile)
        center = jnp.sum(summed, axis=1, keepdims=True) / features
        center = jnp.broadcast_to(center, (ROWS, BLK))
        summed = jnp.zeros((ROWS, BLK), jnp.float32)
        for tile in tiles:
            summed = summed + jnp.square(load(*tile) - center)
        spread = jnp.sum(summed, axis=1, keepdims=True) / features
        rate = jnp.broadcast_to(lax.rsqrt(spread + EPSILON), (ROWS, BLK))
        for piece, at in tiles:
            place = pl.ds(pl.multiple_of(chips[piece] * DEEP + at, BLK), BLK)
            gain = 1.0 + modulation[1:2, place]
            value = (load(piece, at) - center) * rate * gain + modulation[0:1, place]
            column = piece * DEEP + at
            normed[rows, column : column + BLK] = value.astype(jnp.bfloat16)
        return 0

    lax.fori_loop(0, count // ROWS, norm, 0)
    for copy in loads:
        copy.wait()
    for side in range(2):
        for part in range(3):
            made = jnp.dot(
                normed[...], held_weight[side, part], preferred_element_type=jnp.float32
            )
            for slot in range(2):
                total[side * 6 + part * 2 + slot] = made[:, slot * BLK : (slot + 1) * BLK]
    for index in range(4):
        if index % 2:
            kv, q = outs[NEAR[index]], outs[NEAR[index]].at[2 * BLK :]
        else:
            kv, q = outs[index : index + 2]
        base = heads[index]
        q[...] = total[base].T.astype(jnp.bfloat16)
        for part in range(count // BLK):
            rows = slice(part * BLK, (part + 1) * BLK)
            kv[:BLK, rows] = total[base + 2, rows].astype(jnp.bfloat16)
        kv[BLK : 2 * BLK, :] = total[base + 4].T.astype(jnp.bfloat16)


def project(chips, heads, xs, own, other, modulation):
    parts, features, inner = own.shape
    count, deep = xs[0].shape
    shapes = [(2 * BLK, count), (BLK, count)] * 2 + [(3 * BLK, count)] * 2
    return pl.pallas_call(
        project_kernel,
        in_specs=[pl.BlockSpec(memory_space=pltpu.SMEM)] * 2
        + [pl.BlockSpec(memory_space=pl.ANY)] * (len(xs) + 2)
        + [pl.BlockSpec(memory_space=pltpu.VMEM)],
        out_specs=[pl.BlockSpec(memory_space=pltpu.VMEM)] * len(shapes),
        scratch_shapes=[
            pltpu.VMEM((features // deep, count, deep), jnp.bfloat16),
            pltpu.VMEM((2, parts, features, inner), jnp.bfloat16),
            pltpu.VMEM((count, features), jnp.bfloat16),
            pltpu.VMEM((2 * parts * inner // BLK, count, BLK), jnp.float32),
            pltpu.SemaphoreType.DMA((len(xs),)),
            pltpu.SemaphoreType.DMA((2 * features // deep,)),
        ],
        out_shape=[jax.ShapeDtypeStruct(s, jnp.bfloat16) for s in shapes],
        compiler_params=pltpu.CompilerParams(vmem_limit_bytes=56 * MIB),
        cost_estimate=pl.CostEstimate(
            flops=4 * parts * inner * features * count,
            bytes_accessed=2 * features * (count + 2 * parts * inner),
            transcendentals=0,
        ),
        name="project",
    )(chips, heads, *xs, own, other, modulation)


def attend_kernel(factor, unroll, plan, places, counts, first, owner, *refs):
    arrays, outs, rest = refs[: -4 - 8], refs[-4 - 8 : -8], refs[-8:]
    kv, query, asked, scores, tops, totals, sums, arrived = rest
    copies = []
    for kind, index, array, start in plan:
        to = (kv if kind == "kv" else query).at[index]
        rows = to.shape[0]
        copies.append(
            pltpu.make_async_copy(
                arrays[array].at[start : start + rows], to, arrived.at[len(copies)]
            )
        )
    for copy in copies:
        copy.start()
    per_piece = kv.shape[2] // BLK
    rows = len(outs) * per_piece
    tops[...] = jnp.full_like(tops, NEGATIVE)
    totals[...] = jnp.zeros_like(totals)
    sums[...] = jnp.zeros_like(sums)
    for copy in copies:
        copy.wait()
    for index in range(len(outs)):
        for part in range(per_piece):
            asked[index * per_piece + part] = query[index, :, part * BLK : (part + 1) * BLK]

    def find(pair, low, high):
        live = pair < high
        pair = jnp.where(live, pair, low)
        row = owner[pair]
        place = 2 * (pair - first[row])
        wheres = [places[row, place], places[row, place + 1]]
        offsets = [
            jnp.where(live, 0.0, NEGATIVE),
            jnp.where(live & (place + 1 < counts[row]), 0.0, NEGATIVE),
        ]
        return row, wheres, offsets

    def held(where, part):
        start = pl.multiple_of((where & (per_piece - 1)) * BLK, BLK)
        return kv[where >> 2, part * BLK : (part + 1) * BLK, pl.ds(start, BLK)]

    def fold(op, value):
        return op(value.reshape(BLK // 8, 8, BLK), axis=0)

    def rate(low, high, step, _):
        found = []
        for item in range(unroll):
            pair = step * unroll + item
            row, wheres, offsets = find(low + pair, low, high)
            keys = jnp.concatenate([held(where, 0) for where in wheres], axis=0)
            score = jnp.dot(keys, asked[row], preferred_element_type=jnp.float32)
            scores[pair] = score
            best = jnp.maximum(
                fold(jnp.max, score[:BLK]) + offsets[0], fold(jnp.max, score[BLK:]) + offsets[1]
            )
            found.append((row, best))
        for row, best in found:
            tops[row] = jnp.maximum(tops[row], best)
        return 0

    def gather(low, high, step, _):
        found = []
        for item in range(unroll):
            pair = step * unroll + item
            row, wheres, offsets = find(low + pair, low, high)
            top = tops[row][:1]
            score = scores[pair]
            halves = [
                jnp.exp2(score[part * BLK : (part + 1) * BLK] * factor - (top - offsets[part]))
                for part in range(2)
            ]
            total = fold(jnp.sum, halves[0]) + fold(jnp.sum, halves[1])
            weights = jnp.concatenate([half.astype(jnp.bfloat16) for half in halves], axis=0)
            values = jnp.concatenate([held(where, 1) for where in wheres], axis=1)
            summed = jnp.dot(values, weights, preferred_element_type=jnp.float32)
            found.append((row, total, summed))
        for row, total, summed in found:
            totals[row] += total
            sums[row] += summed
        return 0

    whole = first[rows] <= FIT
    size = jnp.where(whole, rows, per_piece)

    def segment(index, _):
        begin = index * size
        low, high = first[begin], first[begin + size]
        steps = (high - low + unroll - 1) // unroll
        lax.fori_loop(0, steps, functools.partial(rate, low, high), 0)

        def settle(row, _):
            top = jnp.max(tops[row], axis=0, keepdims=True) * factor
            tops[row] = jnp.broadcast_to(top, tops.shape[1:])
            return 0

        lax.fori_loop(begin, begin + size, settle, 0)
        lax.fori_loop(0, steps, functools.partial(gather, low, high), 0)
        return 0

    lax.fori_loop(0, jnp.where(whole, 1, len(outs)), segment, 0)

    for index, out in enumerate(outs):
        for part in range(per_piece):
            row = index * per_piece + part
            total = jnp.sum(totals[row], axis=0, keepdims=True)
            value = (sums[row] / total).T.astype(jnp.bfloat16)
            out[part * BLK : (part + 1) * BLK, :] = value


def pair_lists(counts, most):
    twos = (counts + 1) // 2
    rows = counts.shape[0]
    order = jnp.arange(rows + 1, dtype=jnp.int32)
    first = jnp.sum(jnp.where(order[None, :rows] < order[:, None], twos[None, :], 0), axis=1)
    slots = jnp.arange(rows * most // 2, dtype=jnp.int32)
    return first, jnp.sum(jnp.where(first[None, 1:] <= slots[:, None], 1, 0), axis=1)


def attend(factor, lists, plan, arrays, count):
    rows, most = lists[0].shape
    pieces = most * BLK // count
    asking = rows * BLK // count

    def kernel(*refs):
        attend_kernel(factor, PAIRS, plan, *refs)

    shape = (BLK, count)
    return pl.pallas_call(
        kernel,
        in_specs=[pl.BlockSpec(memory_space=pltpu.SMEM)] * len(lists)
        + [pl.BlockSpec(memory_space=pl.ANY)] * len(arrays),
        out_specs=[pl.BlockSpec(memory_space=pltpu.VMEM)] * asking,
        out_shape=[jax.ShapeDtypeStruct((count, BLK), jnp.bfloat16)] * asking,
        scratch_shapes=[
            pltpu.VMEM((pieces, 2 * BLK, count), jnp.bfloat16),
            pltpu.VMEM((asking, *shape), jnp.bfloat16),
            pltpu.VMEM((rows, BLK, BLK), jnp.bfloat16),
            pltpu.VMEM((max(rows * most // 2 // asking, FIT) + PAIRS, 2 * BLK, BLK), jnp.float32),
            pltpu.VMEM((rows, 8, BLK), jnp.float32),
            pltpu.VMEM((rows, 8, BLK), jnp.float32),
            pltpu.VMEM((rows, BLK, BLK), jnp.float32),
            pltpu.SemaphoreType.DMA((len(plan),)),
        ],
        compiler_params=pltpu.CompilerParams(vmem_limit_bytes=42 * MIB),
        cost_estimate=pl.CostEstimate(
            flops=rows * BLK * most * BLK * BLK,
            bytes_accessed=4 * most * BLK * BLK,
            transcendentals=rows * BLK * most * BLK // 4,
        ),
        name="attend",
    )(*lists, *arrays)


def leave_kernel(plan, chips, columns, own, other, *refs):
    heads, outs, ordered, arrived = refs[:4], list(refs[4:-2]), *refs[-2:]
    step = pl.program_id(0)

    @pl.when(step == 0)
    def _():
        copies = [
            pltpu.make_async_copy(head, ordered.at[columns[index]], arrived.at[index])
            for index, head in enumerate(heads)
        ]
        for copy in copies:
            copy.start()
        for copy in copies:
            copy.wait()

    summed = jnp.dot(
        jnp.concatenate([ordered[index] for index in range(4)], axis=1),
        jnp.concatenate([own[...], other[...]], axis=0),
        preferred_element_type=jnp.float32,
    )
    for index, cuts in enumerate(plan):
        mine = [outs.pop(0) for _ in cuts]

        @pl.when(step == index)
        def _():
            for cut, out in zip(cuts, mine):
                out[...] = summed[:, cut[0] : cut[1]].astype(out.dtype)


def leave(chips, columns, weights, heads, plan):
    count = heads[0].shape[0]
    steps = len(plan)
    inner = weights[0].shape[0]
    block = pl.BlockSpec((inner, DEEP), lambda i, chips, columns: (0, chips[i]))
    whole = lambda shape: pl.BlockSpec(shape, lambda i, *_: (0, 0))
    shapes = [(count, cut[1] - cut[0]) for cuts in plan for cut in cuts]

    def kernel(*refs):
        leave_kernel(plan, *refs)

    return pl.pallas_call(
        kernel,
        grid_spec=pltpu.PrefetchScalarGridSpec(
            num_scalar_prefetch=2,
            grid=(steps,),
            in_specs=[block] * 2 + [pl.BlockSpec(memory_space=pl.ANY)] * 4,
            out_specs=[whole(s) for s in shapes],
            scratch_shapes=[
                pltpu.VMEM((4, count, BLK), jnp.bfloat16),
                pltpu.SemaphoreType.DMA((4,)),
            ],
        ),
        out_shape=[jax.ShapeDtypeStruct(s, jnp.bfloat16) for s in shapes],
        compiler_params=pltpu.CompilerParams(vmem_limit_bytes=28 * MIB),
        cost_estimate=pl.CostEstimate(
            flops=4 * steps * DEEP * inner * count,
            bytes_accessed=2 * steps * DEEP * (2 * inner + count),
            transcendentals=0,
        ),
        name="leave",
    )(chips, columns, *weights, *heads)


def arrive_kernel(plan, turned, *refs):
    outs = refs[-len(plan) :]
    at = 0
    for cuts, out in zip(plan, outs):
        share, arrived = refs[at], refs[at + 1 : at + 1 + len(cuts)]
        at += 1 + len(cuts)
        edges = sorted({0, share.shape[1], *[edge for cut in cuts for edge in cut]})
        for low, high in zip(edges, edges[1:]):
            value = share[:, low:high].astype(jnp.float32)
            for (first, last), ref in zip(cuts, arrived):
                if first <= low and high <= last:
                    value += ref[:, low - first : high - first].astype(jnp.float32)
            if turned:
                out[low:high, :] = value.T.astype(out.dtype)
            else:
                out[:, low:high] = value.astype(out.dtype)


def arrive(plan, *arrays, turned=False):
    shapes, at = [], 0
    for cuts in plan:
        shapes.append(arrays[at].shape[::-1] if turned else arrays[at].shape)
        at += 1 + len(cuts)

    def kernel(*refs):
        arrive_kernel(plan, turned, *refs)

    return pl.pallas_call(
        kernel,
        in_specs=[pl.BlockSpec(memory_space=pltpu.VMEM)] * len(arrays),
        out_specs=[pl.BlockSpec(memory_space=pltpu.VMEM)] * len(plan),
        out_shape=[jax.ShapeDtypeStruct(shape, arrays[0].dtype) for shape in shapes],
        compiler_params=pltpu.CompilerParams(vmem_limit_bytes=16 * MIB),
        cost_estimate=pl.CostEstimate(
            flops=0, bytes_accessed=8 * arrays[0].size, transcendentals=0
        ),
        name="arrive",
    )(*arrays)


def gather_tokens(own, first_others, second_others):
    below = shift(own, "z", 1)
    above = shift(own, "z", -1)
    beside = swap(own, "yl")
    below, above, beside = together((below, above, beside), first_others)
    far = shift(below, "z", 1)
    beside_below = swap(below, "yl")
    beside_above = shift(beside, "z", -1)
    far, beside_below, beside_above = together((far, beside_below, beside_above), second_others)
    first, second, third = [slice(*cut) for cut in CUTS]
    parts = [
        swap(far[:, first], "yl"),
        shift(beside_above[:, second], "z", -1),
        shift(beside_below[:, third], "z", 1),
    ]
    places = [(0, 0), (0, -1), (0, 1), (1, 0), (0, 2), (1, -1), (1, 1), (1, 2)]
    return places, [own, below, above, beside, far, beside_below, beside_above, *parts]


def shards(tokens, qkv_weight, out_weight, modulation, block_mask):
    rows, local = tokens.shape
    features = modulation.shape[1]
    heads_here = block_mask.shape[0]
    inner = qkv_weight.shape[2]
    head_size = inner // heads_here
    factor = math.log2(math.e) / math.sqrt(head_size)
    half = rows // 2
    core = lax.axis_index("core")
    frame_x, frame_y = lax.axis_index("x"), lax.axis_index("yh")
    chip_y, chip_z = lax.axis_index("yl"), lax.axis_index("z")
    across = tokens.T

    def chip(dy, dz):
        return ((chip_y + dy) % 2) * 4 + (chip_z + dz) % 4

    def mine_and_given(value, axis):
        size = value.shape[axis] // 2
        mine = lax.dynamic_slice_in_dim(value, core * size, size, axis)
        return mine, lax.dynamic_slice_in_dim(value, (1 - core) * size, size, axis)

    def head_slot(steps):
        head = (frame_x + steps) % 4
        return jnp.where(head // 2 == core, 0, 1), head % 2

    mine, given = mine_and_given(across, 1)
    other = swap(given, "core")
    own = lay(core, mine, other)
    mask_mine, mask_given = mine_and_given(block_mask, 1)
    mask_other = swap(mask_given, "core")

    raw, *_ = lax.optimization_barrier((qkv_weight, own, mask_other))
    other_weight = swap(raw, "core")
    mask_heads = jnp.stack([mask_mine, mask_other])
    mask_rows = []
    for steps in range(4):
        side, slot = head_slot(steps)
        part = lax.dynamic_slice(
            mask_heads, (side, slot, 0, 0), (1, 1, *mask_heads.shape[2:])
        )[0, 0]
        mask_rows.append(shift(part, "x", steps) if steps else part)
    keep = jnp.concatenate(mask_rows, axis=0) != 0
    blocks = jnp.arange(keep.shape[1], dtype=jnp.int32)
    per_core = half // BLK
    piece, inside = blocks // per_core, blocks % per_core
    from_core, from_y = core ^ (piece // 8), frame_y ^ (piece // 4 % 2)
    from_x = (frame_x - piece % 4) % 4
    origin = (from_y * 4 + from_x) * (2 * per_core) + from_core * per_core + inside
    same = origin[:, None] == blocks[None, :]
    keep = jnp.sum(jnp.where(same[None] & keep[:, None, :], 1, 0), axis=2)
    counts = jnp.sum(keep, axis=1)
    earlier = blocks[None, :] < blocks[:, None]
    rank = jnp.sum(jnp.where(earlier[None], keep[:, None, :], 0), axis=2)
    chosen = (keep[:, None, :] != 0) & (rank[:, None, :] == blocks[None, :, None])
    listed = jnp.sum(jnp.where(chosen, blocks[None, None, :], 0), axis=2)
    lists = (listed, counts, *pair_lists(counts, listed.shape[1]))
    places, xs = gather_tokens(own, (), mask_rows[1:])

    chips = jnp.stack([chip(*place) for place in places]).astype(jnp.int32)
    slots = [head_slot(steps) for steps in range(4)]
    bases = jnp.stack([side * 3 * heads_here + slot for side, slot in slots]).astype(jnp.int32)
    made = project(chips, bases, xs, qkv_weight, other_weight, modulation)
    kv, query, kv_two, q_two, *packed = made
    one, three = shift(packed[0], "x", 1), shift(packed[1], "x", 3)
    away_kv = swap(kv, "yh")
    one, three = together((one, three), (away_kv,))
    both = jnp.concatenate([one[: 2 * BLK], three[: 2 * BLK]], axis=0)
    away_both = swap(both, "yh")
    kv_two, q_two = together((kv_two, q_two), (one,))
    two, q_two = shift(kv_two, "x", 2), shift(q_two, "x", 2)
    away_kv_other = swap(away_kv, "core")
    two, kv, both = together((two, kv, both), (away_both, q_two, *lists, away_kv_other))
    away_two = swap(two, "yh")
    near = swap(jnp.concatenate([kv, both], axis=0), "core")
    arrays = [kv, both, two, away_kv, away_both, away_two, near, swap(two, "core")]
    arrays += [away_kv_other, swap(away_both, "core"), swap(away_two, "core")]
    arrays += [query, one, q_two, three]
    step = 2 * BLK
    plan = []
    for index, array in ((0, 0), (4, 3), (12, 8)):
        plan += [("kv", index, array, 0), ("kv", index + 1, array + 1, 0)]
        plan += [("kv", index + 3, array + 1, step), ("kv", index + 2, array + 2, 0)]
    plan += [("kv", 8, 6, 0), ("kv", 9, 6, step), ("kv", 11, 6, 2 * step), ("kv", 10, 7, 0)]
    plan += [("q", index, 11 + index, index % 2 * step) for index in range(4)]
    heads = attend(factor, lists, plan, arrays, half)
    (out_own,) = together((out_weight,), (heads[0],))
    leaving = out_weight, swap(out_own, "core")
    heads = [heads[0]] + [shift(heads[steps], "x", -steps) for steps in (1, 2, 3)]

    columns = jnp.stack([side * heads_here + slot for side, slot in slots]).astype(jnp.int32)
    whole = CUTS[0][0], CUTS[-1][1]

    def shares(targets, cuts, heads):
        chips = jnp.stack([chip(*target) for target in targets]).astype(jnp.int32)
        return leave(chips, columns, leaving, heads, [cuts] * len(targets))

    parts = shares([(1, 2)], CUTS, heads)
    middle = [(0, 2), (1, 1), (1, -1)]
    share = dict(zip(middle, shares(middle, (whole,), heads)))
    first = swap(parts[0], "yl")
    second = shift(parts[1], "z", 1)
    third = shift(parts[2], "z", -1)
    heads = together(heads, (first, second, third))
    near = [(0, -1), (0, 1), (1, 0), (0, 0)]
    share |= dict(zip(near, shares(near, (whole,), heads)))
    down, up, side = arrive(
        [(CUTS[0],), (CUTS[1],), (CUTS[2],)],
        *[share[0, 2], first, share[1, 1], second, share[1, -1], third],
    )
    down, up, side = shift(down, "z", -1), shift(up, "z", 1), swap(side, "yl")
    down, side = arrive(
        [(whole, whole), (whole,)], share[0, -1], down, side, share[1, 0], up
    )
    down, up, side = shift(down, "z", -1), shift(share[0, 1], "z", 1), swap(side, "yl")
    (summed,) = arrive([(whole, whole, whole)], share[0, 0], down, up, side, turned=True)

    kept, given = mine_and_given(summed, 0)
    other = swap(given, "core")
    projected = jnp.concatenate(
        [jnp.where(core == 0, kept, other), jnp.where(core == 0, other, kept)], axis=1
    ).astype(jnp.float32)
    start = lax.axis_index(HEAD) * local
    gate = lax.dynamic_slice_in_dim(modulation, start, local, 1)[2][:, None]
    return (across.astype(jnp.float32) + gate * projected).astype(jnp.bfloat16).T


def solution(mesh):
    fine = Mesh(mesh.devices.reshape(2, 4, 2, 4, 2), ("yh", "x", "yl", "z", "core"))
    placed = (
        P(FRAME, HEAD),
        P(None, None, HEAD),
        P(HEAD, None),
        P(),
        P(HEAD, FRAME, None),
    )
    return jax.shard_map(
        shards, mesh=fine, in_specs=placed, out_specs=P(FRAME, HEAD), check_vma=False
    )
```

```python
import functools
import math

import jax
import jax.numpy as jnp
from jax import lax
from jax.experimental import pallas as pl
from jax.experimental.pallas import tpu as pltpu
from jax.sharding import Mesh
from jax.sharding import PartitionSpec as P

BLK = 128
EPSILON = 1e-06
NEGATIVE = -1e30
FRAME = ("yh", "x")
HEAD = ("yl", "z", "core")
MIB = 1 << 20
PAIRS = 12
FIT = 192
CUTS = ((0, 256), (256, 512), (512, 640))


DEEP = CUTS[-1][1]


def shift(value, axis, steps):
    count = lax.axis_size(axis)
    return lax.ppermute(value, axis, [(i, (i + steps) % count) for i in range(count)])


def swap(value, axis):
    return shift(value, axis, 1)


def lay_kernel(core, mine, other, out):
    first = core[0] == 0
    mine, other = mine[...].astype(jnp.float32), other[...].astype(jnp.float32)
    half = mine.shape[0]
    upper = jnp.where(first, mine, other)
    lower = jnp.where(first, other, mine)
    out[...] = jnp.concatenate([upper, lower], axis=0).T.astype(out.dtype)


def lay(core, mine, other):
    half, count = mine.shape
    return pl.pallas_call(
        lay_kernel,
        in_specs=[pl.BlockSpec(memory_space=pltpu.SMEM)]
        + [pl.BlockSpec(memory_space=pltpu.VMEM)] * 2,
        out_specs=pl.BlockSpec(memory_space=pltpu.VMEM),
        out_shape=jax.ShapeDtypeStruct((count, 2 * half), mine.dtype),
        compiler_params=pltpu.CompilerParams(vmem_limit_bytes=12 * MIB),
        cost_estimate=pl.CostEstimate(
            flops=0, bytes_accessed=8 * half * count, transcendentals=0
        ),
        name="lay",
    )(jnp.reshape(core, (1,)).astype(jnp.int32), mine, other)


def together(arrays, others=()):
    return lax.optimization_barrier((*arrays, *others))[: len(arrays)]


ROWS = 64
NEAR = {1: 4, 3: 5}


def project_kernel(chips, heads, *refs):
    xs, weights, modulation, rest = refs[:10], refs[10:12], refs[12], refs[13:]
    outs, (held_x, held_weight, normed, total, arrived, loaded) = rest[:-6], rest[-6:]
    count, features = normed.shape
    tiles = [(piece, at) for piece in range(8) for at in range(0, DEEP, BLK)]

    places = [held_x.at[piece] for piece in range(7)]
    places += [held_x.at[7, :, cut[0] : cut[1]] for cut in CUTS]
    copies = [
        pltpu.make_async_copy(x, place, arrived.at[index])
        for index, (x, place) in enumerate(zip(xs, places))
    ]
    for copy in copies:
        copy.start()
    loads = []
    for side, weight in enumerate(weights):
        for piece in range(8):
            rows = pl.ds(pl.multiple_of(chips[piece] * DEEP, BLK), DEEP)
            loads.append(
                pltpu.make_async_copy(
                    weight.at[:, rows, :],
                    held_weight.at[side, :, piece * DEEP : (piece + 1) * DEEP, :],
                    loaded.at[side * 8 + piece],
                )
            )
    for copy in copies:
        copy.wait()
    for copy in loads:
        copy.start()

    def norm(i, _):
        rows = pl.ds(pl.multiple_of(i * ROWS, ROWS), ROWS)

        def load(piece, at):
            return held_x[piece, rows, at : at + BLK].astype(jnp.float32)

        summed = jnp.zeros((ROWS, BLK), jnp.float32)
        for tile in tiles:
            summed = summed + load(*tile)
        center = jnp.sum(summed, axis=1, keepdims=True) / features
        center = jnp.broadcast_to(center, (ROWS, BLK))
        summed = jnp.zeros((ROWS, BLK), jnp.float32)
        for tile in tiles:
            summed = summed + jnp.square(load(*tile) - center)
        spread = jnp.sum(summed, axis=1, keepdims=True) / features
        rate = jnp.broadcast_to(lax.rsqrt(spread + EPSILON), (ROWS, BLK))
        for piece, at in tiles:
            place = pl.ds(pl.multiple_of(chips[piece] * DEEP + at, BLK), BLK)
            gain = 1.0 + modulation[1:2, place]
            value = (load(piece, at) - center) * rate * gain + modulation[0:1, place]
            column = piece * DEEP + at
            normed[rows, column : column + BLK] = value.astype(jnp.bfloat16)
        return 0

    lax.fori_loop(0, count // ROWS, norm, 0)
    for copy in loads:
        copy.wait()
    for side in range(2):
        for part in range(3):
            made = jnp.dot(
                normed[...], held_weight[side, part], preferred_element_type=jnp.float32
            )
            for slot in range(2):
                total[side * 6 + part * 2 + slot] = made[:, slot * BLK : (slot + 1) * BLK]
    for index in range(4):
        if index % 2:
            kv, q = outs[NEAR[index]], outs[NEAR[index]].at[2 * BLK :]
        else:
            kv, q = outs[index : index + 2]
        base = heads[index]
        q[...] = total[base].T.astype(jnp.bfloat16)
        for part in range(count // BLK):
            rows = slice(part * BLK, (part + 1) * BLK)
            kv[:BLK, rows] = total[base + 2, rows].astype(jnp.bfloat16)
        kv[BLK : 2 * BLK, :] = total[base + 4].T.astype(jnp.bfloat16)


def project(chips, heads, xs, own, other, modulation):
    parts, features, inner = own.shape
    count, deep = xs[0].shape
    shapes = [(2 * BLK, count), (BLK, count)] * 2 + [(3 * BLK, count)] * 2
    return pl.pallas_call(
        project_kernel,
        in_specs=[pl.BlockSpec(memory_space=pltpu.SMEM)] * 2
        + [pl.BlockSpec(memory_space=pl.ANY)] * (len(xs) + 2)
        + [pl.BlockSpec(memory_space=pltpu.VMEM)],
        out_specs=[pl.BlockSpec(memory_space=pltpu.VMEM)] * len(shapes),
        scratch_shapes=[
            pltpu.VMEM((features // deep, count, deep), jnp.bfloat16),
            pltpu.VMEM((2, parts, features, inner), jnp.bfloat16),
            pltpu.VMEM((count, features), jnp.bfloat16),
            pltpu.VMEM((2 * parts * inner // BLK, count, BLK), jnp.float32),
            pltpu.SemaphoreType.DMA((len(xs),)),
            pltpu.SemaphoreType.DMA((2 * features // deep,)),
        ],
        out_shape=[jax.ShapeDtypeStruct(s, jnp.bfloat16) for s in shapes],
        compiler_params=pltpu.CompilerParams(vmem_limit_bytes=56 * MIB),
        cost_estimate=pl.CostEstimate(
            flops=4 * parts * inner * features * count,
            bytes_accessed=2 * features * (count + 2 * parts * inner),
            transcendentals=0,
        ),
        name="project",
    )(chips, heads, *xs, own, other, modulation)


def attend_kernel(factor, unroll, plan, places, counts, first, owner, *refs):
    arrays, outs, rest = refs[: -4 - 8], refs[-4 - 8 : -8], refs[-8:]
    kv, query, asked, scores, tops, totals, sums, arrived = rest
    copies = []
    for kind, index, array, start, rows in plan:
        to = kv.at[index * 2 * BLK : index * 2 * BLK + rows] if kind == "kv" else query.at[index]
        copies.append(
            pltpu.make_async_copy(
                arrays[array].at[start : start + rows], to, arrived.at[len(copies)]
            )
        )
    for copy in copies:
        copy.start()
    per_piece = kv.shape[1] // BLK
    rows = len(outs) * per_piece
    tops[...] = jnp.full_like(tops, NEGATIVE)
    totals[...] = jnp.zeros_like(totals)
    sums[...] = jnp.zeros_like(sums)
    for copy in copies:
        copy.wait()
    for index in range(len(outs)):
        for part in range(per_piece):
            asked[index * per_piece + part] = query[index, :, part * BLK : (part + 1) * BLK]

    def find(pair, low, high):
        live = pair < high
        pair = jnp.where(live, pair, low)
        row = owner[pair]
        place = 2 * (pair - first[row])
        wheres = [places[row, place], places[row, place + 1]]
        offsets = [
            jnp.where(live, 0.0, NEGATIVE),
            jnp.where(live & (place + 1 < counts[row]), 0.0, NEGATIVE),
        ]
        return row, wheres, offsets

    def held(where, part):
        start = pl.multiple_of((where & (per_piece - 1)) * BLK, BLK)
        row = pl.multiple_of((where >> 2) * (2 * BLK) + part * BLK, BLK)
        return kv[pl.ds(row, BLK), pl.ds(start, BLK)]

    def fold(op, value):
        return op(value.reshape(BLK // 8, 8, BLK), axis=0)

    def rate(low, high, step, _):
        found = []
        for item in range(unroll):
            pair = step * unroll + item
            row, wheres, offsets = find(low + pair, low, high)
            keys = jnp.concatenate([held(where, 0) for where in wheres], axis=0)
            score = jnp.dot(keys, asked[row], preferred_element_type=jnp.float32)
            scores[pair] = score
            best = jnp.maximum(
                fold(jnp.max, score[:BLK]) + offsets[0], fold(jnp.max, score[BLK:]) + offsets[1]
            )
            found.append((row, best))
        for row, best in found:
            tops[row] = jnp.maximum(tops[row], best)
        return 0

    def gather(low, high, step, _):
        found = []
        for item in range(unroll):
            pair = step * unroll + item
            row, wheres, offsets = find(low + pair, low, high)
            top = tops[row][:1]
            score = scores[pair]
            halves = [
                jnp.exp2(score[part * BLK : (part + 1) * BLK] * factor - (top - offsets[part]))
                for part in range(2)
            ]
            total = fold(jnp.sum, halves[0]) + fold(jnp.sum, halves[1])
            weights = jnp.concatenate([half.astype(jnp.bfloat16) for half in halves], axis=0)
            values = jnp.concatenate([held(where, 1) for where in wheres], axis=1)
            summed = jnp.dot(values, weights, preferred_element_type=jnp.float32)
            found.append((row, total, summed))
        for row, total, summed in found:
            totals[row] += total
            sums[row] += summed
        return 0

    whole = first[rows] <= FIT
    size = jnp.where(whole, rows, per_piece)

    def segment(index, _):
        begin = index * size
        low, high = first[begin], first[begin + size]
        steps = (high - low + unroll - 1) // unroll
        lax.fori_loop(0, steps, functools.partial(rate, low, high), 0)

        def settle(row, _):
            top = jnp.max(tops[row], axis=0, keepdims=True) * factor
            tops[row] = jnp.broadcast_to(top, tops.shape[1:])
            return 0

        lax.fori_loop(begin, begin + size, settle, 0)
        lax.fori_loop(0, steps, functools.partial(gather, low, high), 0)
        return 0

    lax.fori_loop(0, jnp.where(whole, 1, len(outs)), segment, 0)

    for index, out in enumerate(outs):
        for part in range(per_piece):
            row = index * per_piece + part
            total = jnp.sum(totals[row], axis=0, keepdims=True)
            value = (sums[row] / total).T.astype(jnp.bfloat16)
            out[part * BLK : (part + 1) * BLK, :] = value


def pair_lists(counts, most):
    twos = (counts + 1) // 2
    rows = counts.shape[0]
    order = jnp.arange(rows + 1, dtype=jnp.int32)
    first = jnp.sum(jnp.where(order[None, :rows] < order[:, None], twos[None, :], 0), axis=1)
    slots = jnp.arange(rows * most // 2, dtype=jnp.int32)
    return first, jnp.sum(jnp.where(first[None, 1:] <= slots[:, None], 1, 0), axis=1)


def attend(factor, lists, plan, arrays, count):
    rows, most = lists[0].shape
    pieces = most * BLK // count
    asking = rows * BLK // count

    def kernel(*refs):
        attend_kernel(factor, PAIRS, plan, *refs)

    shape = (BLK, count)
    return pl.pallas_call(
        kernel,
        in_specs=[pl.BlockSpec(memory_space=pltpu.SMEM)] * len(lists)
        + [pl.BlockSpec(memory_space=pl.ANY)] * len(arrays),
        out_specs=[pl.BlockSpec(memory_space=pltpu.VMEM)] * asking,
        out_shape=[jax.ShapeDtypeStruct((count, BLK), jnp.bfloat16)] * asking,
        scratch_shapes=[
            pltpu.VMEM((pieces * 2 * BLK, count), jnp.bfloat16),
            pltpu.VMEM((asking, *shape), jnp.bfloat16),
            pltpu.VMEM((rows, BLK, BLK), jnp.bfloat16),
            pltpu.VMEM((max(rows * most // 2 // asking, FIT) + PAIRS, 2 * BLK, BLK), jnp.float32),
            pltpu.VMEM((rows, 8, BLK), jnp.float32),
            pltpu.VMEM((rows, 8, BLK), jnp.float32),
            pltpu.VMEM((rows, BLK, BLK), jnp.float32),
            pltpu.SemaphoreType.DMA((len(plan),)),
        ],
        compiler_params=pltpu.CompilerParams(vmem_limit_bytes=42 * MIB),
        cost_estimate=pl.CostEstimate(
            flops=rows * BLK * most * BLK * BLK,
            bytes_accessed=4 * most * BLK * BLK,
            transcendentals=rows * BLK * most * BLK // 4,
        ),
        name="attend",
    )(*lists, *arrays)


def leave_kernel(plan, chips, columns, own, other, *refs):
    heads, outs, ordered, arrived = refs[:4], list(refs[4:-2]), *refs[-2:]
    step = pl.program_id(0)

    @pl.when(step == 0)
    def _():
        copies = [
            pltpu.make_async_copy(head, ordered.at[columns[index]], arrived.at[index])
            for index, head in enumerate(heads)
        ]
        for copy in copies:
            copy.start()
        for copy in copies:
            copy.wait()

    summed = jnp.dot(
        jnp.concatenate([ordered[index] for index in range(4)], axis=1),
        jnp.concatenate([own[...], other[...]], axis=0),
        preferred_element_type=jnp.float32,
    )
    for index, cuts in enumerate(plan):
        mine = [outs.pop(0) for _ in cuts]

        @pl.when(step == index)
        def _():
            for cut, out in zip(cuts, mine):
                out[...] = summed[:, cut[0] : cut[1]].astype(out.dtype)


def leave(chips, columns, weights, heads, plan):
    count = heads[0].shape[0]
    steps = len(plan)
    inner = weights[0].shape[0]
    block = pl.BlockSpec((inner, DEEP), lambda i, chips, columns: (0, chips[i]))
    whole = lambda shape: pl.BlockSpec(shape, lambda i, *_: (0, 0))
    shapes = [(count, cut[1] - cut[0]) for cuts in plan for cut in cuts]

    def kernel(*refs):
        leave_kernel(plan, *refs)

    return pl.pallas_call(
        kernel,
        grid_spec=pltpu.PrefetchScalarGridSpec(
            num_scalar_prefetch=2,
            grid=(steps,),
            in_specs=[block] * 2 + [pl.BlockSpec(memory_space=pl.ANY)] * 4,
            out_specs=[whole(s) for s in shapes],
            scratch_shapes=[
                pltpu.VMEM((4, count, BLK), jnp.bfloat16),
                pltpu.SemaphoreType.DMA((4,)),
            ],
        ),
        out_shape=[jax.ShapeDtypeStruct(s, jnp.bfloat16) for s in shapes],
        compiler_params=pltpu.CompilerParams(vmem_limit_bytes=28 * MIB),
        cost_estimate=pl.CostEstimate(
            flops=4 * steps * DEEP * inner * count,
            bytes_accessed=2 * steps * DEEP * (2 * inner + count),
            transcendentals=0,
        ),
        name="leave",
    )(chips, columns, *weights, *heads)


def arrive_kernel(plan, turned, *refs):
    outs = refs[-len(plan) :]
    at = 0
    for cuts, out in zip(plan, outs):
        share, arrived = refs[at], refs[at + 1 : at + 1 + len(cuts)]
        at += 1 + len(cuts)
        edges = sorted({0, share.shape[1], *[edge for cut in cuts for edge in cut]})
        for low, high in zip(edges, edges[1:]):
            value = share[:, low:high].astype(jnp.float32)
            for (first, last), ref in zip(cuts, arrived):
                if first <= low and high <= last:
                    value += ref[:, low - first : high - first].astype(jnp.float32)
            if turned:
                out[low:high, :] = value.T.astype(out.dtype)
            else:
                out[:, low:high] = value.astype(out.dtype)


def arrive(plan, *arrays, turned=False):
    shapes, at = [], 0
    for cuts in plan:
        shapes.append(arrays[at].shape[::-1] if turned else arrays[at].shape)
        at += 1 + len(cuts)

    def kernel(*refs):
        arrive_kernel(plan, turned, *refs)

    return pl.pallas_call(
        kernel,
        in_specs=[pl.BlockSpec(memory_space=pltpu.VMEM)] * len(arrays),
        out_specs=[pl.BlockSpec(memory_space=pltpu.VMEM)] * len(plan),
        out_shape=[jax.ShapeDtypeStruct(shape, arrays[0].dtype) for shape in shapes],
        compiler_params=pltpu.CompilerParams(vmem_limit_bytes=16 * MIB),
        cost_estimate=pl.CostEstimate(
            flops=0, bytes_accessed=8 * arrays[0].size, transcendentals=0
        ),
        name="arrive",
    )(*arrays)


def gather_tokens(own, first_others, second_others):
    below = shift(own, "z", 1)
    above = shift(own, "z", -1)
    beside = swap(own, "yl")
    below, above, beside = together((below, above, beside), first_others)
    far = shift(below, "z", 1)
    beside_below = swap(below, "yl")
    beside_above = shift(beside, "z", -1)
    far, beside_below, beside_above = together((far, beside_below, beside_above), second_others)
    first, second, third = [slice(*cut) for cut in CUTS]
    parts = [
        swap(far[:, first], "yl"),
        shift(beside_above[:, second], "z", -1),
        shift(beside_below[:, third], "z", 1),
    ]
    places = [(0, 0), (0, -1), (0, 1), (1, 0), (0, 2), (1, -1), (1, 1), (1, 2)]
    return places, [own, below, above, beside, far, beside_below, beside_above, *parts]


def shards(tokens, qkv_weight, out_weight, modulation, block_mask):
    rows, local = tokens.shape
    features = modulation.shape[1]
    heads_here = block_mask.shape[0]
    inner = qkv_weight.shape[2]
    head_size = inner // heads_here
    factor = math.log2(math.e) / math.sqrt(head_size)
    half = rows // 2
    core = lax.axis_index("core")
    frame_x, frame_y = lax.axis_index("x"), lax.axis_index("yh")
    chip_y, chip_z = lax.axis_index("yl"), lax.axis_index("z")
    across = tokens.T

    def chip(dy, dz):
        return ((chip_y + dy) % 2) * 4 + (chip_z + dz) % 4

    def mine_and_given(value, axis):
        size = value.shape[axis] // 2
        mine = lax.dynamic_slice_in_dim(value, core * size, size, axis)
        return mine, lax.dynamic_slice_in_dim(value, (1 - core) * size, size, axis)

    def head_slot(steps):
        head = (frame_x + steps) % 4
        return jnp.where(head // 2 == core, 0, 1), head % 2

    mine, given = mine_and_given(across, 1)
    other = swap(given, "core")
    own = lay(core, mine, other)
    mask_mine, mask_given = mine_and_given(block_mask, 1)
    mask_other = swap(mask_given, "core")

    raw, *_ = lax.optimization_barrier((qkv_weight, own, mask_other))
    other_weight = swap(raw, "core")
    mask_heads = jnp.stack([mask_mine, mask_other])
    mask_rows = []
    for steps in range(4):
        side, slot = head_slot(steps)
        part = lax.dynamic_slice(
            mask_heads, (side, slot, 0, 0), (1, 1, *mask_heads.shape[2:])
        )[0, 0]
        mask_rows.append(shift(part, "x", steps) if steps else part)
    keep = jnp.concatenate(mask_rows, axis=0) != 0
    blocks = jnp.arange(keep.shape[1], dtype=jnp.int32)
    per_core = half // BLK
    piece, inside = blocks // per_core, blocks % per_core
    from_core, from_y = core ^ (piece // 8), frame_y ^ (piece // 4 % 2)
    order = piece % 4
    from_x = (frame_x - jnp.where(order < 2, order, 5 - order)) % 4
    origin = (from_y * 4 + from_x) * (2 * per_core) + from_core * per_core + inside
    same = origin[:, None] == blocks[None, :]
    keep = jnp.sum(jnp.where(same[None] & keep[:, None, :], 1, 0), axis=2)
    counts = jnp.sum(keep, axis=1)
    earlier = blocks[None, :] < blocks[:, None]
    rank = jnp.sum(jnp.where(earlier[None], keep[:, None, :], 0), axis=2)
    chosen = (keep[:, None, :] != 0) & (rank[:, None, :] == blocks[None, :, None])
    listed = jnp.sum(jnp.where(chosen, blocks[None, None, :], 0), axis=2)
    lists = (listed, counts, *pair_lists(counts, listed.shape[1]))
    places, xs = gather_tokens(own, (), mask_rows[1:])

    chips = jnp.stack([chip(*place) for place in places]).astype(jnp.int32)
    slots = [head_slot(steps) for steps in range(4)]
    bases = jnp.stack([side * 3 * heads_here + slot for side, slot in slots]).astype(jnp.int32)
    made = project(chips, bases, xs, qkv_weight, other_weight, modulation)
    kv, query, kv_two, q_two, *packed = made
    one, three = shift(packed[0], "x", 1), shift(packed[1], "x", 3)
    away_kv = swap(kv, "yh")
    one, three = together((one, three), (away_kv,))
    both = jnp.concatenate([one[: 2 * BLK], three[: 2 * BLK]], axis=0)
    away_both = swap(both, "yh")
    kv_two, q_two = together((kv_two, q_two), (one,))
    two, q_two = shift(kv_two, "x", 2), shift(q_two, "x", 2)
    away_kv_other = swap(away_kv, "core")
    two, kv, both = together((two, kv, both), (away_both, q_two, *lists, away_kv_other))
    away_two = swap(two, "yh")
    near = swap(jnp.concatenate([kv, both], axis=0), "core")
    arrays = [kv, both, two, away_kv, away_both, away_two, near, swap(two, "core")]
    arrays += [away_kv_other, swap(away_both, "core"), swap(away_two, "core")]
    arrays += [query, one, q_two, three]
    step = 2 * BLK
    plan = []
    for index, array in ((0, 0), (4, 3), (12, 8)):
        plan += [("kv", index, array, 0, step), ("kv", index + 1, array + 1, 0, 2 * step)]
        plan += [("kv", index + 3, array + 2, 0, step)]
    plan += [("kv", 8, 6, 0, 3 * step), ("kv", 11, 7, 0, step)]
    plan += [("q", index, 11 + index, index % 2 * step, BLK) for index in range(4)]
    heads = attend(factor, lists, plan, arrays, half)
    (out_own,) = together((out_weight,), (heads[0],))
    leaving = out_weight, swap(out_own, "core")
    heads = [heads[0]] + [shift(heads[steps], "x", -steps) for steps in (1, 2, 3)]

    columns = jnp.stack([side * heads_here + slot for side, slot in slots]).astype(jnp.int32)
    whole = CUTS[0][0], CUTS[-1][1]

    def shares(targets, cuts, heads):
        chips = jnp.stack([chip(*target) for target in targets]).astype(jnp.int32)
        return leave(chips, columns, leaving, heads, [cuts] * len(targets))

    parts = shares([(1, 2)], CUTS, heads)
    middle = [(0, 2), (1, 1), (1, -1)]
    share = dict(zip(middle, shares(middle, (whole,), heads)))
    first = swap(parts[0], "yl")
    second = shift(parts[1], "z", 1)
    third = shift(parts[2], "z", -1)
    heads = together(heads, (first, second, third))
    near = [(0, -1), (0, 1), (1, 0), (0, 0)]
    share |= dict(zip(near, shares(near, (whole,), heads)))
    down, up, side = arrive(
        [(CUTS[0],), (CUTS[1],), (CUTS[2],)],
        *[share[0, 2], first, share[1, 1], second, share[1, -1], third],
    )
    down, up, side = shift(down, "z", -1), shift(up, "z", 1), swap(side, "yl")
    down, side = arrive(
        [(whole, whole), (whole,)], share[0, -1], down, side, share[1, 0], up
    )
    down, up, side = shift(down, "z", -1), shift(share[0, 1], "z", 1), swap(side, "yl")
    (summed,) = arrive([(whole, whole, whole)], share[0, 0], down, up, side, turned=True)

    kept, given = mine_and_given(summed, 0)
    other = swap(given, "core")
    projected = jnp.concatenate(
        [jnp.where(core == 0, kept, other), jnp.where(core == 0, other, kept)], axis=1
    ).astype(jnp.float32)
    start = lax.axis_index(HEAD) * local
    gate = lax.dynamic_slice_in_dim(modulation, start, local, 1)[2][:, None]
    return (across.astype(jnp.float32) + gate * projected).astype(jnp.bfloat16).T


def solution(mesh):
    fine = Mesh(mesh.devices.reshape(2, 4, 2, 4, 2), ("yh", "x", "yl", "z", "core"))
    placed = (
        P(FRAME, HEAD),
        P(None, None, HEAD),
        P(HEAD, None),
        P(),
        P(HEAD, FRAME, None),
    )
    return jax.shard_map(
        shards, mesh=fine, in_specs=placed, out_specs=P(FRAME, HEAD), check_vma=False
    )
```
